256 devices in a mesh: lon: 64 (over z, x, core), lat: 4 (over y).
Axes of the slice: x: 4, y: 4, z: 8, core: 2. Of those that a mesh axis runs over, the one named last changes fastest.
Arguments:
- piece_height: float32 [4096, 128, 128], P('lon', 'lat')
- piece_weight: float32 [4096, 128, 128], P('lon', 'lat'), may hold values from 0.05 to 2
- piece_column: int32 [4096], P('lon'), may hold values from 0 to 262016, as said below
- piece_width: int32 [4096], P('lon'), may hold values from 64 to 128
Outputs:
- solution_field: float32 [128, 262144], P('lat', 'lon')
- residual: float32 [128, 262144], P('lat', 'lon')
The draws below stay inside these ranges and needn't reach their ends.
Inputs may be any that keep to these rules, and one draw needn't show every extreme that they name: Every value is a multiple of 128 and a piece lies inside one tile of 4096 columns, tile piece_column // 4096. The pieces of one device name each tile at most 2 times; one tile is named exactly 2 times by the pieces of every device.
All inputs are finite; a program needn't handle non-finite values.
Results may differ from the reference program's by a relative error of at most 0.0007.
Values sent between devices are 32-bit elements; how exact they have to be, the bound alone decides.
No kernel may reach another device: no remote copies, remote signals or barrier semaphores. Data moves between devices by JAX's collectives and lax.ppermute only.
A program may use at most 128 MiB of HBM per device.

```python
import math
import jax
import jax.numpy as jnp

ROWS = 128
COLS_DEV = 4096
BW = 128
CAPACITY = 2
ITERS = 4
PIECES_DEV = 64
PIECES = 4096
N_LON = 64


def piece_columns(key):
    key = jax.random.fold_in(key, 11)
    key_common, key_order, key_block = jax.random.split(key, 3)
    slot_total = N_LON * CAPACITY
    common_tile = jax.random.randint(key_common, (), 0, N_LON)

    def one_owner(owner_key):
        first_key, second_key = jax.random.split(owner_key)
        others = jax.random.permutation(first_key, slot_total - CAPACITY).astype(jnp.int32)
        others = jnp.where(others >= CAPACITY * common_tile, others + CAPACITY, others)
        leading = CAPACITY * common_tile + jnp.arange(CAPACITY, dtype=jnp.int32)
        chosen = jnp.concatenate([leading, others])[:PIECES_DEV]
        chosen = jax.random.permutation(second_key, chosen)
        return chosen // CAPACITY
    tiles = jax.vmap(one_owner)(jax.random.split(key_order, N_LON)).reshape(-1)
    blocks = jax.random.randint(key_block, (PIECES,), 0, COLS_DEV // BW)
    return (tiles * COLS_DEV + blocks * BW).astype(jnp.int32)


def draw_piece_column(key, part):
    return piece_columns(key)


def draw_piece_height(key, part):
    columns = piece_columns(key)
    key = jax.random.fold_in(key, 3)
    key_cell, key_offset = jax.random.split(key, 2)
    ramp = jnp.exp(math.log(3.0) * columns.astype(jnp.float32) / (COLS_DEV * N_LON))
    cells = jax.random.normal(key_cell, (PIECES, ROWS, BW), jnp.float32)
    offset = 2.0 * jax.random.normal(key_offset, (PIECES, 1, 1), jnp.float32)
    return ((cells + offset) * ramp[:, None, None]).astype(jnp.float32)


def set_ends(array, key, least, high):
    longest = array.shape.index(max(array.shape))
    spots = []
    for shift in (0, 1):
        where = [jax.random.randint(jax.random.fold_in(key, axis), (), 0, length) for axis, length in enumerate(array.shape)]
        where[longest] = (where[longest] + shift) % array.shape[longest]
        spots.append(tuple(where))
    return array.at[spots[0]].set(least).at[spots[1]].set(high)


def block_levels(own_key, dims, shards, least, top_value):
    def one(axis_at, shards_of):
        steps = jax.random.uniform(jax.random.fold_in(jax.random.fold_in(own_key, 6), axis_at), (shards_of,), jnp.float32, least / len(shards), top_value / len(shards))
        return jnp.repeat(jnp.exp(steps), dims[axis_at] // shards_of).reshape((-1,) + (1,) * (len(dims) - axis_at - 1))

    level = one(*shards[0])
    for cut in shards[1:]:
        level = level * one(*cut)
    return level


def setup_inputs(seed: int = 0) -> dict:
    arg_keys = jax.random.split(jax.random.key(seed), 5)
    return {
        "piece_height": draw_piece_height(jax.random.fold_in(arg_keys[4], 71), 0),
        "piece_weight": jnp.clip(jnp.exp(math.log(2.0) - 3.6888794 * jax.random.uniform(arg_keys[1], (PIECES, ROWS, BW), jnp.float32) ** block_levels(arg_keys[1], (PIECES, ROWS, BW), ((0, 64), (1, 4)), -0.2, 0.2)), 0.05, 2.0),
        "piece_column": draw_piece_column(jax.random.fold_in(arg_keys[4], 71), 0),
        "piece_width": set_ends(jax.random.randint(arg_keys[3], (PIECES,), BW // 2, BW + 1), jax.random.fold_in(arg_keys[3], 1), BW // 2, BW).astype(jnp.int32),
    }


MU_DATA = 0.5
DAMPING = 0.5
RIDGE = 0.05


def piece_terms(height, weight, width, north_step, row_global):
    column = jnp.arange(height.shape[2], dtype=jnp.int32)
    valid_cell = column[None, None, :] < width[:, None, None]
    east_edge = (column[None, None, :] + 1) < width[:, None, None]
    north_edge = valid_cell & (row_global[None, :, None] < ROWS - 1)
    weights_full = weight.astype(jnp.float32)
    east_step = jnp.concatenate([height[:, :, 1:] - height[:, :, :-1], jnp.zeros_like(height[:, :, :1])], axis=2)
    cell_weight = jnp.where(valid_cell, weights_full, jnp.float32(0.0))
    east_weight = jnp.where(east_edge, weights_full, jnp.float32(0.0))
    north_weight = jnp.where(north_edge, weights_full, jnp.float32(0.0))
    return (cell_weight, cell_weight * height, east_weight, east_weight * east_step,
            north_weight, north_weight * north_step)


def reference(piece_height, piece_weight, piece_column, piece_width):
    row_global = jnp.arange(ROWS, dtype=jnp.int32)
    north_step = jnp.concatenate([piece_height[:, 1:, :] - piece_height[:, :-1, :],
                                  jnp.zeros_like(piece_height[:, :1, :])], axis=1)
    terms = piece_terms(piece_height, piece_weight, piece_width, north_step, row_global)
    block_ids = (piece_column // BW).astype(jnp.int32)
    total_blocks = N_LON * COLS_DEV // BW
    fields = []
    for term in terms:
        summed = jax.ops.segment_sum(term, block_ids, num_segments=total_blocks)
        fields.append(jnp.transpose(summed, (1, 0, 2)).reshape(ROWS, total_blocks * BW))
    weight_sum, height_sum, east_weight_sum, east_sum, north_weight_sum, north_sum = fields
    target_east = east_sum / (east_weight_sum + DAMPING)
    target_north = north_sum / (north_weight_sum + DAMPING)
    south_target = jnp.concatenate([jnp.zeros_like(target_north[:1]), target_north[:-1]], axis=0)
    right_side = MU_DATA * height_sum - (target_east - jnp.roll(target_east, 1, axis=1)) - (target_north - south_target)
    diagonal = MU_DATA * weight_sum + RIDGE
    has_upper = (row_global < ROWS - 1)[:, None]
    has_lower = (row_global > 0)[:, None]

    def operate(field):
        coupling = 2.0 * field - jnp.roll(field, 1, axis=1) - jnp.roll(field, -1, axis=1)
        coupling = coupling + jnp.where(has_upper, field - jnp.roll(field, -1, axis=0), jnp.float32(0.0))
        coupling = coupling + jnp.where(has_lower, field - jnp.roll(field, 1, axis=0), jnp.float32(0.0))
        return diagonal * field + coupling

    solution_field = jnp.zeros_like(right_side)
    residual = right_side
    direction = right_side
    norm_now = jnp.sum(residual * residual)
    for iteration in range(ITERS):
        image = operate(direction)
        alpha = norm_now / jnp.sum(direction * image)
        solution_field = solution_field + alpha * direction
        residual = residual - alpha * image
        norm_next = jnp.sum(residual * residual)
        direction = residual + (norm_next / norm_now) * direction
        norm_now = norm_next
    return solution_field, residual
```

```python
import jax
import jax.numpy as jnp
from jax import lax
from jax.experimental import pallas as pl
from jax.experimental.pallas import tpu as pltpu
from jax.sharding import PartitionSpec as P

ROWS = 128
COLS_DEV = 4096
BW = 128
BLOCKS = COLS_DEV // BW
CAPACITY = 2

MU_DATA = 0.5
DAMPING = 0.5
RIDGE = 0.05
HIGHEST = lax.Precision.HIGHEST

MID = 5.5
HALF = 5.5
VMEM_BYTES = 40 * 1024 * 1024
F32 = jnp.float32


def passed_along(block, axis, distance):
    devices = range(lax.axis_size(axis))
    route = [(i, i + distance) for i in devices if i + distance in devices]
    return lax.ppermute(block, axis, route)


def passed_around(block, axis, distance):
    count = lax.axis_size(axis)
    return lax.ppermute(block, axis, [(i, (i + distance) % count) for i in range(count)])


def pack_kernel(column_ref, height_ref, weight_ref, out_ref, count_ref):
    tiles, pieces = out_ref.shape[0], height_ref.shape[0]

    @pl.loop(0, tiles)
    def _(t):
        count_ref[t] = 0

    @pl.loop(0, pieces, unroll=4)
    def _(p):
        tile = column_ref[p] // COLS_DEV
        slot = count_ref[tile]
        count_ref[tile] = slot + 1
        out_ref[tile, 2 * slot] = height_ref[p]
        out_ref[tile, 2 * slot + 1] = weight_ref[p]


def pack(piece_column, piece_height, piece_weight, tiles):
    rows = piece_height.shape[1]
    return pl.pallas_call(
        pack_kernel,
        out_shape=jax.ShapeDtypeStruct((tiles, 2 * CAPACITY, rows, BW), F32),
        in_specs=[
            pl.BlockSpec(memory_space=pltpu.SMEM),
            pl.BlockSpec(memory_space=pltpu.VMEM),
            pl.BlockSpec(memory_space=pltpu.VMEM),
        ],
        out_specs=pl.BlockSpec(memory_space=pltpu.VMEM),
        scratch_shapes=[pltpu.SMEM((tiles,), jnp.int32)],
        compiler_params=pltpu.CompilerParams(vmem_limit_bytes=VMEM_BYTES),
        name="pack",
    )(piece_column, piece_height, piece_weight)


def small_messages(piece_height, piece_column, piece_width, lon):
    pieces = piece_column.shape[0]
    lon_count = lax.axis_size("lon")
    tile = piece_column // COLS_DEV
    block = piece_column % COLS_DEV // BW
    ids = jnp.arange(pieces, dtype=jnp.int32)
    same = (tile[:, None] == tile[None, :]) & (ids[None, :] < ids[:, None])
    rank = jnp.sum(same.astype(jnp.int32), axis=1)
    place = (tile ^ lon) * CAPACITY + rank
    hot = jnp.arange(lon_count * CAPACITY, dtype=jnp.int32)[:, None] == place[None, :]
    hot_int = hot.astype(jnp.int32)
    block_of = jnp.sum(hot_int * (block + 1)[None, :], axis=1).reshape(lon_count, CAPACITY)
    width_of = jnp.sum(hot_int * piece_width[None, :], axis=1).reshape(lon_count, CAPACITY)
    next_first = passed_along(piece_height[:, 0, :], "lat", -1)
    first = jnp.dot(hot.astype(F32), next_first, precision=HIGHEST)
    facts = jnp.concatenate([block_of, width_of], axis=1).astype(F32)
    facts = jnp.pad(facts, ((0, 0), (0, BW - 2 * CAPACITY)))[:, None, :]
    first = first.reshape(lon_count, CAPACITY, BW)
    return jnp.concatenate([first, facts, jnp.zeros_like(facts)], axis=1)


def exchanged(message, lon_count):
    shape = message.shape
    bit = 1
    while bit < lon_count:
        split = message.reshape((lon_count // (2 * bit), 2, bit) + shape[1:])
        moved = lax.ppermute(split[:, 1], "lon", [(i, i ^ bit) for i in range(lon_count)])
        message = jnp.stack([split[:, 0], moved], axis=1).reshape(shape)
        bit *= 2
    return message


def sums_kernel(place_ref, facts_ref, got_ref, first_ref, rhs_ref, diag_ref, up_ref, down_ref,
                edge_ref, total_ref):
    step, steps = pl.program_id(0), pl.num_programs(0)
    sources, _, rows, _ = got_ref.shape
    lon, lat, lat_count = place_ref[0], place_ref[1], place_ref[2]
    lane = lax.broadcasted_iota(jnp.int32, (rows, BW), 1)
    row = lax.broadcasted_iota(jnp.int32, (rows, BW), 0)

    @pl.when(step == 0)
    def _():
        total_ref[...] = jnp.zeros_like(total_ref)

    for s in range(sources):
        entry = (step * sources + s) ^ lon
        for slot in range(CAPACITY):
            block = facts_ref[entry * 2 * CAPACITY + slot] - 1
            width = facts_ref[entry * 2 * CAPACITY + CAPACITY + slot]

            @pl.when(block >= 0)
            def _(s=s, slot=slot, block=block, width=width, entry=entry):
                height = got_ref[s, 2 * slot]
                weight = got_ref[s, 2 * slot + 1]
                above = first_ref[entry, pl.ds(slot, 1), :]
                cell = jnp.where(lane < width, weight, 0.0)
                east = jnp.where(lane + 1 < width, weight, 0.0)
                east_step = pltpu.roll(height, BW - 1, 1) - height
                raised = jnp.where(row == rows - 1, above, pltpu.roll(height, rows - 1, 0))
                total_ref[block, 0] += cell
                total_ref[block, 1] += cell * height
                total_ref[block, 2] += east
                total_ref[block, 3] += east * east_step
                total_ref[block, 4] += cell * (raised - height)

    @pl.when(step == steps - 1)
    def _():
        last = (row == rows - 1) & (lat == lat_count - 1)
        first = (row == 0) & (lat == 0)
        sides = 4.0 - last.astype(F32) - first.astype(F32) + RIDGE
        row8 = row[:8]

        @pl.loop(0, BLOCKS)
        def _(i):
            cell, height = total_ref[i, 0], total_ref[i, 1]
            east = total_ref[i, 3] / (total_ref[i, 2] + DAMPING)
            north = jnp.where(last, 0.0, total_ref[i, 4] / (cell + DAMPING))
            south = jnp.where(row == 0, 0.0, pltpu.roll(north, 1, 0))
            rhs = MU_DATA * height - (east - pltpu.roll(east, 1, 1)) - (north - south)
            diag = MU_DATA * cell + sides
            rhs_ref[i] = rhs
            diag_ref[i] = diag
            top = pltpu.roll(diag[rows - 8:], 4, 0)
            top = jnp.where(row8 == 0, pltpu.roll(north[rows - 8:], 1, 0), top)
            up_ref[i] = jnp.where(row8 >= 4, rhs[rows - 8:], top)
            down_ref[i] = jnp.where(row8 >= 4, pltpu.roll(diag[:8], 4, 0), rhs[:8])

        for side, block in ((0, 0), (1, BLOCKS - 1)):
            edge_ref[side, 0:rows] = rhs_ref[block]
            edge_ref[side, rows:2 * rows] = diag_ref[block]
            edge_ref[side, 2 * rows:2 * rows + 8] = up_ref[block]


def sums(place, facts, got, first, batch=8):
    tiles, arrays, rows, _ = got.shape
    whole = lambda *shape: pl.BlockSpec(shape, lambda i: (0,) * len(shape))
    field = (BLOCKS, rows, BW)
    strip = (BLOCKS, 8, BW)
    edge = (2, 2 * rows + 8, BW)
    return pl.pallas_call(
        sums_kernel,
        grid=(tiles // batch,),
        out_shape=[jax.ShapeDtypeStruct(s, F32) for s in (field, field, strip, strip, edge)],
        in_specs=[
            pl.BlockSpec(memory_space=pltpu.SMEM),
            pl.BlockSpec(memory_space=pltpu.SMEM),
            pl.BlockSpec((batch, arrays, rows, BW), lambda i: (i, 0, 0, 0)),
            whole(*first.shape),
        ],
        out_specs=[whole(*s) for s in (field, field, strip, strip, edge)],
        scratch_shapes=[pltpu.VMEM((BLOCKS, 5, rows, BW), F32)],
        compiler_params=pltpu.CompilerParams(vmem_limit_bytes=VMEM_BYTES),
        name="sums",
    )(place, facts, got, first)


PAIRS = [(i, j) for j in range(5) for i in range(min(j, 3) + 1)]


def basis_kernel(place_ref, rhs_ref, diag_ref, up_ref, south_ref, north_ref, west_ref, east_ref,
                 q_ref, gram_ref, scale_ref, v_ref):
    rows = rhs_ref.shape[1]
    tall = rows + 16
    lat, lat_count = place_ref[1], place_ref[2]
    row = lax.broadcasted_iota(jnp.int32, (rows, BW), 0)
    row8 = row[:8]
    row_all = lax.broadcasted_iota(jnp.int32, (tall, BW), 0)
    lane = lax.broadcasted_iota(jnp.int32, (tall, BW), 1)
    inside = ((row_all >= 8) | (lat > 0)) & ((row_all < rows + 8) | (lat < lat_count - 1))

    def assemble(i, rhs, diag, up, south, north):
        first = jnp.where(row == 0, south[0:1], 0.0) + rhs
        below = jnp.where(row8 >= 4, south, 0.0)
        above = jnp.where(row8 == 0, north + up, jnp.where(row8 < 4, north, 0.0))
        v_ref[0, i] = jnp.concatenate([below, first, above], axis=0)
        diag = jnp.concatenate([pltpu.roll(south, 4, 0), diag, pltpu.roll(north, 4, 0)], axis=0)
        scale_ref[i] = (diag - MID) * (2.0 / HALF)

    for i, ref in ((0, west_ref), (BLOCKS + 1, east_ref)):
        two = 2 * rows
        assemble(i, ref[0:rows], ref[rows:two], ref[two:two + 8], ref[two + 8:two + 16],
                 ref[two + 16:two + 24])

    @pl.loop(0, BLOCKS)
    def _(i):
        assemble(i + 1, rhs_ref[i], diag_ref[i], up_ref[i], south_ref[i], north_ref[i])

    def applied(k, i):
        v = v_ref[k, i]
        left = v_ref[k, jnp.maximum(i - 1, 0)]
        right = v_ref[k, jnp.minimum(i + 1, BLOCKS + 1)]
        west = pltpu.roll(jnp.where(lane == BW - 1, left, v), 1, 1)
        east = pltpu.roll(jnp.where(lane == 0, right, v), BW - 1, 1)
        south = pltpu.roll(v, 1, 0)
        north = pltpu.roll(v, tall - 1, 0)
        image = scale_ref[i] * v - (2.0 / HALF) * ((west + east) + (south + north))
        if k == 0:
            image = 0.5 * image
        else:
            image = image - v_ref[k - 1, i]
        return jnp.where(inside, image, 0.0)

    for k in range(3):
        @pl.loop(0, BLOCKS + 2)
        def _(i, k=k):
            v_ref[k + 1, i] = applied(k, i)

    def products(i, carry):
        last = applied(3, i + 1)[8:8 + rows]
        q = [v_ref[k, i + 1, 8:8 + rows] for k in range(4)] + [last]
        for k in range(5):
            q_ref[k, i] = q[k]
        out = []
        for total, (a, b) in zip(carry, PAIRS):
            term = q[a] * q[b]
            out.append(total + sum(term[8 * n:8 * n + 8] for n in range(rows // 8)))
        return tuple(out)

    zero = tuple(jnp.zeros((8, BW), F32) for _ in PAIRS)
    totals = lax.fori_loop(0, BLOCKS, products, zero)
    lane1 = lax.broadcasted_iota(jnp.int32, (1, BW), 1)
    gram = jnp.zeros((1, BW), F32)
    for n, total in enumerate(totals):
        value = jnp.sum(jnp.sum(total, axis=0, keepdims=True), axis=1, keepdims=True)
        gram = jnp.where(lane1 == n, value, gram)
    gram_ref[...] = gram


def basis(place, rhs, diag, up, south, north, west, east):
    rows = rhs.shape[1]
    vmem = pl.BlockSpec(memory_space=pltpu.VMEM)
    return pl.pallas_call(
        basis_kernel,
        out_shape=[
            jax.ShapeDtypeStruct((5, BLOCKS, rows, BW), F32),
            jax.ShapeDtypeStruct((1, BW), F32),
        ],
        in_specs=[pl.BlockSpec(memory_space=pltpu.SMEM)] + [vmem] * 7,
        out_specs=[vmem, vmem],
        scratch_shapes=[
            pltpu.VMEM((BLOCKS + 2, rows + 16, BW), F32),
            pltpu.VMEM((4, BLOCKS + 2, rows + 16, BW), F32),
        ],
        compiler_params=pltpu.CompilerParams(vmem_limit_bytes=VMEM_BYTES),
        name="basis",
    )(place, rhs, diag, up, south, north, west, east)


def solved(gram):
    g = {}
    for n, (a, b) in enumerate(PAIRS):
        g[a, b] = g[b, a] = gram[n]
    m = [[None] * 4 for _ in range(4)]
    for j in range(4):
        for i in range(j + 1):
            if j == 0:
                value = MID * g[i, 0] + HALF * g[i, 1]
            else:
                value = MID * g[i, j] + (0.5 * HALF) * (g[i, j + 1] + g[i, j - 1])
            m[i][j] = m[j][i] = value
    y = [g[0, i] for i in range(4)]
    inverse = []
    factor = [[None] * 4 for _ in range(4)]
    for k in range(4):
        pivot = m[k][k]
        inverse.append(jnp.where(pivot > 0.0, 1.0 / jnp.where(pivot > 0.0, pivot, 1.0), 0.0))
        for i in range(k + 1, 4):
            factor[i][k] = m[k][i] * inverse[k]
        for i in range(k + 1, 4):
            for j in range(i, 4):
                m[i][j] = m[i][j] - factor[i][k] * m[k][j]
            y[i] = y[i] - factor[i][k] * y[k]
    c = [y[k] * inverse[k] for k in range(4)]
    for k in range(3, -1, -1):
        for i in range(k):
            c[i] = c[i] - factor[k][i] * c[k]
    half = 0.5 * HALF
    r = [
        1.0 - (MID * c[0] + half * c[1]),
        -(HALF * c[0] + MID * c[1] + half * c[2]),
        -(half * c[1] + MID * c[2] + half * c[3]),
        -(half * c[2] + MID * c[3]),
        -(half * c[3]),
    ]
    return c, r


def combine_kernel(gram_ref, q_ref, x_ref, r_ref, c_ref):
    @pl.when(pl.program_id(0) == 0)
    def _():
        gram = jnp.sum(gram_ref[...], axis=0, keepdims=True)
        lane = lax.broadcasted_iota(jnp.int32, (1, BW), 1)
        pick = lambda n: jnp.sum(jnp.where(lane == n, gram, 0.0), axis=1, keepdims=True)
        c, r = solved([pick(n) for n in range(len(PAIRS))])
        for n, value in enumerate(c + r):
            c_ref[n] = jnp.broadcast_to(value, (8, BW))

    rows = q_ref.shape[2]
    factors = [jnp.concatenate([c_ref[n]] * (rows // 8), axis=0) for n in range(9)]
    for i in range(q_ref.shape[1]):
        q = [q_ref[k, i] for k in range(5)]
        columns = slice(i * BW, (i + 1) * BW)
        x_ref[:, columns] = sum(factors[k] * q[k] for k in range(4))
        r_ref[:, columns] = sum(factors[4 + k] * q[k] for k in range(5))


def combine(gram, q, batch=8):
    _, blocks, rows, _ = q.shape
    out = jax.ShapeDtypeStruct((rows, blocks * BW), F32)
    spec = pl.BlockSpec((rows, batch * BW), lambda i: (0, i))
    return pl.pallas_call(
        combine_kernel,
        grid=(blocks // batch,),
        out_shape=[out, out],
        in_specs=[
            pl.BlockSpec(gram.shape, lambda i: (0, 0)),
            pl.BlockSpec((5, batch, rows, BW), lambda i: (0, i, 0, 0)),
        ],
        out_specs=[spec, spec],
        scratch_shapes=[pltpu.VMEM((9, 8, BW), F32)],
        compiler_params=pltpu.CompilerParams(vmem_limit_bytes=VMEM_BYTES),
        name="combine",
    )(gram, q)


def body(piece_height, piece_weight, piece_column, piece_width):
    lon_count, lat_count = lax.axis_size("lon"), lax.axis_size("lat")
    lon, lat = lax.axis_index("lon"), lax.axis_index("lat")
    place = jnp.stack([lon, lat, jnp.int32(lat_count)]).astype(jnp.int32)

    packed = pack(piece_column, piece_height, piece_weight, lon_count)
    got = lax.all_to_all(packed, "lon", split_axis=0, concat_axis=0, tiled=True)

    small = exchanged(small_messages(piece_height, piece_column, piece_width, lon), lon_count)
    facts = small[:, CAPACITY, :2 * CAPACITY].astype(jnp.int32).reshape(-1)

    rhs, diag, up, down, edge = sums(place, facts, got, small)
    south = passed_along(up, "lat", 1)
    north = passed_along(down, "lat", -1)
    to_west = jnp.concatenate([edge[0], south[0], north[0]], axis=0)
    to_east = jnp.concatenate([edge[1], south[-1], north[-1]], axis=0)
    west = passed_around(to_east, "lon", 1)
    east = passed_around(to_west, "lon", -1)
    q, gram = basis(place, rhs, diag, up, south, north, west, east)
    spread = jnp.broadcast_to(gram[None], (lon_count * lat_count, 1, BW))
    grams = lax.all_to_all(spread, ("lon", "lat"), split_axis=0, concat_axis=0, tiled=True)
    return tuple(combine(grams.reshape(lon_count * lat_count, BW), q))


def solution(mesh):
    return jax.shard_map(
        body,
        mesh=mesh,
        in_specs=(P("lon", "lat", None), P("lon", "lat", None), P("lon"), P("lon")),
        out_specs=(P("lat", "lon"), P("lat", "lon")),
        check_vma=False,
    )
```

```python
import jax
import jax.numpy as jnp
from jax import lax
from jax.experimental import pallas as pl
from jax.experimental.pallas import tpu as pltpu
from jax.sharding import PartitionSpec as P

ROWS = 128
COLS_DEV = 4096
BW = 128
BLOCKS = COLS_DEV // BW
CAPACITY = 2
NEAR = 8

MU_DATA = 0.5
DAMPING = 0.5
RIDGE = 0.05
HIGHEST = lax.Precision.HIGHEST

MID = 5.5
HALF = 5.5
VMEM_BYTES = 40 * 1024 * 1024
PACK_VMEM_BYTES = 60 * 1024 * 1024
F32 = jnp.float32


def passed_along(block, axis, distance):
    devices = range(lax.axis_size(axis))
    route = [(i, i + distance) for i in devices if i + distance in devices]
    return lax.ppermute(block, axis, route)


def passed_around(block, axis, distance):
    count = lax.axis_size(axis)
    return lax.ppermute(block, axis, [(i, (i + distance) % count) for i in range(count)])


def pack_kernel(column_ref, height_ref, weight_ref, out_ref, count_ref, sem):
    tiles, pieces = out_ref.shape[0], height_ref.shape[0]

    @pl.loop(0, tiles, unroll=8)
    def _(t):
        count_ref[t] = 0

    @pl.loop(0, pieces, unroll=4)
    def _(p):
        tile = column_ref[p] // COLS_DEV
        slot = count_ref[tile]
        count_ref[tile] = slot + 1
        pltpu.make_async_copy(height_ref.at[p], out_ref.at[tile, 2 * slot], sem.at[0]).start()
        pltpu.make_async_copy(weight_ref.at[p], out_ref.at[tile, 2 * slot + 1], sem.at[1]).start()

    half = out_ref.at[pl.ds(0, pieces), 0]
    pltpu.make_async_copy(height_ref, half, sem.at[0]).wait()
    pltpu.make_async_copy(weight_ref, half, sem.at[1]).wait()


def pack(piece_column, piece_height, piece_weight, tiles):
    rows = piece_height.shape[1]
    return pl.pallas_call(
        pack_kernel,
        out_shape=jax.ShapeDtypeStruct((tiles, 2 * CAPACITY, rows, BW), F32),
        in_specs=[
            pl.BlockSpec(memory_space=pltpu.SMEM),
            pl.BlockSpec(memory_space=pl.ANY),
            pl.BlockSpec(memory_space=pl.ANY),
        ],
        out_specs=pl.BlockSpec(memory_space=pl.ANY),
        scratch_shapes=[pltpu.SMEM((tiles,), jnp.int32), pltpu.SemaphoreType.DMA((2,))],
        compiler_params=pltpu.CompilerParams(vmem_limit_bytes=PACK_VMEM_BYTES),
        name="pack",
    )(piece_column, piece_height, piece_weight)


def small_messages(piece_height, piece_column, piece_width, lon):
    pieces = piece_column.shape[0]
    lon_count = lax.axis_size("lon")
    tile = piece_column // COLS_DEV
    block = piece_column % COLS_DEV // BW
    ids = jnp.arange(pieces, dtype=jnp.int32)
    same = (tile[:, None] == tile[None, :]) & (ids[None, :] < ids[:, None])
    rank = jnp.sum(same.astype(jnp.int32), axis=1)
    place = (tile ^ lon) * CAPACITY + rank
    hot = jnp.arange(lon_count * CAPACITY, dtype=jnp.int32)[:, None] == place[None, :]
    hot_int = hot.astype(jnp.int32)
    block_of = jnp.sum(hot_int * (block + 1)[None, :], axis=1).reshape(lon_count, CAPACITY)
    width_of = jnp.sum(hot_int * piece_width[None, :], axis=1).reshape(lon_count, CAPACITY)
    next_first = passed_along(piece_height[:, 0, :], "lat", -1)
    first = jnp.dot(hot.astype(F32), next_first, precision=HIGHEST)
    facts = jnp.concatenate([block_of, width_of], axis=1).astype(F32)
    facts = jnp.pad(facts, ((0, 0), (0, BW - 2 * CAPACITY)))[:, None, :]
    first = first.reshape(lon_count, CAPACITY, BW)
    return jnp.concatenate([first, facts, jnp.zeros_like(facts)], axis=1)


def exchanged(message, lon_count):
    shape = message.shape
    bit = 1
    while bit < NEAR:
        split = message.reshape((lon_count // (2 * bit), 2, bit) + shape[1:])
        moved = lax.ppermute(split[:, 1], "lon", [(i, i ^ bit) for i in range(lon_count)])
        message = jnp.stack([split[:, 0], moved], axis=1).reshape(shape)
        bit *= 2
    parts = [message[:NEAR]]
    for far in range(NEAR, lon_count, NEAR):
        route = [(i, i ^ far) for i in range(lon_count)]
        parts.append(lax.ppermute(message[far:far + NEAR], "lon", route))
    return jnp.concatenate(parts, axis=0)


def sums_kernel(place_ref, facts_ref, got_ref, first_ref, rhs_ref, diag_ref, up_ref, down_ref,
                edge_ref, total_ref):
    step, steps = pl.program_id(0), pl.num_programs(0)
    sources, _, rows, _ = got_ref.shape
    lon, lat, lat_count = place_ref[0], place_ref[1], place_ref[2]
    lane = lax.broadcasted_iota(jnp.int32, (rows, BW), 1)
    row = lax.broadcasted_iota(jnp.int32, (rows, BW), 0)

    @pl.when(step == 0)
    def _():
        total_ref[...] = jnp.zeros_like(total_ref)

    for s in range(sources):
        entry = (step * sources + s) ^ lon
        for slot in range(CAPACITY):
            block = facts_ref[entry * 2 * CAPACITY + slot] - 1
            block = jnp.where(block < 0, BLOCKS, block)
            width = facts_ref[entry * 2 * CAPACITY + CAPACITY + slot]
            height = got_ref[s, 2 * slot]
            weight = got_ref[s, 2 * slot + 1]
            above = first_ref[entry, pl.ds(slot, 1), :]
            cell = jnp.where(lane < width, weight, 0.0)
            east = jnp.where(lane < width - 1, weight, 0.0)
            east_step = pltpu.roll(height, BW - 1, 1) - height
            raised = jnp.where(row == rows - 1, above, pltpu.roll(height, rows - 1, 0))
            terms = (cell, cell * height, east, east * east_step, cell * (raised - height))
            for n, term in enumerate(terms):
                total_ref[block, n] += term

    @pl.when(step == steps - 1)
    def _():
        last = (row == rows - 1) & (lat == lat_count - 1)
        first = (row == 0) & (lat == 0)
        sides = 4.0 - last.astype(F32) - first.astype(F32) + RIDGE
        row8 = row[:8]

        @pl.loop(0, BLOCKS, unroll=4)
        def _(i):
            cell, height = total_ref[i, 0], total_ref[i, 1]
            east = total_ref[i, 3] / (total_ref[i, 2] + DAMPING)
            north = jnp.where(last, 0.0, total_ref[i, 4] / (cell + DAMPING))
            south = jnp.where(row == 0, 0.0, pltpu.roll(north, 1, 0))
            rhs = MU_DATA * height - (east - pltpu.roll(east, 1, 1)) - (north - south)
            diag = MU_DATA * cell + sides
            rhs_ref[i] = rhs
            diag_ref[i] = diag
            top = pltpu.roll(diag[rows - 8:], 4, 0)
            top = jnp.where(row8 == 0, pltpu.roll(north[rows - 8:], 1, 0), top)
            up_ref[i] = jnp.where(row8 >= 4, rhs[rows - 8:], top)
            down_ref[i] = jnp.where(row8 >= 4, pltpu.roll(diag[:8], 4, 0), rhs[:8])

        for side, block in ((0, 0), (1, BLOCKS - 1)):
            edge_ref[side, 0:rows] = rhs_ref[block]
            edge_ref[side, rows:2 * rows] = diag_ref[block]
            edge_ref[side, 2 * rows:2 * rows + 8] = up_ref[block]


def sums(place, facts, got, first, batch=8):
    tiles, arrays, rows, _ = got.shape
    whole = lambda *shape: pl.BlockSpec(shape, lambda i: (0,) * len(shape))
    field = (BLOCKS, rows, BW)
    strip = (BLOCKS, 8, BW)
    edge = (2, 2 * rows + 8, BW)
    return pl.pallas_call(
        sums_kernel,
        grid=(tiles // batch,),
        out_shape=[jax.ShapeDtypeStruct(s, F32) for s in (field, field, strip, strip, edge)],
        in_specs=[
            pl.BlockSpec(memory_space=pltpu.SMEM),
            pl.BlockSpec(memory_space=pltpu.SMEM),
            pl.BlockSpec((batch, arrays, rows, BW), lambda i: (i, 0, 0, 0)),
            whole(*first.shape),
        ],
        out_specs=[whole(*s) for s in (field, field, strip, strip, edge)],
        scratch_shapes=[pltpu.VMEM((BLOCKS + 1, 5, rows, BW), F32)],
        compiler_params=pltpu.CompilerParams(vmem_limit_bytes=VMEM_BYTES),
        name="sums",
    )(place, facts, got, first)


PAIRS = [(i, j) for j in range(5) for i in range(min(j, 3) + 1)]


def basis_kernel(place_ref, rhs_ref, diag_ref, up_ref, south_ref, north_ref, west_ref, east_ref,
                 q_ref, gram_ref, scale_ref, *v_refs):
    rows = rhs_ref.shape[1]
    tall = rows + 16
    lat, lat_count = place_ref[1], place_ref[2]
    row = lax.broadcasted_iota(jnp.int32, (rows, BW), 0)
    row8 = row[:8]
    lane = lax.broadcasted_iota(jnp.int32, (tall, BW), 1)

    def assemble(i, rhs, diag, up, south, north):
        first = jnp.where(row == 0, south[0:1], 0.0) + rhs
        below = jnp.where(row8 >= 4, south, 0.0)
        above = jnp.where(row8 == 0, north + up, jnp.where(row8 < 4, north, 0.0))
        v_refs[0][i, 8:8 + tall] = jnp.concatenate([below, first, above], axis=0)
        diag = jnp.concatenate([pltpu.roll(south, 4, 0), diag, pltpu.roll(north, 4, 0)], axis=0)
        scale_ref[i] = (diag - MID) * (2.0 / HALF)

    for i, ref in ((0, west_ref), (BLOCKS + 1, east_ref)):
        two = 2 * rows
        assemble(i, ref[0:rows], ref[rows:two], ref[two:two + 8], ref[two + 8:two + 16],
                 ref[two + 16:two + 24])

    @pl.loop(0, BLOCKS, unroll=4)
    def _(i):
        assemble(i + 1, rhs_ref[i], diag_ref[i], up_ref[i], south_ref[i], north_ref[i])

    def applied(k, i):
        body = slice(8, 8 + tall)
        v = v_refs[k][i, body]
        left = v_refs[k][jnp.maximum(i - 1, 0), body]
        right = v_refs[k][jnp.minimum(i + 1, BLOCKS + 1), body]
        west = pltpu.roll(jnp.where(lane == BW - 1, left, v), 1, 1)
        east = pltpu.roll(jnp.where(lane == 0, right, v), BW - 1, 1)
        south = v_refs[k][i, 7:7 + tall]
        north = v_refs[k][i, 9:9 + tall]
        image = scale_ref[i] * v - (2.0 / HALF) * ((west + east) + (south + north))
        if k == 0:
            image = 0.5 * image
        else:
            image = image - v_refs[k - 1][i, body]
        ends = (jnp.where(lat > 0, image[:8], 0.0), image[8:rows + 8],
                jnp.where(lat < lat_count - 1, image[rows + 8:], 0.0))
        return jnp.concatenate(ends, axis=0)

    for k in range(3):
        @pl.loop(0, BLOCKS + 2, unroll=17)
        def _(i, k=k):
            v_refs[k + 1][i, 8:8 + tall] = applied(k, i)

    def products(i, carry):
        last = applied(3, i + 1)[8:8 + rows]
        q = [v_refs[k][i + 1, 16:16 + rows] for k in range(4)] + [last]
        for k in range(5):
            q_ref[k, i] = q[k]
        out = []
        for total, (a, b) in zip(carry, PAIRS):
            term = q[a] * q[b]
            out.append(total + sum(term[8 * n:8 * n + 8] for n in range(rows // 8)))
        return tuple(out)

    zero = tuple(jnp.zeros((8, BW), F32) for _ in PAIRS)
    totals = lax.fori_loop(0, BLOCKS, products, zero, unroll=4)
    lane1 = lax.broadcasted_iota(jnp.int32, (1, BW), 1)
    gram = jnp.zeros((1, BW), F32)
    for n, total in enumerate(totals):
        value = jnp.sum(jnp.sum(total, axis=0, keepdims=True), axis=1, keepdims=True)
        gram = jnp.where(lane1 == n, value, gram)
    gram_ref[...] = gram


def basis(place, rhs, diag, up, south, north, west, east):
    rows = rhs.shape[1]
    vmem = pl.BlockSpec(memory_space=pltpu.VMEM)
    return pl.pallas_call(
        basis_kernel,
        out_shape=[
            jax.ShapeDtypeStruct((5, BLOCKS, rows, BW), F32),
            jax.ShapeDtypeStruct((1, BW), F32),
        ],
        in_specs=[pl.BlockSpec(memory_space=pltpu.SMEM)] + [vmem] * 7,
        out_specs=[vmem, vmem],
        scratch_shapes=[
            pltpu.VMEM((BLOCKS + 2, rows + 16, BW), F32),
        ] + [pltpu.VMEM((BLOCKS + 2, rows + 32, BW), F32)] * 4,
        compiler_params=pltpu.CompilerParams(vmem_limit_bytes=VMEM_BYTES),
        name="basis",
    )(place, rhs, diag, up, south, north, west, east)


def solved(gram):
    g = {}
    for n, (a, b) in enumerate(PAIRS):
        g[a, b] = g[b, a] = gram[n]
    m = [[None] * 4 for _ in range(4)]
    for j in range(4):
        for i in range(j + 1):
            if j == 0:
                value = MID * g[i, 0] + HALF * g[i, 1]
            else:
                value = MID * g[i, j] + (0.5 * HALF) * (g[i, j + 1] + g[i, j - 1])
            m[i][j] = m[j][i] = value
    y = [g[0, i] for i in range(4)]
    inverse = []
    factor = [[None] * 4 for _ in range(4)]
    for k in range(4):
        pivot = m[k][k]
        inverse.append(jnp.where(pivot > 0.0, 1.0 / jnp.where(pivot > 0.0, pivot, 1.0), 0.0))
        for i in range(k + 1, 4):
            factor[i][k] = m[k][i] * inverse[k]
        for i in range(k + 1, 4):
            for j in range(i, 4):
                m[i][j] = m[i][j] - factor[i][k] * m[k][j]
            y[i] = y[i] - factor[i][k] * y[k]
    c = [y[k] * inverse[k] for k in range(4)]
    for k in range(3, -1, -1):
        for i in range(k):
            c[i] = c[i] - factor[k][i] * c[k]
    half = 0.5 * HALF
    r = [
        1.0 - (MID * c[0] + half * c[1]),
        -(HALF * c[0] + MID * c[1] + half * c[2]),
        -(half * c[1] + MID * c[2] + half * c[3]),
        -(half * c[2] + MID * c[3]),
        -(half * c[3]),
    ]
    return c, r


def combine_kernel(gram_ref, q_ref, x_ref, r_ref, c_ref):
    @pl.when(pl.program_id(0) == 0)
    def _():
        gram = jnp.sum(gram_ref[...], axis=0, keepdims=True)
        lane = lax.broadcasted_iota(jnp.int32, (1, BW), 1)
        pick = lambda n: jnp.sum(jnp.where(lane == n, gram, 0.0), axis=1, keepdims=True)
        c, r = solved([pick(n) for n in range(len(PAIRS))])
        for n, value in enumerate(c + r):
            c_ref[n] = jnp.broadcast_to(value, (8, BW))

    rows = q_ref.shape[2]
    factors = [jnp.concatenate([c_ref[n]] * (rows // 8), axis=0) for n in range(9)]
    for i in range(q_ref.shape[1]):
        q = [q_ref[k, i] for k in range(5)]
        columns = slice(i * BW, (i + 1) * BW)
        x_ref[:, columns] = sum(factors[k] * q[k] for k in range(4))
        r_ref[:, columns] = sum(factors[4 + k] * q[k] for k in range(5))


def combine(gram, q, batch=8):
    _, blocks, rows, _ = q.shape
    out = jax.ShapeDtypeStruct((rows, blocks * BW), F32)
    spec = pl.BlockSpec((rows, batch * BW), lambda i: (0, i))
    return pl.pallas_call(
        combine_kernel,
        grid=(blocks // batch,),
        out_shape=[out, out],
        in_specs=[
            pl.BlockSpec(gram.shape, lambda i: (0, 0)),
            pl.BlockSpec((5, batch, rows, BW), lambda i: (0, i, 0, 0)),
        ],
        out_specs=[spec, spec],
        scratch_shapes=[pltpu.VMEM((9, 8, BW), F32)],
        compiler_params=pltpu.CompilerParams(vmem_limit_bytes=VMEM_BYTES),
        name="combine",
    )(gram, q)


def body(piece_height, piece_weight, piece_column, piece_width):
    lon_count, lat_count = lax.axis_size("lon"), lax.axis_size("lat")
    lon, lat = lax.axis_index("lon"), lax.axis_index("lat")
    place = jnp.stack([lon, lat, jnp.int32(lat_count)]).astype(jnp.int32)

    packed = pack(piece_column, piece_height, piece_weight, lon_count)
    got = lax.all_to_all(packed, "lon", split_axis=0, concat_axis=0, tiled=True)

    small = exchanged(small_messages(piece_height, piece_column, piece_width, lon), lon_count)
    facts = small[:, CAPACITY, :2 * CAPACITY].astype(jnp.int32).reshape(-1)

    rhs, diag, up, down, edge = sums(place, facts, got, small)
    south = passed_along(up, "lat", 1)
    north = passed_along(down, "lat", -1)
    to_west = jnp.concatenate([edge[0], south[0], north[0]], axis=0)
    to_east = jnp.concatenate([edge[1], south[-1], north[-1]], axis=0)
    west = passed_around(to_east, "lon", 1)
    east = passed_around(to_west, "lon", -1)
    q, gram = basis(place, rhs, diag, up, south, north, west, east)
    spread = jnp.broadcast_to(gram[None], (lon_count * lat_count, 1, BW))
    grams = lax.all_to_all(spread, ("lon", "lat"), split_axis=0, concat_axis=0, tiled=True)
    return tuple(combine(grams.reshape(lon_count * lat_count, BW), q))


def solution(mesh):
    return jax.shard_map(
        body,
        mesh=mesh,
        in_specs=(P("lon", "lat", None), P("lon", "lat", None), P("lon"), P("lon")),
        out_specs=(P("lat", "lon"), P("lat", "lon")),
        check_vma=False,
    )
```

```python
import jax
import jax.numpy as jnp
from jax import lax
from jax.experimental import pallas as pl
from jax.experimental.pallas import tpu as pltpu
from jax.sharding import PartitionSpec as P

ROWS = 128
COLS_DEV = 4096
BW = 128
BLOCKS = COLS_DEV // BW
CAPACITY = 2

MU_DATA = 0.5
DAMPING = 0.5
RIDGE = 0.05

MID = 5.5
HALF = 5.5
VMEM_BYTES = 40 * 1024 * 1024
PACK_VMEM_BYTES = 60 * 1024 * 1024
F32 = jnp.float32


def passed_along(block, axis, distance):
    devices = range(lax.axis_size(axis))
    route = [(i, i + distance) for i in devices if i + distance in devices]
    return lax.ppermute(block, axis, route)


def passed_around(block, axis, distance):
    count = lax.axis_size(axis)
    return lax.ppermute(block, axis, [(i, (i + distance) % count) for i in range(count)])


def pack_kernel(column_ref, height_ref, weight_ref, out_ref, held_ref, count_ref, in_sem, out_sem):
    tiles, pieces = out_ref.shape[0], height_ref.shape[0]
    rows = height_ref.shape[1]
    batch = pieces // in_sem.shape[0]

    def loads(g):
        part = pl.ds(g * batch, batch)
        sources = (height_ref, weight_ref)
        return [pltpu.make_async_copy(source.at[part], held_ref.at[part, pl.ds(n * rows, rows)],
                                      in_sem.at[g, n]) for n, source in enumerate(sources)]

    for g in range(in_sem.shape[0]):
        for load in loads(g):
            load.start()

    @pl.loop(0, tiles, unroll=8)
    def _(t):
        count_ref[t] = 0

    for g in range(in_sem.shape[0]):
        for load in loads(g):
            load.wait()

        @pl.loop(g * batch, (g + 1) * batch, unroll=4)
        def _(p):
            tile = column_ref[p] // COLS_DEV
            slot = count_ref[tile]
            count_ref[tile] = slot + 1
            pltpu.make_async_copy(held_ref.at[p], out_ref.at[tile, slot, pl.ds(0, 2 * rows)],
                                  out_sem).start()

    pltpu.make_async_copy(held_ref, out_ref.at[pl.ds(0, pieces), 0, pl.ds(0, 2 * rows)],
                          out_sem).wait()


def pack(piece_column, piece_height, piece_weight, tiles, batches=8):
    pieces, rows, _ = piece_height.shape
    tall = lambda array: array.reshape(pieces, rows, 1, BW)
    return pl.pallas_call(
        pack_kernel,
        out_shape=jax.ShapeDtypeStruct((tiles, CAPACITY, 2 * rows + 2, 1, BW), F32),
        in_specs=[
            pl.BlockSpec(memory_space=pltpu.SMEM),
            pl.BlockSpec(memory_space=pl.ANY),
            pl.BlockSpec(memory_space=pl.ANY),
        ],
        out_specs=pl.BlockSpec(memory_space=pl.ANY),
        scratch_shapes=[
            pltpu.VMEM((pieces, 2 * rows, 1, BW), F32),
            pltpu.SMEM((tiles,), jnp.int32),
            pltpu.SemaphoreType.DMA((batches, 2)),
            pltpu.SemaphoreType.DMA,
        ],
        compiler_params=pltpu.CompilerParams(vmem_limit_bytes=PACK_VMEM_BYTES),
        name="pack",
    )(piece_column, tall(piece_height), tall(piece_weight))


def label_kernel(column_ref, width_ref, source_ref, packed_ref, out_ref, first_ref, held_ref,
                 count_ref, sem):
    tiles, pieces = out_ref.shape[0], first_ref.shape[0]
    end = out_ref.shape[2]
    load = pltpu.make_async_copy(source_ref, first_ref, sem.at[0])
    load.start()
    lane = lax.broadcasted_iota(jnp.int32, (1, BW), 1)
    held_ref[...] = jnp.zeros_like(held_ref)

    @pl.loop(0, tiles, unroll=8)
    def _(t):
        count_ref[t] = 0

    load.wait()

    @pl.loop(0, pieces, unroll=4)
    def _(p):
        tile = column_ref[p] // COLS_DEV
        block = column_ref[p] % COLS_DEV // BW
        slot = count_ref[tile]
        count_ref[tile] = slot + 1
        held_ref[tile, slot, 0] = first_ref[p]
        facts = jnp.where(lane == 0, block + 1, jnp.where(lane == 1, width_ref[p], 0))
        held_ref[tile, slot, 1] = facts.astype(F32)

    copy = pltpu.make_async_copy(held_ref, out_ref.at[:, :, pl.ds(end - 2, 2)], sem.at[1])
    copy.start()
    copy.wait()


def label(piece_column, piece_width, next_first, packed):
    tiles = packed.shape[0]
    return pl.pallas_call(
        label_kernel,
        out_shape=jax.ShapeDtypeStruct(packed.shape, F32),
        in_specs=[
            pl.BlockSpec(memory_space=pltpu.SMEM),
            pl.BlockSpec(memory_space=pltpu.SMEM),
            pl.BlockSpec(memory_space=pl.ANY),
            pl.BlockSpec(memory_space=pl.ANY),
        ],
        out_specs=pl.BlockSpec(memory_space=pl.ANY),
        scratch_shapes=[
            pltpu.VMEM(next_first.shape, F32),
            pltpu.VMEM((tiles, CAPACITY, 2, 1, BW), F32),
            pltpu.SMEM((tiles,), jnp.int32),
            pltpu.SemaphoreType.DMA((2,)),
        ],
        input_output_aliases={3: 0},
        compiler_params=pltpu.CompilerParams(vmem_limit_bytes=PACK_VMEM_BYTES),
        name="label",
    )(piece_column, piece_width, next_first, packed)


def sums_kernel(place_ref, facts_ref, got_ref, rhs_ref, diag_ref, up_ref, down_ref, edge_ref,
                total_ref):
    step, steps = pl.program_id(0), pl.num_programs(0)
    rows = rhs_ref.shape[1]
    part = 2 * rows + 2
    slots = got_ref.shape[0] // part
    lat, lat_count = place_ref[0], place_ref[1]
    lane = lax.broadcasted_iota(jnp.int32, (rows, BW), 1)
    row = lax.broadcasted_iota(jnp.int32, (rows, BW), 0)

    @pl.when(step == 0)
    def _():
        total_ref[...] = jnp.zeros_like(total_ref)

    for s in range(slots):
        block = facts_ref[2 * (step * slots + s)] - 1
        block = jnp.where(block < 0, BLOCKS, block)
        width = facts_ref[2 * (step * slots + s) + 1]
        height = got_ref[s * part:s * part + rows]
        weight = got_ref[s * part + rows:s * part + 2 * rows]
        above = got_ref[s * part + 2 * rows:s * part + 2 * rows + 1]
        cell = jnp.where(lane < width, weight, 0.0)
        east = jnp.where(lane < width - 1, weight, 0.0)
        east_step = pltpu.roll(height, BW - 1, 1) - height
        raised = jnp.where(row == rows - 1, above, pltpu.roll(height, rows - 1, 0))
        terms = (cell, cell * height, east, east * east_step, cell * (raised - height))
        for n, term in enumerate(terms):
            total_ref[block, n] += term

    @pl.when(step == steps - 1)
    def _():
        last = (row == rows - 1) & (lat == lat_count - 1)
        first = (row == 0) & (lat == 0)
        sides = 4.0 - last.astype(F32) - first.astype(F32) + RIDGE
        row8 = row[:8]

        @pl.loop(0, BLOCKS, unroll=4)
        def _(i):
            cell, height = total_ref[i, 0], total_ref[i, 1]
            east = total_ref[i, 3] / (total_ref[i, 2] + DAMPING)
            north = jnp.where(last, 0.0, total_ref[i, 4] / (cell + DAMPING))
            south = jnp.where(row == 0, 0.0, pltpu.roll(north, 1, 0))
            rhs = MU_DATA * height - (east - pltpu.roll(east, 1, 1)) - (north - south)
            diag = MU_DATA * cell + sides
            rhs_ref[i] = rhs
            diag_ref[i] = diag
            top = pltpu.roll(diag[rows - 8:], 4, 0)
            top = jnp.where(row8 == 0, pltpu.roll(north[rows - 8:], 1, 0), top)
            up_ref[i] = jnp.where(row8 >= 4, rhs[rows - 8:], top)
            down_ref[i] = jnp.where(row8 >= 4, pltpu.roll(diag[:8], 4, 0), rhs[:8])

        for side, block in ((0, 0), (1, BLOCKS - 1)):
            edge_ref[side, 0:rows] = rhs_ref[block]
            edge_ref[side, rows:2 * rows] = diag_ref[block]
            edge_ref[side, 2 * rows:2 * rows + 8] = up_ref[block]


def sums(place, facts, got, rows, batch=8):
    part = 2 * rows + 2
    slots = got.shape[0] // part
    whole = lambda *shape: pl.BlockSpec(shape, lambda i: (0,) * len(shape))
    field = (BLOCKS, rows, BW)
    strip = (BLOCKS, 8, BW)
    edge = (2, 2 * rows + 8, BW)
    return pl.pallas_call(
        sums_kernel,
        grid=(slots // (2 * batch),),
        out_shape=[jax.ShapeDtypeStruct(s, F32) for s in (field, field, strip, strip, edge)],
        in_specs=[
            pl.BlockSpec(memory_space=pltpu.SMEM),
            pl.BlockSpec(memory_space=pltpu.SMEM),
            pl.BlockSpec((2 * batch * part, BW), lambda i: (i, 0)),
        ],
        out_specs=[whole(*s) for s in (field, field, strip, strip, edge)],
        scratch_shapes=[pltpu.VMEM((BLOCKS + 1, 5, rows, BW), F32)],
        compiler_params=pltpu.CompilerParams(vmem_limit_bytes=VMEM_BYTES),
        name="sums",
    )(place, facts, got)


PAIRS = [(i, j) for j in range(5) for i in range(min(j, 3) + 1)]


def basis_kernel(place_ref, rhs_ref, diag_ref, up_ref, south_ref, north_ref, west_ref, east_ref,
                 q_ref, gram_ref, scale_ref, *v_refs):
    rows = rhs_ref.shape[1]
    tall = rows + 16
    lat, lat_count = place_ref[0], place_ref[1]
    row = lax.broadcasted_iota(jnp.int32, (rows, BW), 0)
    row8 = row[:8]
    lane = lax.broadcasted_iota(jnp.int32, (tall, BW), 1)

    def assemble(i, rhs, diag, up, south, north):
        first = jnp.where(row == 0, south[0:1], 0.0) + rhs
        below = jnp.where(row8 >= 4, south, 0.0)
        above = jnp.where(row8 == 0, north + up, jnp.where(row8 < 4, north, 0.0))
        v_refs[0][i, 8:8 + tall] = jnp.concatenate([below, first, above], axis=0)
        diag = jnp.concatenate([pltpu.roll(south, 4, 0), diag, pltpu.roll(north, 4, 0)], axis=0)
        scale_ref[i] = (diag - MID) * (2.0 / HALF)

    for i, ref in ((0, west_ref), (BLOCKS + 1, east_ref)):
        two = 2 * rows
        assemble(i, ref[0:rows], ref[rows:two], ref[two:two + 8], ref[two + 8:two + 16],
                 ref[two + 16:two + 24])

    @pl.loop(0, BLOCKS, unroll=4)
    def _(i):
        assemble(i + 1, rhs_ref[i], diag_ref[i], up_ref[i], south_ref[i], north_ref[i])

    def applied(k, i):
        body = slice(8, 8 + tall)
        v = v_refs[k][i, body]
        left = v_refs[k][jnp.maximum(i - 1, 0), body]
        right = v_refs[k][jnp.minimum(i + 1, BLOCKS + 1), body]
        west = pltpu.roll(jnp.where(lane == BW - 1, left, v), 1, 1)
        east = pltpu.roll(jnp.where(lane == 0, right, v), BW - 1, 1)
        south = v_refs[k][i, 7:7 + tall]
        north = v_refs[k][i, 9:9 + tall]
        image = scale_ref[i] * v - (2.0 / HALF) * ((west + east) + (south + north))
        if k == 0:
            image = 0.5 * image
        else:
            image = image - v_refs[k - 1][i, body]
        ends = (jnp.where(lat > 0, image[:8], 0.0), image[8:rows + 8],
                jnp.where(lat < lat_count - 1, image[rows + 8:], 0.0))
        return jnp.concatenate(ends, axis=0)

    for k in range(3):
        @pl.loop(0, BLOCKS + 2, unroll=17)
        def _(i, k=k):
            v_refs[k + 1][i, 8:8 + tall] = applied(k, i)

    def products(i, carry):
        last = applied(3, i + 1)[8:8 + rows]
        q = [v_refs[k][i + 1, 16:16 + rows] for k in range(4)] + [last]
        for k in range(5):
            q_ref[k, i] = q[k]
        out = []
        for total, (a, b) in zip(carry, PAIRS):
            term = q[a] * q[b]
            out.append(total + sum(term[8 * n:8 * n + 8] for n in range(rows // 8)))
        return tuple(out)

    zero = tuple(jnp.zeros((8, BW), F32) for _ in PAIRS)
    totals = lax.fori_loop(0, BLOCKS, products, zero, unroll=4)
    lane1 = lax.broadcasted_iota(jnp.int32, (1, BW), 1)
    gram = jnp.zeros((1, BW), F32)
    for n, total in enumerate(totals):
        value = jnp.sum(jnp.sum(total, axis=0, keepdims=True), axis=1, keepdims=True)
        gram = jnp.where(lane1 == n, value, gram)
    gram_ref[...] = gram


def basis(place, rhs, diag, up, south, north, west, east):
    rows = rhs.shape[1]
    vmem = pl.BlockSpec(memory_space=pltpu.VMEM)
    return pl.pallas_call(
        basis_kernel,
        out_shape=[
            jax.ShapeDtypeStruct((5, BLOCKS, rows, BW), F32),
            jax.ShapeDtypeStruct((1, BW), F32),
        ],
        in_specs=[pl.BlockSpec(memory_space=pltpu.SMEM)] + [vmem] * 7,
        out_specs=[vmem, vmem],
        scratch_shapes=[
            pltpu.VMEM((BLOCKS + 2, rows + 16, BW), F32),
        ] + [pltpu.VMEM((BLOCKS + 2, rows + 32, BW), F32)] * 4,
        compiler_params=pltpu.CompilerParams(vmem_limit_bytes=VMEM_BYTES),
        name="basis",
    )(place, rhs, diag, up, south, north, west, east)


def solved(gram):
    g = {}
    for n, (a, b) in enumerate(PAIRS):
        g[a, b] = g[b, a] = gram[n]
    m = [[None] * 4 for _ in range(4)]
    for j in range(4):
        for i in range(j + 1):
            if j == 0:
                value = MID * g[i, 0] + HALF * g[i, 1]
            else:
                value = MID * g[i, j] + (0.5 * HALF) * (g[i, j + 1] + g[i, j - 1])
            m[i][j] = m[j][i] = value
    y = [g[0, i] for i in range(4)]
    inverse = []
    factor = [[None] * 4 for _ in range(4)]
    for k in range(4):
        pivot = m[k][k]
        inverse.append(jnp.where(pivot > 0.0, 1.0 / jnp.where(pivot > 0.0, pivot, 1.0), 0.0))
        for i in range(k + 1, 4):
            factor[i][k] = m[k][i] * inverse[k]
        for i in range(k + 1, 4):
            for j in range(i, 4):
                m[i][j] = m[i][j] - factor[i][k] * m[k][j]
            y[i] = y[i] - factor[i][k] * y[k]
    c = [y[k] * inverse[k] for k in range(4)]
    for k in range(3, -1, -1):
        for i in range(k):
            c[i] = c[i] - factor[k][i] * c[k]
    half = 0.5 * HALF
    r = [
        1.0 - (MID * c[0] + half * c[1]),
        -(HALF * c[0] + MID * c[1] + half * c[2]),
        -(half * c[1] + MID * c[2] + half * c[3]),
        -(half * c[2] + MID * c[3]),
        -(half * c[3]),
    ]
    return c, r


def combine_kernel(gram_ref, q_ref, x_ref, r_ref, c_ref):
    @pl.when(pl.program_id(0) == 0)
    def _():
        gram = jnp.sum(gram_ref[...], axis=0, keepdims=True)
        lane = lax.broadcasted_iota(jnp.int32, (1, BW), 1)
        pick = lambda n: jnp.sum(jnp.where(lane == n, gram, 0.0), axis=1, keepdims=True)
        c, r = solved([pick(n) for n in range(len(PAIRS))])
        for n, value in enumerate(c + r):
            c_ref[n] = jnp.broadcast_to(value, (8, BW))

    rows = q_ref.shape[2]
    factors = [jnp.concatenate([c_ref[n]] * (rows // 8), axis=0) for n in range(9)]
    for i in range(q_ref.shape[1]):
        q = [q_ref[k, i] for k in range(5)]
        columns = slice(i * BW, (i + 1) * BW)
        x_ref[:, columns] = sum(factors[k] * q[k] for k in range(4))
        r_ref[:, columns] = sum(factors[4 + k] * q[k] for k in range(5))


def combine(gram, q, batch=8):
    _, blocks, rows, _ = q.shape
    out = jax.ShapeDtypeStruct((rows, blocks * BW), F32)
    spec = pl.BlockSpec((rows, batch * BW), lambda i: (0, i))
    return pl.pallas_call(
        combine_kernel,
        grid=(blocks // batch,),
        out_shape=[out, out],
        in_specs=[
            pl.BlockSpec(gram.shape, lambda i: (0, 0)),
            pl.BlockSpec((5, batch, rows, BW), lambda i: (0, i, 0, 0)),
        ],
        out_specs=[spec, spec],
        scratch_shapes=[pltpu.VMEM((9, 8, BW), F32)],
        compiler_params=pltpu.CompilerParams(vmem_limit_bytes=VMEM_BYTES),
        name="combine",
    )(gram, q)


def body(piece_height, piece_weight, piece_column, piece_width):
    lon_count, lat_count = lax.axis_size("lon"), lax.axis_size("lat")
    rows = piece_height.shape[1]
    place = jnp.stack([lax.axis_index("lat"), jnp.int32(lat_count)]).astype(jnp.int32)

    next_first = passed_along(piece_height[:, :1, :], "lat", -1)
    packed = pack(piece_column, piece_height, piece_weight, lon_count)
    labelled = label(piece_column, piece_width, next_first, packed)
    got = lax.all_to_all(labelled, "lon", split_axis=0, concat_axis=0, tiled=True)
    facts = got[:, :, -1, 0, :2].astype(jnp.int32).reshape(-1)
    got = got.reshape(lon_count * CAPACITY * (2 * rows + 2), BW)
    rhs, diag, up, down, edge = sums(place, facts, got, rows)
    south = passed_along(up, "lat", 1)
    north = passed_along(down, "lat", -1)
    to_west = jnp.concatenate([edge[0], south[0], north[0]], axis=0)
    to_east = jnp.concatenate([edge[1], south[-1], north[-1]], axis=0)
    west = passed_around(to_east, "lon", 1)
    east = passed_around(to_west, "lon", -1)
    q, gram = basis(place, rhs, diag, up, south, north, west, east)
    spread = jnp.broadcast_to(gram[None], (lon_count * lat_count, 1, BW))
    grams = lax.all_to_all(spread, ("lon", "lat"), split_axis=0, concat_axis=0, tiled=True)
    return tuple(combine(grams.reshape(lon_count * lat_count, BW), q))


def solution(mesh):
    return jax.shard_map(
        body,
        mesh=mesh,
        in_specs=(P("lon", "lat", None), P("lon", "lat", None), P("lon"), P("lon")),
        out_specs=(P("lat", "lon"), P("lat", "lon")),
        check_vma=False,
    )
```

```python
import jax
import jax.numpy as jnp
from jax import lax
from jax.experimental import pallas as pl
from jax.experimental.pallas import tpu as pltpu
from jax.sharding import PartitionSpec as P

ROWS = 128
COLS_DEV = 4096
BW = 128
BLOCKS = COLS_DEV // BW
CAPACITY = 2

MU_DATA = 0.5
DAMPING = 0.5
RIDGE = 0.05

MID = 5.5
HALF = 5.5
VMEM_BYTES = 40 * 1024 * 1024
PACK_VMEM_BYTES = 60 * 1024 * 1024
SOME_VMEM_BYTES = 50 * 1024 * 1024
F32 = jnp.float32


def passed_along(block, axis, distance):
    devices = range(lax.axis_size(axis))
    route = [(i, i + distance) for i in devices if i + distance in devices]
    return lax.ppermute(block, axis, route)


def swapped(block, axis, start, around):
    count = lax.axis_size(axis)
    lows = range(start, count if around else count - 1, 2)
    pairs = [(low, (low + 1) % count) for low in lows]
    return lax.ppermute(block, axis, pairs + [(b, a) for a, b in pairs])


def pack_kernel(column_ref, width_ref, height_ref, weight_ref, out_ref, held_ref, facts_ref,
                count_ref, in_sem, out_sem, facts_sem):
    tiles, pieces = out_ref.shape[0], height_ref.shape[0]
    rows = height_ref.shape[1]
    batch = pieces // in_sem.shape[0]
    lane = lax.broadcasted_iota(jnp.int32, (1, BW), 1)

    def loads(g):
        part = pl.ds(g * batch, batch)
        sources = (height_ref, weight_ref)
        return [pltpu.make_async_copy(source.at[part], held_ref.at[part, pl.ds(n * rows, rows)],
                                      in_sem.at[g, n]) for n, source in enumerate(sources)]

    for g in range(in_sem.shape[0]):
        for load in loads(g):
            load.start()

    facts_ref[...] = jnp.zeros_like(facts_ref)

    @pl.loop(0, tiles, unroll=8)
    def _(t):
        count_ref[t] = 0

    for g in range(in_sem.shape[0]):
        for load in loads(g):
            load.wait()

        @pl.loop(g * batch, (g + 1) * batch, unroll=4)
        def _(p):
            tile = column_ref[p] // COLS_DEV
            block = column_ref[p] % COLS_DEV // BW
            slot = count_ref[tile]
            count_ref[tile] = slot + 1
            facts = jnp.where(lane == 0, block + 1, jnp.where(lane == 1, width_ref[p], 0))
            facts_ref[tile, slot] = facts.astype(F32)
            pltpu.make_async_copy(held_ref.at[p], out_ref.at[tile, slot, pl.ds(0, 2 * rows)],
                                  out_sem).start()

    facts = pltpu.make_async_copy(facts_ref, out_ref.at[:, :, 2 * rows + 1], facts_sem)
    facts.start()
    pltpu.make_async_copy(held_ref, out_ref.at[pl.ds(0, pieces), 0, pl.ds(0, 2 * rows)],
                          out_sem).wait()
    facts.wait()


def pack(piece_column, piece_width, piece_height, piece_weight, tiles, batches=8):
    pieces, rows, _ = piece_height.shape
    tall = lambda array: array.reshape(pieces, rows, 1, BW)
    return pl.pallas_call(
        pack_kernel,
        out_shape=jax.ShapeDtypeStruct((tiles, CAPACITY, 2 * rows + 2, 1, BW), F32),
        in_specs=[
            pl.BlockSpec(memory_space=pltpu.SMEM),
            pl.BlockSpec(memory_space=pltpu.SMEM),
            pl.BlockSpec(memory_space=pl.ANY),
            pl.BlockSpec(memory_space=pl.ANY),
        ],
        out_specs=pl.BlockSpec(memory_space=pl.ANY),
        scratch_shapes=[
            pltpu.VMEM((pieces, 2 * rows, 1, BW), F32),
            pltpu.VMEM((tiles, CAPACITY, 1, BW), F32),
            pltpu.SMEM((tiles,), jnp.int32),
            pltpu.SemaphoreType.DMA((batches, 2)),
            pltpu.SemaphoreType.DMA,
            pltpu.SemaphoreType.DMA,
        ],
        compiler_params=pltpu.CompilerParams(vmem_limit_bytes=PACK_VMEM_BYTES),
        name="pack",
    )(piece_column, piece_width, tall(piece_height), tall(piece_weight))


def label_kernel(column_ref, first_ref, packed_ref, out_ref, count_ref, sem):
    tiles, pieces = out_ref.shape[0], first_ref.shape[0]
    end = out_ref.shape[2]

    @pl.loop(0, tiles, unroll=8)
    def _(t):
        count_ref[t] = 0

    @pl.loop(0, pieces, unroll=8)
    def _(p):
        tile = column_ref[p] // COLS_DEV
        slot = count_ref[tile]
        count_ref[tile] = slot + 1
        pltpu.make_async_copy(first_ref.at[p], out_ref.at[tile, slot, end - 2], sem).start()

    pltpu.make_async_copy(first_ref, out_ref.at[pl.ds(0, pieces), 0, end - 2], sem).wait()


def label(piece_column, next_first, packed):
    return pl.pallas_call(
        label_kernel,
        out_shape=jax.ShapeDtypeStruct(packed.shape, F32),
        in_specs=[
            pl.BlockSpec(memory_space=pltpu.SMEM),
            pl.BlockSpec(memory_space=pltpu.VMEM),
            pl.BlockSpec(memory_space=pl.ANY),
        ],
        out_specs=pl.BlockSpec(memory_space=pl.ANY),
        scratch_shapes=[
            pltpu.SMEM(packed.shape[:1], jnp.int32),
            pltpu.SemaphoreType.DMA,
        ],
        input_output_aliases={2: 0},
        compiler_params=pltpu.CompilerParams(vmem_limit_bytes=SOME_VMEM_BYTES),
        name="label",
    )(piece_column, next_first, packed)


def sums_kernel(place_ref, got_ref, rows_ref, rhs_ref, diag_ref, one_ref, two_ref, edge_ref,
                held_ref, facts_ref, total_ref, facts_sem, sem):
    rows = rhs_ref.shape[1]
    part = 2 * rows + 2
    chunks, height, _ = held_ref.shape
    slots = height // part
    lat, lat_count, lon = place_ref[0], place_ref[1], place_ref[2]
    lane = lax.broadcasted_iota(jnp.int32, (rows, BW), 1)
    row = lax.broadcasted_iota(jnp.int32, (rows, BW), 0)

    def load(n):
        rows_of = rows_ref.at[pl.ds(n * height, height)]
        return pltpu.make_async_copy(rows_of, held_ref.at[n], sem.at[n])

    facts = pltpu.make_async_copy(got_ref.at[:, :, part - 1], facts_ref, facts_sem)
    facts.start()
    for n in range(chunks):
        load(n).start()
    total_ref[...] = jnp.zeros_like(total_ref)
    facts.wait()

    @pl.loop(0, chunks)
    def _(n):
        load(n).wait()
        for s in range(slots):
            source, slot = n * (slots // CAPACITY) + s // CAPACITY, s % CAPACITY
            block = facts_ref[source, slot, 0, 0].astype(jnp.int32) - 1
            block = jnp.where(block < 0, BLOCKS, block)
            width = facts_ref[source, slot, 0, 1].astype(jnp.int32)
            height = held_ref[n, s * part:s * part + rows]
            weight = held_ref[n, s * part + rows:s * part + 2 * rows]
            above = held_ref[n, s * part + 2 * rows:s * part + 2 * rows + 1]
            cell = jnp.where(lane < width, weight, 0.0)
            east = jnp.where(lane < width - 1, weight, 0.0)
            east_step = pltpu.roll(height, BW - 1, 1) - height
            raised = jnp.where(row == rows - 1, above, pltpu.roll(height, rows - 1, 0))
            terms = (cell, cell * height, east, east * east_step, cell * (raised - height))
            for k, term in enumerate(terms):
                total_ref[block, k] += term

    last = (row == rows - 1) & (lat == lat_count - 1)
    first = (row == 0) & (lat == 0)
    sides = 4.0 - last.astype(F32) - first.astype(F32) + RIDGE
    row8 = row[:8]
    lat_even = lat % 2 == 0

    @pl.loop(0, BLOCKS, unroll=4)
    def _(i):
        cell, height = total_ref[i, 0], total_ref[i, 1]
        east = total_ref[i, 3] / (total_ref[i, 2] + DAMPING)
        north = jnp.where(last, 0.0, total_ref[i, 4] / (cell + DAMPING))
        south = jnp.where(row == 0, 0.0, pltpu.roll(north, 1, 0))
        rhs = MU_DATA * height - (east - pltpu.roll(east, 1, 1)) - (north - south)
        diag = MU_DATA * cell + sides
        rhs_ref[i] = rhs
        diag_ref[i] = diag
        top = pltpu.roll(diag[rows - 8:], 4, 0)
        top = jnp.where(row8 == 0, pltpu.roll(north[rows - 8:], 1, 0), top)
        up = jnp.where(row8 >= 4, rhs[rows - 8:], top)
        down = jnp.where(row8 >= 4, pltpu.roll(diag[:8], 4, 0), rhs[:8])
        one_ref[i] = jnp.where(lat_even, up, down)
        two_ref[i] = jnp.where(lat_even, down, up)

    first_edge = (BLOCKS - 1) * (1 - lon % 2)
    for side, block in ((0, first_edge), (1, BLOCKS - 1 - first_edge)):
        edge_ref[side, 0:rows] = rhs_ref[block]
        edge_ref[side, rows:2 * rows] = diag_ref[block]
        up = jnp.where(lat_even, one_ref[block], two_ref[block])
        edge_ref[side, 2 * rows:2 * rows + 8] = up


def sums(place, got, rows, chunks=4):
    tiles, _, part, _, _ = got.shape
    height = tiles * CAPACITY * part // chunks
    field = (BLOCKS, rows, BW)
    strip = (BLOCKS, 8, BW)
    edge = (2, 2 * rows + 8, BW)
    vmem = pl.BlockSpec(memory_space=pltpu.VMEM)
    return pl.pallas_call(
        sums_kernel,
        out_shape=[jax.ShapeDtypeStruct(s, F32) for s in (field, field, strip, strip, edge)],
        in_specs=[
            pl.BlockSpec(memory_space=pltpu.SMEM),
            pl.BlockSpec(memory_space=pl.ANY),
            pl.BlockSpec(memory_space=pl.ANY),
        ],
        out_specs=[vmem] * 5,
        scratch_shapes=[
            pltpu.VMEM((chunks, height, BW), F32),
            pltpu.SMEM((tiles, CAPACITY, 1, BW), F32),
            pltpu.VMEM((BLOCKS + 1, 5, rows, BW), F32),
            pltpu.SemaphoreType.DMA,
            pltpu.SemaphoreType.DMA((chunks,)),
        ],
        compiler_params=pltpu.CompilerParams(vmem_limit_bytes=VMEM_BYTES),
        name="sums",
    )(place, got, got.reshape(chunks * height, BW))


PAIRS = [(i, j) for j in range(5) for i in range(min(j, 3) + 1)]


def basis_kernel(place_ref, rhs_ref, diag_ref, own_one_ref, own_two_ref, one_ref, two_ref,
                 lon_one_ref, lon_two_ref, q_ref, gram_ref, scale_ref, *v_refs):
    rows = rhs_ref.shape[1]
    tall = rows + 16
    lat, lat_count, lon = place_ref[0], place_ref[1], place_ref[2]
    lat_even = lat % 2 == 0
    row = lax.broadcasted_iota(jnp.int32, (rows, BW), 0)
    row8 = row[:8]
    lane = lax.broadcasted_iota(jnp.int32, (tall, BW), 1)

    def assemble(i, rhs, diag, up, one, two):
        south = jnp.where(lat_even, two, one)
        north = jnp.where(lat_even, one, two)
        first = jnp.where(row == 0, south[0:1], 0.0) + rhs
        below = jnp.where(row8 >= 4, south, 0.0)
        above = jnp.where(row8 == 0, north + up, jnp.where(row8 < 4, north, 0.0))
        v_refs[0][i, 8:8 + tall] = jnp.concatenate([below, first, above], axis=0)
        diag = jnp.concatenate([pltpu.roll(south, 4, 0), diag, pltpu.roll(north, 4, 0)], axis=0)
        scale_ref[i] = (diag - MID) * (2.0 / HALF)

    side = (BLOCKS + 1) * (1 - lon % 2)
    for i, ref in ((side, lon_one_ref), (BLOCKS + 1 - side, lon_two_ref)):
        two = 2 * rows
        assemble(i, ref[0:rows], ref[rows:two], ref[two:two + 8], ref[two + 8:two + 16],
                 ref[two + 16:two + 24])

    @pl.loop(0, BLOCKS, unroll=4)
    def _(i):
        up = jnp.where(lat_even, own_one_ref[i], own_two_ref[i])
        assemble(i + 1, rhs_ref[i], diag_ref[i], up, one_ref[i], two_ref[i])

    def applied(k, i):
        body = slice(8, 8 + tall)
        v = v_refs[k][i, body]
        left = v_refs[k][jnp.maximum(i - 1, 0), body]
        right = v_refs[k][jnp.minimum(i + 1, BLOCKS + 1), body]
        west = pltpu.roll(jnp.where(lane == BW - 1, left, v), 1, 1)
        east = pltpu.roll(jnp.where(lane == 0, right, v), BW - 1, 1)
        south = v_refs[k][i, 7:7 + tall]
        north = v_refs[k][i, 9:9 + tall]
        image = scale_ref[i] * v - (2.0 / HALF) * ((west + east) + (south + north))
        if k == 0:
            image = 0.5 * image
        else:
            image = image - v_refs[k - 1][i, body]
        ends = (jnp.where(lat > 0, image[:8], 0.0), image[8:rows + 8],
                jnp.where(lat < lat_count - 1, image[rows + 8:], 0.0))
        return jnp.concatenate(ends, axis=0)

    for k in range(3):
        @pl.loop(0, BLOCKS + 2, unroll=17)
        def _(i, k=k):
            v_refs[k + 1][i, 8:8 + tall] = applied(k, i)

    def products(i, carry):
        last = applied(3, i + 1)[8:8 + rows]
        q = [v_refs[k][i + 1, 16:16 + rows] for k in range(4)] + [last]
        for k in range(5):
            q_ref[k, i] = q[k]
        out = []
        for total, (a, b) in zip(carry, PAIRS):
            term = q[a] * q[b]
            out.append(total + sum(term[8 * n:8 * n + 8] for n in range(rows // 8)))
        return tuple(out)

    zero = tuple(jnp.zeros((8, BW), F32) for _ in PAIRS)
    totals = lax.fori_loop(0, BLOCKS, products, zero, unroll=4)
    lane1 = lax.broadcasted_iota(jnp.int32, (1, BW), 1)
    gram = jnp.zeros((1, BW), F32)
    for n, total in enumerate(totals):
        value = jnp.sum(jnp.sum(total, axis=0, keepdims=True), axis=1, keepdims=True)
        gram = jnp.where(lane1 == n, value, gram)
    gram_ref[...] = gram


def basis(place, rhs, diag, *strips):
    rows = rhs.shape[1]
    vmem = pl.BlockSpec(memory_space=pltpu.VMEM)
    return pl.pallas_call(
        basis_kernel,
        out_shape=[
            jax.ShapeDtypeStruct((5, BLOCKS, rows, BW), F32),
            jax.ShapeDtypeStruct((1, BW), F32),
        ],
        in_specs=[pl.BlockSpec(memory_space=pltpu.SMEM)] + [vmem] * 8,
        out_specs=[vmem, vmem],
        scratch_shapes=[
            pltpu.VMEM((BLOCKS + 2, rows + 16, BW), F32),
        ] + [pltpu.VMEM((BLOCKS + 2, rows + 32, BW), F32)] * 4,
        compiler_params=pltpu.CompilerParams(vmem_limit_bytes=VMEM_BYTES),
        name="basis",
    )(place, rhs, diag, *strips)


def solved(gram):
    g = {}
    for n, (a, b) in enumerate(PAIRS):
        g[a, b] = g[b, a] = gram[n]
    m = [[None] * 4 for _ in range(4)]
    for j in range(4):
        for i in range(j + 1):
            if j == 0:
                value = MID * g[i, 0] + HALF * g[i, 1]
            else:
                value = MID * g[i, j] + (0.5 * HALF) * (g[i, j + 1] + g[i, j - 1])
            m[i][j] = m[j][i] = value
    y = [g[0, i] for i in range(4)]
    inverse = []
    factor = [[None] * 4 for _ in range(4)]
    for k in range(4):
        pivot = m[k][k]
        inverse.append(jnp.where(pivot > 0.0, 1.0 / jnp.where(pivot > 0.0, pivot, 1.0), 0.0))
        for i in range(k + 1, 4):
            factor[i][k] = m[k][i] * inverse[k]
        for i in range(k + 1, 4):
            for j in range(i, 4):
                m[i][j] = m[i][j] - factor[i][k] * m[k][j]
            y[i] = y[i] - factor[i][k] * y[k]
    c = [y[k] * inverse[k] for k in range(4)]
    for k in range(3, -1, -1):
        for i in range(k):
            c[i] = c[i] - factor[k][i] * c[k]
    half = 0.5 * HALF
    r = [
        1.0 - (MID * c[0] + half * c[1]),
        -(HALF * c[0] + MID * c[1] + half * c[2]),
        -(half * c[1] + MID * c[2] + half * c[3]),
        -(half * c[2] + MID * c[3]),
        -(half * c[3]),
    ]
    return c, r


def combine_kernel(gram_ref, q_ref, x_ref, r_ref, c_ref):
    @pl.when(pl.program_id(0) == 0)
    def _():
        gram = jnp.sum(gram_ref[...], axis=0, keepdims=True)
        lane = lax.broadcasted_iota(jnp.int32, (1, BW), 1)
        pick = lambda n: jnp.sum(jnp.where(lane == n, gram, 0.0), axis=1, keepdims=True)
        c, r = solved([pick(n) for n in range(len(PAIRS))])
        for n, value in enumerate(c + r):
            c_ref[n] = jnp.broadcast_to(value, (8, BW))

    rows = q_ref.shape[2]
    factors = [jnp.concatenate([c_ref[n]] * (rows // 8), axis=0) for n in range(9)]
    for i in range(q_ref.shape[1]):
        q = [q_ref[k, i] for k in range(5)]
        columns = slice(i * BW, (i + 1) * BW)
        x_ref[:, columns] = sum(factors[k] * q[k] for k in range(4))
        r_ref[:, columns] = sum(factors[4 + k] * q[k] for k in range(5))


def combine(gram, q, batch=8):
    _, blocks, rows, _ = q.shape
    out = jax.ShapeDtypeStruct((rows, blocks * BW), F32)
    spec = pl.BlockSpec((rows, batch * BW), lambda i: (0, i))
    return pl.pallas_call(
        combine_kernel,
        grid=(blocks // batch,),
        out_shape=[out, out],
        in_specs=[
            pl.BlockSpec(gram.shape, lambda i: (0, 0)),
            pl.BlockSpec((5, batch, rows, BW), lambda i: (0, i, 0, 0)),
        ],
        out_specs=[spec, spec],
        scratch_shapes=[pltpu.VMEM((9, 8, BW), F32)],
        compiler_params=pltpu.CompilerParams(vmem_limit_bytes=VMEM_BYTES),
        name="combine",
    )(gram, q)


def body(piece_height, piece_weight, piece_column, piece_width):
    lon_count, lat_count = lax.axis_size("lon"), lax.axis_size("lat")
    rows = piece_height.shape[1]
    lon, lat = lax.axis_index("lon"), lax.axis_index("lat")
    place = jnp.stack([lat, jnp.int32(lat_count), lon]).astype(jnp.int32)

    next_first = passed_along(piece_height[:, :1, :], "lat", -1)
    packed = pack(piece_column, piece_width, piece_height, piece_weight, lon_count)
    labelled = label(piece_column, next_first, packed)
    got = lax.all_to_all(labelled, "lon", split_axis=0, concat_axis=0, tiled=True)
    rhs, diag, own_one, own_two, edge = sums(place, got, rows)

    one = swapped(own_one, "lat", 0, False)
    two = swapped(own_two, "lat", 1, False)
    first_edge = (BLOCKS - 1) * (1 - lon % 2)
    strips = []
    for start, block in ((0, first_edge), (1, BLOCKS - 1 - first_edge)):
        pick = lambda strip: lax.dynamic_index_in_dim(strip, block, 0, keepdims=False)
        message = jnp.concatenate([edge[start], pick(one), pick(two)], axis=0)
        strips.append(swapped(message, "lon", start, True))
    q, gram = basis(place, rhs, diag, own_one, own_two, one, two, *strips)
    spread = jnp.broadcast_to(gram[None], (lon_count * lat_count, 1, BW))
    grams = lax.all_to_all(spread, ("lon", "lat"), split_axis=0, concat_axis=0, tiled=True)
    return tuple(combine(grams.reshape(lon_count * lat_count, BW), q))


def solution(mesh):
    return jax.shard_map(
        body,
        mesh=mesh,
        in_specs=(P("lon", "lat", None), P("lon", "lat", None), P("lon"), P("lon")),
        out_specs=(P("lat", "lon"), P("lat", "lon")),
        check_vma=False,
    )
```

```python
import jax
import jax.numpy as jnp
from jax import lax
from jax.experimental import pallas as pl
from jax.experimental.pallas import tpu as pltpu
from jax.sharding import PartitionSpec as P

ROWS = 128
COLS_DEV = 4096
BW = 128
BLOCKS = COLS_DEV // BW
CAPACITY = 2

MU_DATA = 0.5
DAMPING = 0.5
RIDGE = 0.05

MID = 4.0
VMEM_BYTES = 40 * 1024 * 1024
PACK_VMEM_BYTES = 60 * 1024 * 1024
SOME_VMEM_BYTES = 50 * 1024 * 1024
F32 = jnp.float32


def passed_along(block, axis, distance):
    devices = range(lax.axis_size(axis))
    route = [(i, i + distance) for i in devices if i + distance in devices]
    return lax.ppermute(block, axis, route)


def swapped(block, axis, start, around):
    count = lax.axis_size(axis)
    lows = range(start, count if around else count - 1, 2)
    pairs = [(low, (low + 1) % count) for low in lows]
    return lax.ppermute(block, axis, pairs + [(b, a) for a, b in pairs])


def pack_kernel(column_ref, width_ref, height_ref, weight_ref, out_ref, held_ref, facts_ref,
                count_ref, in_sem, out_sem, facts_sem):
    tiles, pieces = out_ref.shape[0], height_ref.shape[0]
    rows = height_ref.shape[1]
    part = 2 * rows
    batch = pieces // in_sem.shape[0]
    lane = lax.broadcasted_iota(jnp.int32, (1, BW), 1)

    def loads(g):
        part = pl.ds(g * batch, batch)
        sources = (height_ref, weight_ref)
        return [pltpu.make_async_copy(source.at[part], held_ref.at[part, pl.ds(n * rows, rows)],
                                      in_sem.at[g, n]) for n, source in enumerate(sources)]

    for g in range(in_sem.shape[0]):
        for load in loads(g):
            load.start()

    facts_ref[...] = jnp.zeros_like(facts_ref)

    @pl.loop(0, tiles, unroll=8)
    def _(t):
        count_ref[t] = 0

    for g in range(in_sem.shape[0]):
        for load in loads(g):
            load.wait()

        @pl.loop(g * batch, (g + 1) * batch, unroll=4)
        def _(p):
            tile = column_ref[p] // COLS_DEV
            block = column_ref[p] % COLS_DEV // BW
            slot = count_ref[tile]
            count_ref[tile] = slot + 1
            at = 2 * slot
            facts = jnp.where(lane == at, block + 1, jnp.where(lane == at + 1, width_ref[p], 0))
            facts_ref[tile] += facts.astype(F32)
            pltpu.make_async_copy(held_ref.at[p], out_ref.at[tile, pl.ds(slot * part, part)],
                                  out_sem).start()

    facts = pltpu.make_async_copy(facts_ref, out_ref.at[:, CAPACITY * (part + 1)], facts_sem)
    facts.start()
    pltpu.make_async_copy(held_ref, out_ref.at[pl.ds(0, pieces), pl.ds(0, part)], out_sem).wait()
    facts.wait()


def pack(piece_column, piece_width, piece_height, piece_weight, tiles, batches=8):
    pieces, rows, _ = piece_height.shape
    tall = lambda array: array.reshape(pieces, rows, 1, BW)
    return pl.pallas_call(
        pack_kernel,
        out_shape=jax.ShapeDtypeStruct((tiles, CAPACITY * (2 * rows + 1) + 1, 1, BW), F32),
        in_specs=[
            pl.BlockSpec(memory_space=pltpu.SMEM),
            pl.BlockSpec(memory_space=pltpu.SMEM),
            pl.BlockSpec(memory_space=pl.ANY),
            pl.BlockSpec(memory_space=pl.ANY),
        ],
        out_specs=pl.BlockSpec(memory_space=pl.ANY),
        scratch_shapes=[
            pltpu.VMEM((pieces, 2 * rows, 1, BW), F32),
            pltpu.VMEM((tiles, 1, BW), F32),
            pltpu.SMEM((tiles,), jnp.int32),
            pltpu.SemaphoreType.DMA((batches, 2)),
            pltpu.SemaphoreType.DMA,
            pltpu.SemaphoreType.DMA,
        ],
        compiler_params=pltpu.CompilerParams(vmem_limit_bytes=PACK_VMEM_BYTES),
        name="pack",
    )(piece_column, piece_width, tall(piece_height), tall(piece_weight))


def label_kernel(column_ref, first_ref, packed_ref, out_ref, count_ref, sem):
    tiles, pieces = out_ref.shape[0], first_ref.shape[0]
    first = out_ref.shape[1] - CAPACITY - 1

    @pl.loop(0, tiles, unroll=8)
    def _(t):
        count_ref[t] = 0

    @pl.loop(0, pieces, unroll=8)
    def _(p):
        tile = column_ref[p] // COLS_DEV
        slot = count_ref[tile]
        count_ref[tile] = slot + 1
        pltpu.make_async_copy(first_ref.at[p], out_ref.at[tile, first + slot], sem).start()

    pltpu.make_async_copy(first_ref, out_ref.at[pl.ds(0, pieces), first], sem).wait()


def label(piece_column, next_first, packed):
    return pl.pallas_call(
        label_kernel,
        out_shape=jax.ShapeDtypeStruct(packed.shape, F32),
        in_specs=[
            pl.BlockSpec(memory_space=pltpu.SMEM),
            pl.BlockSpec(memory_space=pltpu.VMEM),
            pl.BlockSpec(memory_space=pl.ANY),
        ],
        out_specs=pl.BlockSpec(memory_space=pl.ANY),
        scratch_shapes=[
            pltpu.SMEM(packed.shape[:1], jnp.int32),
            pltpu.SemaphoreType.DMA,
        ],
        input_output_aliases={2: 0},
        compiler_params=pltpu.CompilerParams(vmem_limit_bytes=SOME_VMEM_BYTES),
        name="label",
    )(piece_column, next_first, packed)


def sums_kernel(place_ref, got_ref, rows_ref, rhs_ref, diag_ref, one_ref, two_ref, edge_ref,
                held_ref, facts_ref, total_ref, facts_sem, sem):
    rows = rhs_ref.shape[1]
    part = 2 * rows
    message = CAPACITY * (part + 1) + 1
    chunks, height, _ = held_ref.shape
    sources = height // message
    lat, lat_count, lon = place_ref[0], place_ref[1], place_ref[2]
    lane = lax.broadcasted_iota(jnp.int32, (rows, BW), 1)
    row = lax.broadcasted_iota(jnp.int32, (rows, BW), 0)

    def load(n):
        rows_of = rows_ref.at[pl.ds(n * height, height)]
        return pltpu.make_async_copy(rows_of, held_ref.at[n], sem.at[n])

    facts = pltpu.make_async_copy(got_ref.at[:, message - 1], facts_ref, facts_sem)
    facts.start()
    for n in range(chunks):
        load(n).start()
    total_ref[...] = jnp.zeros_like(total_ref)
    facts.wait()

    @pl.loop(0, chunks)
    def _(n):
        load(n).wait()
        for s in range(sources * CAPACITY):
            source, slot = s // CAPACITY, s % CAPACITY
            block = facts_ref[n * sources + source, 0, 2 * slot].astype(jnp.int32) - 1
            block = jnp.where(block < 0, BLOCKS, block)
            width = facts_ref[n * sources + source, 0, 2 * slot + 1].astype(jnp.int32)
            base = source * message
            start, first = base + slot * part, base + CAPACITY * part + slot
            height = held_ref[n, start:start + rows]
            weight = held_ref[n, start + rows:start + part]
            above = held_ref[n, first:first + 1]
            cell = jnp.where(lane < width, weight, 0.0)
            east = jnp.where(lane < width - 1, weight, 0.0)
            east_step = pltpu.roll(height, BW - 1, 1) - height
            raised = jnp.where(row == rows - 1, above, pltpu.roll(height, rows - 1, 0))
            terms = (cell, cell * height, east, east * east_step, cell * (raised - height))
            for k, term in enumerate(terms):
                total_ref[block, k] += term

    last = (row == rows - 1) & (lat == lat_count - 1)
    first = (row == 0) & (lat == 0)
    sides = 4.0 - last.astype(F32) - first.astype(F32) + RIDGE
    row8 = row[:8]
    lat_even = lat % 2 == 0

    @pl.loop(0, BLOCKS, unroll=4)
    def _(i):
        cell, height = total_ref[i, 0], total_ref[i, 1]
        east = total_ref[i, 3] / (total_ref[i, 2] + DAMPING)
        north = jnp.where(last, 0.0, total_ref[i, 4] / (cell + DAMPING))
        south = jnp.where(row == 0, 0.0, pltpu.roll(north, 1, 0))
        rhs = MU_DATA * height - (east - pltpu.roll(east, 1, 1)) - (north - south)
        diag = MU_DATA * cell + sides
        rhs_ref[i] = rhs
        diag_ref[i] = diag
        top = pltpu.roll(diag[rows - 8:], 4, 0)
        top = jnp.where(row8 == 0, pltpu.roll(north[rows - 8:], 1, 0), top)
        up = jnp.where(row8 >= 4, rhs[rows - 8:], top)
        down = jnp.where(row8 >= 4, pltpu.roll(diag[:8], 4, 0), rhs[:8])
        one_ref[i] = jnp.where(lat_even, up, down)
        two_ref[i] = jnp.where(lat_even, down, up)

    first_edge = (BLOCKS - 1) * (1 - lon % 2)
    for side, block in ((0, first_edge), (1, BLOCKS - 1 - first_edge)):
        edge_ref[side, 0:rows] = rhs_ref[block]
        edge_ref[side, rows:2 * rows] = diag_ref[block]
        up = jnp.where(lat_even, one_ref[block], two_ref[block])
        edge_ref[side, 2 * rows:2 * rows + 8] = up


def sums(place, got, rows, chunks=2):
    tiles, message, _, _ = got.shape
    height = tiles * message // chunks
    field = (BLOCKS, rows, BW)
    strip = (BLOCKS, 8, BW)
    edge = (2, 2 * rows + 8, BW)
    vmem = pl.BlockSpec(memory_space=pltpu.VMEM)
    return pl.pallas_call(
        sums_kernel,
        out_shape=[jax.ShapeDtypeStruct(s, F32) for s in (field, field, strip, strip, edge)],
        in_specs=[
            pl.BlockSpec(memory_space=pltpu.SMEM),
            pl.BlockSpec(memory_space=pl.ANY),
            pl.BlockSpec(memory_space=pl.ANY),
        ],
        out_specs=[vmem] * 5,
        scratch_shapes=[
            pltpu.VMEM((chunks, height, BW), F32),
            pltpu.SMEM((tiles, 1, BW), F32),
            pltpu.VMEM((BLOCKS + 1, 5, rows, BW), F32),
            pltpu.SemaphoreType.DMA,
            pltpu.SemaphoreType.DMA((chunks,)),
        ],
        compiler_params=pltpu.CompilerParams(vmem_limit_bytes=VMEM_BYTES),
        name="sums",
    )(place, got, got.reshape(chunks * height, BW))


def two_sum(a, b):
    total = a + b
    part = total - a
    return total, (a - (total - part)) + (b - part)


def pair_sum(high, low, other_high, other_low):
    total, error = two_sum(high, other_high)
    return total, low + other_low + error


def two_product(a, b):
    def split(x):
        big = 4097.0 * x
        top = big - (big - x)
        return top, x - top

    product = a * b
    (a_top, a_end), (b_top, b_end) = split(a), split(b)
    return product, ((a_top * b_top - product) + a_top * b_end + a_end * b_top) + a_end * b_end


def all_rows(high, low):
    for shift in (4, 2, 1):
        high, low = pair_sum(high, low, pltpu.roll(high, shift, 0), pltpu.roll(low, shift, 0))
    return high, low


PAIRS = [(i, j) for j in range(5) for i in range(min(j, 3) + 1)]
LOW = 16


def basis_kernel(place_ref, rhs_ref, diag_ref, own_one_ref, own_two_ref, one_ref, two_ref,
                 lon_one_ref, lon_two_ref, q_ref, gram_ref, scale_ref, *v_refs):
    rows = rhs_ref.shape[1]
    tall = rows + 16
    lat, lat_count, lon = place_ref[0], place_ref[1], place_ref[2]
    lat_even = lat % 2 == 0
    row = lax.broadcasted_iota(jnp.int32, (rows, BW), 0)
    row8 = row[:8]
    lane = lax.broadcasted_iota(jnp.int32, (tall, BW), 1)

    def assemble(i, rhs, diag, up, one, two):
        south = jnp.where(lat_even, two, one)
        north = jnp.where(lat_even, one, two)
        first = jnp.where(row == 0, south[0:1], 0.0) + rhs
        below = jnp.where(row8 >= 4, south, 0.0)
        above = jnp.where(row8 == 0, north + up, jnp.where(row8 < 4, north, 0.0))
        v_refs[0][i, 8:8 + tall] = jnp.concatenate([below, first, above], axis=0)
        diag = jnp.concatenate([pltpu.roll(south, 4, 0), diag, pltpu.roll(north, 4, 0)], axis=0)
        scale_ref[i] = (diag - MID) * 0.125

    side = (BLOCKS + 1) * (1 - lon % 2)
    for i, ref in ((side, lon_one_ref), (BLOCKS + 1 - side, lon_two_ref)):
        two = 2 * rows
        assemble(i, ref[0:rows], ref[rows:two], ref[two:two + 8], ref[two + 8:two + 16],
                 ref[two + 16:two + 24])

    @pl.loop(0, BLOCKS, unroll=4)
    def _(i):
        up = jnp.where(lat_even, own_one_ref[i], own_two_ref[i])
        assemble(i + 1, rhs_ref[i], diag_ref[i], up, one_ref[i], two_ref[i])

    def applied(k, i):
        body = slice(8, 8 + tall)
        v = v_refs[k][i, body]
        left = v_refs[k][jnp.maximum(i - 1, 0), body]
        right = v_refs[k][jnp.minimum(i + 1, BLOCKS + 1), body]
        west = pltpu.roll(jnp.where(lane == BW - 1, left, v), 1, 1)
        east = pltpu.roll(jnp.where(lane == 0, right, v), BW - 1, 1)
        south = v_refs[k][i, 7:7 + tall]
        north = v_refs[k][i, 9:9 + tall]
        image = scale_ref[i] * v - 0.125 * ((west + east) + (south + north))
        if k == 0:
            image = 0.5 * image
        else:
            image = image - 0.0625 * v_refs[k - 1][i, body]
        ends = (jnp.where(lat > 0, image[:8], 0.0), image[8:rows + 8],
                jnp.where(lat < lat_count - 1, image[rows + 8:], 0.0))
        return jnp.concatenate(ends, axis=0)

    for k in range(3):
        @pl.loop(0, BLOCKS + 2, unroll=34)
        def _(i, k=k):
            v_refs[k + 1][i, 8:8 + tall] = applied(k, i)

    def products(i, carry):
        last = applied(3, i + 1)[8:8 + rows]
        q = [v_refs[k][i + 1, 16:16 + rows] for k in range(4)] + [last]
        for k in range(5):
            q_ref[k, i] = q[k]
        out = []
        for total, (a, b) in zip(carry, PAIRS):
            term = q[a] * q[b]
            out.append(total + sum(term[8 * n:8 * n + 8] for n in range(rows // 8)))
        return tuple(out)

    zero = tuple(jnp.zeros((8, BW), F32) for _ in PAIRS)
    totals = lax.fori_loop(0, BLOCKS, products, zero, unroll=8)
    row_of = lax.broadcasted_iota(jnp.int32, (8, BW), 0)
    lane_of = lax.broadcasted_iota(jnp.int32, (8, BW), 1)
    gram = jnp.zeros((8, BW), F32)
    for start in range(0, len(PAIRS), 8):
        high = jnp.zeros((8, BW), F32)
        low = jnp.zeros((8, BW), F32)
        for n, total in enumerate(totals[start:start + 8]):
            pair = all_rows(total, jnp.zeros_like(total))
            high = jnp.where(row_of == n, pair[0], high)
            low = jnp.where(row_of == n, pair[1], low)
        shift = BW // 2
        while shift:
            high, low = pair_sum(high, low, pltpu.roll(high, shift, 1), pltpu.roll(low, shift, 1))
            shift //= 2
        gram = jnp.where(lane_of == row_of + start, high, gram)
        gram = jnp.where(lane_of == row_of + start + LOW, low, gram)
    gram_ref[...] = jnp.sum(gram, axis=0, keepdims=True)


def basis(place, rhs, diag, *strips):
    rows = rhs.shape[1]
    vmem = pl.BlockSpec(memory_space=pltpu.VMEM)
    return pl.pallas_call(
        basis_kernel,
        out_shape=[
            jax.ShapeDtypeStruct((5, BLOCKS, rows, BW), F32),
            jax.ShapeDtypeStruct((1, BW), F32),
        ],
        in_specs=[pl.BlockSpec(memory_space=pltpu.SMEM)] + [vmem] * 8,
        out_specs=[vmem, vmem],
        scratch_shapes=[
            pltpu.VMEM((BLOCKS + 2, rows + 16, BW), F32),
        ] + [pltpu.VMEM((BLOCKS + 2, rows + 32, BW), F32)] * 4,
        compiler_params=pltpu.CompilerParams(vmem_limit_bytes=VMEM_BYTES),
        name="basis",
    )(place, rhs, diag, *strips)


def solved(high, low):
    g = {}
    for n, (a, b) in enumerate(PAIRS):
        g[a, b] = g[b, a] = (high[n], low[n])

    def times(factor, pair):
        return factor * pair[0], factor * pair[1]

    m = [[None] * 4 for _ in range(4)]
    for j in range(4):
        for i in range(j + 1):
            value = pair_sum(*times(MID, g[i, j]), *times(8.0 if j else 16.0, g[i, j + 1]))
            if j:
                value = pair_sum(*value, *times(0.5, g[i, j - 1]))
            m[i][j] = m[j][i] = two_sum(*value)

    work = [[m[i][j][0] for j in range(4)] for i in range(4)]
    inverse = []
    factor = [[None] * 4 for _ in range(4)]
    for k in range(4):
        pivot = work[k][k]
        inverse.append(jnp.where(pivot > 0.0, 1.0 / jnp.where(pivot > 0.0, pivot, 1.0), 0.0))
        for i in range(k + 1, 4):
            factor[i][k] = work[k][i] * inverse[k]
        for i in range(k + 1, 4):
            for j in range(i, 4):
                work[i][j] = work[i][j] - factor[i][k] * work[k][j]

    def solve(y):
        y = list(y)
        for k in range(4):
            for i in range(k + 1, 4):
                y[i] = y[i] - factor[i][k] * y[k]
        y = [y[k] * inverse[k] for k in range(4)]
        for k in range(3, -1, -1):
            for i in range(k):
                y[i] = y[i] - factor[k][i] * y[k]
        return y

    rest = [g[0, i] for i in range(4)]
    c = solve([pair[0] for pair in rest])
    found = [c]
    for _ in range(2):
        for i in range(4):
            for j in range(4):
                product, error = two_product(m[i][j][0], c[j])
                total, lost = two_sum(rest[i][0], -product)
                rest[i] = total, rest[i][1] + (lost - error - m[i][j][1] * c[j])
        rest = [two_sum(*pair) for pair in rest]
        c = solve([pair[0] for pair in rest])
        found.append(c)
    c = [found[0][k] + (found[1][k] + found[2][k]) for k in range(4)]
    r = [
        1.0 - (MID * c[0] + 0.5 * c[1]),
        -(16.0 * c[0] + MID * c[1] + 0.5 * c[2]),
        -(8.0 * c[1] + MID * c[2] + 0.5 * c[3]),
        -(8.0 * c[2] + MID * c[3]),
        -(8.0 * c[3]),
    ]
    return c, r


def combine_kernel(gram_ref, q_ref, x_ref, r_ref):
    rows = q_ref.shape[2]
    terms = [(gram_ref[n:n + 8], jnp.zeros((8, BW), F32)) for n in range(0, gram_ref.shape[0], 8)]
    while len(terms) > 1:
        terms = [pair_sum(*terms[n], *terms[n + 1]) for n in range(0, len(terms), 2)]
    high, low = all_rows(*terms[0])
    high, low = two_sum(high, low + pltpu.roll(high, BW - LOW, 1))
    first = high[0:1, 0:1]
    scale = jnp.where(first > 1e25, 2.0 ** -60, jnp.where(first < 1e-15, 2.0 ** 60, 1.0))
    lane = lax.broadcasted_iota(jnp.int32, (1, BW), 1)

    def pick(values, n):
        row = jnp.where(lane == n, values[0:1], 0.0)
        return scale * jnp.sum(row, axis=1, keepdims=True)

    count = range(len(PAIRS))
    c, r = solved([pick(high, n) for n in count], [pick(low, n) for n in count])
    c = [jnp.broadcast_to(value, (rows, BW)) for value in c]
    r = [jnp.broadcast_to(value, (rows, BW)) for value in r]
    for i in range(q_ref.shape[1]):
        q = [q_ref[k, i] for k in range(5)]
        columns = slice(i * BW, (i + 1) * BW)
        x_ref[:, columns] = sum(c[k] * q[k] for k in range(4))
        r_ref[:, columns] = sum(r[k] * q[k] for k in range(5))


def combine(gram, q):
    _, blocks, rows, _ = q.shape
    out = jax.ShapeDtypeStruct((rows, blocks * BW), F32)
    vmem = pl.BlockSpec(memory_space=pltpu.VMEM)
    return pl.pallas_call(
        combine_kernel,
        out_shape=[out, out],
        in_specs=[vmem, vmem],
        out_specs=[vmem, vmem],
        compiler_params=pltpu.CompilerParams(vmem_limit_bytes=VMEM_BYTES),
        name="combine",
    )(gram, q)


def body(piece_height, piece_weight, piece_column, piece_width):
    lon_count, lat_count = lax.axis_size("lon"), lax.axis_size("lat")
    rows = piece_height.shape[1]
    lon, lat = lax.axis_index("lon"), lax.axis_index("lat")
    place = jnp.stack([lat, jnp.int32(lat_count), lon]).astype(jnp.int32)

    next_first = passed_along(piece_height[:, :1, :], "lat", -1)
    packed = pack(piece_column, piece_width, piece_height, piece_weight, lon_count)
    labelled = label(piece_column, next_first, packed)
    got = lax.all_to_all(labelled, "lon", split_axis=0, concat_axis=0, tiled=True)
    rhs, diag, own_one, own_two, edge = sums(place, got, rows)

    one = swapped(own_one, "lat", 0, False)
    two = swapped(own_two, "lat", 1, False)
    first_edge = (BLOCKS - 1) * (1 - lon % 2)
    strips = []
    for start, block in ((0, first_edge), (1, BLOCKS - 1 - first_edge)):
        pick = lambda strip: lax.dynamic_index_in_dim(strip, block, 0, keepdims=False)
        message = jnp.concatenate([edge[start], pick(one), pick(two)], axis=0)
        strips.append(swapped(message, "lon", start, True))
    q, gram = basis(place, rhs, diag, own_one, own_two, one, two, *strips)
    spread = jnp.broadcast_to(gram[None], (lon_count * lat_count, 1, BW))
    grams = lax.all_to_all(spread, ("lon", "lat"), split_axis=0, concat_axis=0, tiled=True)
    return tuple(combine(grams.reshape(lon_count * lat_count, BW), q))


def solution(mesh):
    return jax.shard_map(
        body,
        mesh=mesh,
        in_specs=(P("lon", "lat", None), P("lon", "lat", None), P("lon"), P("lon")),
        out_specs=(P("lat", "lon"), P("lat", "lon")),
        check_vma=False,
    )
```

```python
import jax
import jax.numpy as jnp
from jax import lax
from jax.experimental import pallas as pl
from jax.experimental.pallas import tpu as pltpu
from jax.sharding import PartitionSpec as P

ROWS = 128
COLS_DEV = 4096
BW = 128
BLOCKS = COLS_DEV // BW
CAPACITY = 2

MU_DATA = 0.5
DAMPING = 0.5
RIDGE = 0.05

MID = 4.0
VMEM_BYTES = 40 * 1024 * 1024
PACK_VMEM_BYTES = 60 * 1024 * 1024
F32 = jnp.float32


def passed_along(block, axis, distance):
    devices = range(lax.axis_size(axis))
    route = [(i, i + distance) for i in devices if i + distance in devices]
    return lax.ppermute(block, axis, route)


def swapped(block, axis, start, around):
    count = lax.axis_size(axis)
    lows = range(start, count if around else count - 1, 2)
    pairs = [(low, (low + 1) % count) for low in lows]
    return lax.ppermute(block, axis, pairs + [(b, a) for a, b in pairs])


def pack_kernel(column_ref, width_ref, height_ref, weight_ref, out_ref, held_ref, facts_ref,
                count_ref, in_sem, out_sem, facts_sem):
    tiles, pieces = out_ref.shape[0], height_ref.shape[0]
    rows = height_ref.shape[1]
    part = 2 * rows
    batch = pieces // in_sem.shape[0]
    lane = lax.broadcasted_iota(jnp.int32, (1, BW), 1)

    def loads(g):
        part = pl.ds(g * batch, batch)
        sources = (height_ref, weight_ref)
        return [pltpu.make_async_copy(source.at[part], held_ref.at[part, pl.ds(n * rows, rows)],
                                      in_sem.at[g, n]) for n, source in enumerate(sources)]

    for g in range(in_sem.shape[0]):
        for load in loads(g):
            load.start()

    facts_ref[...] = jnp.zeros_like(facts_ref)

    @pl.loop(0, tiles, unroll=8)
    def _(t):
        count_ref[t] = 0

    for g in range(in_sem.shape[0]):
        for load in loads(g):
            load.wait()

        @pl.loop(g * batch, (g + 1) * batch, unroll=4)
        def _(p):
            tile = column_ref[p] // COLS_DEV
            block = column_ref[p] % COLS_DEV // BW
            slot = count_ref[tile]
            count_ref[tile] = slot + 1
            at = 2 * slot
            facts = jnp.where(lane == at, block + 1, jnp.where(lane == at + 1, width_ref[p], 0))
            facts_ref[tile] += facts.astype(F32)
            pltpu.make_async_copy(held_ref.at[p], out_ref.at[tile, pl.ds(slot * part, part)],
                                  out_sem).start()

    facts = pltpu.make_async_copy(facts_ref, out_ref.at[:, CAPACITY * part], facts_sem)
    facts.start()
    pltpu.make_async_copy(held_ref, out_ref.at[pl.ds(0, pieces), pl.ds(0, part)], out_sem).wait()
    facts.wait()


def pack(piece_column, piece_width, piece_height, piece_weight, tiles, batches=8):
    pieces, rows, _ = piece_height.shape
    tall = lambda array: array.reshape(pieces, rows, 1, BW)
    return pl.pallas_call(
        pack_kernel,
        out_shape=jax.ShapeDtypeStruct((tiles, CAPACITY * 2 * rows + 1, 1, BW), F32),
        in_specs=[
            pl.BlockSpec(memory_space=pltpu.SMEM),
            pl.BlockSpec(memory_space=pltpu.SMEM),
            pl.BlockSpec(memory_space=pl.ANY),
            pl.BlockSpec(memory_space=pl.ANY),
        ],
        out_specs=pl.BlockSpec(memory_space=pl.ANY),
        scratch_shapes=[
            pltpu.VMEM((pieces, 2 * rows, 1, BW), F32),
            pltpu.VMEM((tiles, 1, BW), F32),
            pltpu.SMEM((tiles,), jnp.int32),
            pltpu.SemaphoreType.DMA((batches, 2)),
            pltpu.SemaphoreType.DMA,
            pltpu.SemaphoreType.DMA,
        ],
        compiler_params=pltpu.CompilerParams(vmem_limit_bytes=PACK_VMEM_BYTES),
        name="pack",
    )(piece_column, piece_width, tall(piece_height), tall(piece_weight))


def sums_kernel(place_ref, got_ref, rows_ref, above_ref, rhs_ref, diag_ref, one_ref, two_ref, edge_ref,
                held_ref, facts_ref, total_ref, facts_sem, sem):
    rows = rhs_ref.shape[1]
    part = 2 * rows
    message = CAPACITY * part + 1
    chunks, height, _ = held_ref.shape
    sources = height // message
    lat, lat_count, lon = place_ref[0], place_ref[1], place_ref[2]
    lane = lax.broadcasted_iota(jnp.int32, (rows, BW), 1)
    row = lax.broadcasted_iota(jnp.int32, (rows, BW), 0)

    def load(n):
        rows_of = rows_ref.at[pl.ds(n * height, height)]
        return pltpu.make_async_copy(rows_of, held_ref.at[n], sem.at[n])

    facts = pltpu.make_async_copy(got_ref.at[:, message - 1], facts_ref, facts_sem)
    facts.start()
    for n in range(chunks):
        load(n).start()
    total_ref[...] = jnp.zeros_like(total_ref)
    facts.wait()

    @pl.loop(0, chunks)
    def _(n):
        load(n).wait()
        for s in range(sources * CAPACITY):
            source, slot = s // CAPACITY, s % CAPACITY
            block = facts_ref[n * sources + source, 0, 2 * slot].astype(jnp.int32) - 1
            block = jnp.where(block < 0, BLOCKS, block)
            width = facts_ref[n * sources + source, 0, 2 * slot + 1].astype(jnp.int32)
            base = source * message
            start = base + slot * part
            height = held_ref[n, start:start + rows]
            weight = held_ref[n, start + rows:start + part]
            above = above_ref[n * sources + source, slot]
            cell = jnp.where(lane < width, weight, 0.0)
            east = jnp.where(lane < width - 1, weight, 0.0)
            east_step = pltpu.roll(height, BW - 1, 1) - height
            raised = jnp.where(row == rows - 1, above, pltpu.roll(height, rows - 1, 0))
            terms = (cell, cell * height, east, east * east_step, cell * (raised - height))
            for k, term in enumerate(terms):
                total_ref[block, k] += term

    last = (row == rows - 1) & (lat == lat_count - 1)
    first = (row == 0) & (lat == 0)
    sides = 4.0 - last.astype(F32) - first.astype(F32) + RIDGE
    row8 = row[:8]
    lat_even = lat % 2 == 0

    @pl.loop(0, BLOCKS, unroll=4)
    def _(i):
        cell, height = total_ref[i, 0], total_ref[i, 1]
        east = total_ref[i, 3] / (total_ref[i, 2] + DAMPING)
        north = jnp.where(last, 0.0, total_ref[i, 4] / (cell + DAMPING))
        south = jnp.where(row == 0, 0.0, pltpu.roll(north, 1, 0))
        rhs = MU_DATA * height - (east - pltpu.roll(east, 1, 1)) - (north - south)
        diag = MU_DATA * cell + sides
        rhs_ref[i] = rhs
        diag_ref[i] = diag
        top = pltpu.roll(diag[rows - 8:], 4, 0)
        top = jnp.where(row8 == 0, pltpu.roll(north[rows - 8:], 1, 0), top)
        up = jnp.where(row8 >= 4, rhs[rows - 8:], top)
        down = jnp.where(row8 >= 4, pltpu.roll(diag[:8], 4, 0), rhs[:8])
        one_ref[i] = jnp.where(lat_even, up, down)
        two_ref[i] = jnp.where(lat_even, down, up)

    first_edge = (BLOCKS - 1) * (1 - lon % 2)
    for side, block in ((0, first_edge), (1, BLOCKS - 1 - first_edge)):
        edge_ref[side, 0:rows] = rhs_ref[block]
        edge_ref[side, rows:2 * rows] = diag_ref[block]
        up = jnp.where(lat_even, one_ref[block], two_ref[block])
        edge_ref[side, 2 * rows:2 * rows + 8] = up


def sums(place, got, above, rows, chunks=2):
    tiles, message, _, _ = got.shape
    height = tiles * message // chunks
    field = (BLOCKS, rows, BW)
    strip = (BLOCKS, 8, BW)
    edge = (2, 2 * rows + 8, BW)
    vmem = pl.BlockSpec(memory_space=pltpu.VMEM)
    return pl.pallas_call(
        sums_kernel,
        out_shape=[jax.ShapeDtypeStruct(s, F32) for s in (field, field, strip, strip, edge)],
        in_specs=[
            pl.BlockSpec(memory_space=pltpu.SMEM),
            pl.BlockSpec(memory_space=pl.ANY),
            pl.BlockSpec(memory_space=pl.ANY),
            vmem,
        ],
        out_specs=[vmem] * 5,
        scratch_shapes=[
            pltpu.VMEM((chunks, height, BW), F32),
            pltpu.SMEM((tiles, 1, BW), F32),
            pltpu.VMEM((BLOCKS + 1, 5, rows, BW), F32),
            pltpu.SemaphoreType.DMA,
            pltpu.SemaphoreType.DMA((chunks,)),
        ],
        compiler_params=pltpu.CompilerParams(vmem_limit_bytes=VMEM_BYTES),
        name="sums",
    )(place, got, got.reshape(chunks * height, BW), above)


def two_sum(a, b):
    total = a + b
    part = total - a
    return total, (a - (total - part)) + (b - part)


def pair_sum(high, low, other_high, other_low):
    total, error = two_sum(high, other_high)
    return total, low + other_low + error


def two_product(a, b):
    def split(x):
        big = 4097.0 * x
        top = big - (big - x)
        return top, x - top

    product = a * b
    (a_top, a_end), (b_top, b_end) = split(a), split(b)
    return product, ((a_top * b_top - product) + a_top * b_end + a_end * b_top) + a_end * b_end


def all_rows(high, low):
    for shift in (4, 2, 1):
        high, low = pair_sum(high, low, pltpu.roll(high, shift, 0), pltpu.roll(low, shift, 0))
    return high, low


PAIRS = [(i, j) for j in range(5) for i in range(min(j, 3) + 1)]
LOW = 16


def basis_kernel(place_ref, rhs_ref, diag_ref, own_one_ref, own_two_ref, one_ref, two_ref,
                 lon_one_ref, lon_two_ref, q_ref, gram_ref, scale_ref, *v_refs):
    rows = rhs_ref.shape[1]
    tall = rows + 16
    lat, lat_count, lon = place_ref[0], place_ref[1], place_ref[2]
    lat_even = lat % 2 == 0
    row = lax.broadcasted_iota(jnp.int32, (rows, BW), 0)
    row8 = row[:8]
    lane = lax.broadcasted_iota(jnp.int32, (tall, BW), 1)

    def assemble(i, rhs, diag, up, one, two):
        south = jnp.where(lat_even, two, one)
        north = jnp.where(lat_even, one, two)
        first = jnp.where(row == 0, south[0:1], 0.0) + rhs
        below = jnp.where(row8 >= 4, south, 0.0)
        above = jnp.where(row8 == 0, north + up, jnp.where(row8 < 4, north, 0.0))
        v_refs[0][i, 8:8 + tall] = jnp.concatenate([below, first, above], axis=0)
        diag = jnp.concatenate([pltpu.roll(south, 4, 0), diag, pltpu.roll(north, 4, 0)], axis=0)
        scale_ref[i] = (diag - MID) * 0.125

    side = (BLOCKS + 1) * (1 - lon % 2)
    for i, ref in ((side, lon_one_ref), (BLOCKS + 1 - side, lon_two_ref)):
        two = 2 * rows
        assemble(i, ref[0:rows], ref[rows:two], ref[two:two + 8], ref[two + 8:two + 16],
                 ref[two + 16:two + 24])

    @pl.loop(0, BLOCKS, unroll=4)
    def _(i):
        up = jnp.where(lat_even, own_one_ref[i], own_two_ref[i])
        assemble(i + 1, rhs_ref[i], diag_ref[i], up, one_ref[i], two_ref[i])

    def applied(k, i):
        body = slice(8, 8 + tall)
        v = v_refs[k][i, body]
        left = v_refs[k][jnp.maximum(i - 1, 0), body]
        right = v_refs[k][jnp.minimum(i + 1, BLOCKS + 1), body]
        west = pltpu.roll(jnp.where(lane == BW - 1, left, v), 1, 1)
        east = pltpu.roll(jnp.where(lane == 0, right, v), BW - 1, 1)
        south = v_refs[k][i, 7:7 + tall]
        north = v_refs[k][i, 9:9 + tall]
        image = scale_ref[i] * v - 0.125 * ((west + east) + (south + north))
        if k == 0:
            image = 0.5 * image
        else:
            image = image - 0.0625 * v_refs[k - 1][i, body]
        ends = (jnp.where(lat > 0, image[:8], 0.0), image[8:rows + 8],
                jnp.where(lat < lat_count - 1, image[rows + 8:], 0.0))
        return jnp.concatenate(ends, axis=0)

    for k in range(3):
        @pl.loop(0, BLOCKS + 2, unroll=34)
        def _(i, k=k):
            v_refs[k + 1][i, 8:8 + tall] = applied(k, i)

    def products(i, carry):
        last = applied(3, i + 1)[8:8 + rows]
        q = [v_refs[k][i + 1, 16:16 + rows] for k in range(4)] + [last]
        for k in range(5):
            q_ref[k, i] = q[k]
        out = []
        for total, (a, b) in zip(carry, PAIRS):
            term = q[a] * q[b]
            out.append(total + sum(term[8 * n:8 * n + 8] for n in range(rows // 8)))
        return tuple(out)

    zero = tuple(jnp.zeros((8, BW), F32) for _ in PAIRS)
    totals = lax.fori_loop(0, BLOCKS, products, zero, unroll=8)
    row_of = lax.broadcasted_iota(jnp.int32, (8, BW), 0)
    lane_of = lax.broadcasted_iota(jnp.int32, (8, BW), 1)
    gram = jnp.zeros((8, BW), F32)
    for start in range(0, len(PAIRS), 8):
        high = jnp.zeros((8, BW), F32)
        low = jnp.zeros((8, BW), F32)
        for n, total in enumerate(totals[start:start + 8]):
            pair = all_rows(total, jnp.zeros_like(total))
            high = jnp.where(row_of == n, pair[0], high)
            low = jnp.where(row_of == n, pair[1], low)
        shift = BW // 2
        while shift:
            high, low = pair_sum(high, low, pltpu.roll(high, shift, 1), pltpu.roll(low, shift, 1))
            shift //= 2
        gram = jnp.where(lane_of == row_of + start, high, gram)
        gram = jnp.where(lane_of == row_of + start + LOW, low, gram)
    gram_ref[...] = jnp.sum(gram, axis=0, keepdims=True)


def basis(place, rhs, diag, *strips):
    rows = rhs.shape[1]
    vmem = pl.BlockSpec(memory_space=pltpu.VMEM)
    return pl.pallas_call(
        basis_kernel,
        out_shape=[
            jax.ShapeDtypeStruct((5, BLOCKS, rows, BW), F32),
            jax.ShapeDtypeStruct((1, BW), F32),
        ],
        in_specs=[pl.BlockSpec(memory_space=pltpu.SMEM)] + [vmem] * 8,
        out_specs=[vmem, vmem],
        scratch_shapes=[
            pltpu.VMEM((BLOCKS + 2, rows + 16, BW), F32),
        ] + [pltpu.VMEM((BLOCKS + 2, rows + 32, BW), F32)] * 4,
        compiler_params=pltpu.CompilerParams(vmem_limit_bytes=VMEM_BYTES),
        name="basis",
    )(place, rhs, diag, *strips)


def solved(high, low):
    g = {}
    for n, (a, b) in enumerate(PAIRS):
        g[a, b] = g[b, a] = (high[n], low[n])

    def times(factor, pair):
        return factor * pair[0], factor * pair[1]

    m = [[None] * 4 for _ in range(4)]
    for j in range(4):
        for i in range(j + 1):
            value = pair_sum(*times(MID, g[i, j]), *times(8.0 if j else 16.0, g[i, j + 1]))
            if j:
                value = pair_sum(*value, *times(0.5, g[i, j - 1]))
            m[i][j] = m[j][i] = two_sum(*value)

    work = [[m[i][j][0] for j in range(4)] for i in range(4)]
    inverse = []
    factor = [[None] * 4 for _ in range(4)]
    for k in range(4):
        pivot = work[k][k]
        inverse.append(jnp.where(pivot > 0.0, 1.0 / jnp.where(pivot > 0.0, pivot, 1.0), 0.0))
        for i in range(k + 1, 4):
            factor[i][k] = work[k][i] * inverse[k]
        for i in range(k + 1, 4):
            for j in range(i, 4):
                work[i][j] = work[i][j] - factor[i][k] * work[k][j]

    def solve(y):
        y = list(y)
        for k in range(4):
            for i in range(k + 1, 4):
                y[i] = y[i] - factor[i][k] * y[k]
        y = [y[k] * inverse[k] for k in range(4)]
        for k in range(3, -1, -1):
            for i in range(k):
                y[i] = y[i] - factor[k][i] * y[k]
        return y

    rest = [g[0, i] for i in range(4)]
    c = solve([pair[0] for pair in rest])
    found = [c]
    for _ in range(2):
        for i in range(4):
            for j in range(4):
                product, error = two_product(m[i][j][0], c[j])
                total, lost = two_sum(rest[i][0], -product)
                rest[i] = total, rest[i][1] + (lost - error - m[i][j][1] * c[j])
        rest = [two_sum(*pair) for pair in rest]
        c = solve([pair[0] for pair in rest])
        found.append(c)
    c = [found[0][k] + (found[1][k] + found[2][k]) for k in range(4)]
    r = [
        1.0 - (MID * c[0] + 0.5 * c[1]),
        -(16.0 * c[0] + MID * c[1] + 0.5 * c[2]),
        -(8.0 * c[1] + MID * c[2] + 0.5 * c[3]),
        -(8.0 * c[2] + MID * c[3]),
        -(8.0 * c[3]),
    ]
    return c, r


def combine_kernel(gram_ref, q_ref, x_ref, r_ref):
    rows = q_ref.shape[2]
    terms = [(gram_ref[n:n + 8], jnp.zeros((8, BW), F32)) for n in range(0, gram_ref.shape[0], 8)]
    while len(terms) > 1:
        terms = [pair_sum(*terms[n], *terms[n + 1]) for n in range(0, len(terms), 2)]
    high, low = all_rows(*terms[0])
    high, low = two_sum(high, low + pltpu.roll(high, BW - LOW, 1))
    first = high[0:1, 0:1]
    scale = jnp.where(first > 1e25, 2.0 ** -60, jnp.where(first < 1e-15, 2.0 ** 60, 1.0))
    lane = lax.broadcasted_iota(jnp.int32, (1, BW), 1)

    def pick(values, n):
        row = jnp.where(lane == n, values[0:1], 0.0)
        return scale * jnp.sum(row, axis=1, keepdims=True)

    count = range(len(PAIRS))
    c, r = solved([pick(high, n) for n in count], [pick(low, n) for n in count])
    c = [jnp.broadcast_to(value, (rows, BW)) for value in c]
    r = [jnp.broadcast_to(value, (rows, BW)) for value in r]
    for i in range(q_ref.shape[1]):
        q = [q_ref[k, i] for k in range(5)]
        columns = slice(i * BW, (i + 1) * BW)
        x_ref[:, columns] = sum(c[k] * q[k] for k in range(4))
        r_ref[:, columns] = sum(r[k] * q[k] for k in range(5))


def combine(gram, q):
    _, blocks, rows, _ = q.shape
    out = jax.ShapeDtypeStruct((rows, blocks * BW), F32)
    vmem = pl.BlockSpec(memory_space=pltpu.VMEM)
    return pl.pallas_call(
        combine_kernel,
        out_shape=[out, out],
        in_specs=[vmem, vmem],
        out_specs=[vmem, vmem],
        compiler_params=pltpu.CompilerParams(vmem_limit_bytes=VMEM_BYTES),
        name="combine",
    )(gram, q)


def body(piece_height, piece_weight, piece_column, piece_width):
    lon_count, lat_count = lax.axis_size("lon"), lax.axis_size("lat")
    rows = piece_height.shape[1]
    lon, lat = lax.axis_index("lon"), lax.axis_index("lat")
    place = jnp.stack([lat, jnp.int32(lat_count), lon]).astype(jnp.int32)

    packed = pack(piece_column, piece_width, piece_height, piece_weight, lon_count)
    got = lax.all_to_all(packed, "lon", split_axis=0, concat_axis=0, tiled=True)
    part = 2 * rows
    above = passed_along(got[:, :CAPACITY * part:part], "lat", -1)
    rhs, diag, own_one, own_two, edge = sums(place, got, above, rows)

    one = swapped(own_one, "lat", 0, False)
    two = swapped(own_two, "lat", 1, False)
    first_edge = (BLOCKS - 1) * (1 - lon % 2)
    strips = []
    for start, block in ((0, first_edge), (1, BLOCKS - 1 - first_edge)):
        pick = lambda strip: lax.dynamic_index_in_dim(strip, block, 0, keepdims=False)
        message = jnp.concatenate([edge[start], pick(one), pick(two)], axis=0)
        strips.append(swapped(message, "lon", start, True))
    q, gram = basis(place, rhs, diag, own_one, own_two, one, two, *strips)
    spread = jnp.broadcast_to(gram[None], (lon_count * lat_count, 1, BW))
    grams = lax.all_to_all(spread, ("lon", "lat"), split_axis=0, concat_axis=0, tiled=True)
    return tuple(combine(grams.reshape(lon_count * lat_count, BW), q))


def solution(mesh):
    return jax.shard_map(
        body,
        mesh=mesh,
        in_specs=(P("lon", "lat", None), P("lon", "lat", None), P("lon"), P("lon")),
        out_specs=(P("lat", "lon"), P("lat", "lon")),
        check_vma=False,
    )
```

```python
import jax
import jax.numpy as jnp
from jax import lax
from jax.experimental import pallas as pl
from jax.experimental.pallas import tpu as pltpu
from jax.sharding import PartitionSpec as P

ROWS = 128
COLS_DEV = 4096
BW = 128
BLOCKS = COLS_DEV // BW
CAPACITY = 2

MU_DATA = 0.5
DAMPING = 0.5
RIDGE = 0.05

MID = 4.0
VMEM_BYTES = 40 * 1024 * 1024
PACK_VMEM_BYTES = 60 * 1024 * 1024
F32 = jnp.float32


def passed_along(block, axis, distance):
    devices = range(lax.axis_size(axis))
    route = [(i, i + distance) for i in devices if i + distance in devices]
    return lax.ppermute(block, axis, route)


def swapped(block, axis, start, around):
    count = lax.axis_size(axis)
    lows = range(start, count if around else count - 1, 2)
    pairs = [(low, (low + 1) % count) for low in lows]
    return lax.ppermute(block, axis, pairs + [(b, a) for a, b in pairs])


def pack_kernel(column_ref, width_ref, height_ref, weight_ref, out_ref, held_ref, facts_ref,
                count_ref, in_sem, out_sem, facts_sem):
    tiles, pieces = out_ref.shape[0], height_ref.shape[0]
    rows = height_ref.shape[1]
    part = 2 * rows
    batch = pieces // in_sem.shape[0]
    lane = lax.broadcasted_iota(jnp.int32, (1, BW), 1)

    def loads(g):
        part = pl.ds(g * batch, batch)
        sources = (height_ref, weight_ref)
        return [pltpu.make_async_copy(source.at[part], held_ref.at[part, pl.ds(n * rows, rows)],
                                      in_sem.at[g, n]) for n, source in enumerate(sources)]

    for g in range(in_sem.shape[0]):
        for load in loads(g):
            load.start()

    facts_ref[...] = jnp.zeros_like(facts_ref)

    @pl.loop(0, tiles, unroll=8)
    def _(t):
        count_ref[t] = 0

    for g in range(in_sem.shape[0]):
        for load in loads(g):
            load.wait()

        @pl.loop(g * batch, (g + 1) * batch, unroll=4)
        def _(p):
            tile = column_ref[p] // COLS_DEV
            block = column_ref[p] % COLS_DEV // BW
            slot = count_ref[tile]
            count_ref[tile] = slot + 1
            at = 2 * slot
            facts = jnp.where(lane == at, block + 1, jnp.where(lane == at + 1, width_ref[p], 0))
            facts_ref[tile] += facts.astype(F32)
            pltpu.make_async_copy(held_ref.at[p], out_ref.at[tile, pl.ds(slot * part, part)],
                                  out_sem).start()

    facts = pltpu.make_async_copy(facts_ref, out_ref.at[:, CAPACITY * part], facts_sem)
    facts.start()
    pltpu.make_async_copy(held_ref, out_ref.at[pl.ds(0, pieces), pl.ds(0, part)], out_sem).wait()
    facts.wait()


def pack(piece_column, piece_width, piece_height, piece_weight, tiles, batches=8):
    pieces, rows, _ = piece_height.shape
    tall = lambda array: array.reshape(pieces, rows, 1, BW)
    return pl.pallas_call(
        pack_kernel,
        out_shape=jax.ShapeDtypeStruct((tiles, CAPACITY * 2 * rows + 1, 1, BW), F32),
        in_specs=[
            pl.BlockSpec(memory_space=pltpu.SMEM),
            pl.BlockSpec(memory_space=pltpu.SMEM),
            pl.BlockSpec(memory_space=pl.ANY),
            pl.BlockSpec(memory_space=pl.ANY),
        ],
        out_specs=pl.BlockSpec(memory_space=pl.ANY),
        scratch_shapes=[
            pltpu.VMEM((pieces, 2 * rows, 1, BW), F32),
            pltpu.VMEM((tiles, 1, BW), F32),
            pltpu.SMEM((tiles,), jnp.int32),
            pltpu.SemaphoreType.DMA((batches, 2)),
            pltpu.SemaphoreType.DMA,
            pltpu.SemaphoreType.DMA,
        ],
        compiler_params=pltpu.CompilerParams(vmem_limit_bytes=PACK_VMEM_BYTES),
        name="pack",
    )(piece_column, piece_width, tall(piece_height), tall(piece_weight))


def gather_kernel(place_ref, got_ref, rows_ref, rhs_ref, diag_ref, one_ref, two_ref, last_ref,
                  inverse_ref, blocks_ref, total_ref, held_ref, facts_ref, facts_sem, sem):
    rows = rhs_ref.shape[1]
    lat, lat_count = place_ref[0], place_ref[1]
    part = 2 * rows
    message = CAPACITY * part + 1
    chunks, height, _ = held_ref.shape
    sources = height // message
    lane = lax.broadcasted_iota(jnp.int32, (rows, BW), 1)
    row = lax.broadcasted_iota(jnp.int32, (rows, BW), 0)

    def load(n):
        rows_of = rows_ref.at[pl.ds(n * height, height)]
        return pltpu.make_async_copy(rows_of, held_ref.at[n], sem.at[n])

    facts = pltpu.make_async_copy(got_ref.at[:, message - 1], facts_ref, facts_sem)
    facts.start()
    for n in range(chunks):
        load(n).start()
    total_ref[...] = jnp.zeros_like(total_ref)
    facts.wait()

    @pl.loop(0, chunks)
    def _(n):
        load(n).wait()
        for s in range(sources * CAPACITY):
            source, slot = s // CAPACITY, s % CAPACITY
            block = facts_ref[n * sources + source, 0, 2 * slot].astype(jnp.int32) - 1
            block = jnp.where(block < 0, BLOCKS, block)
            width = facts_ref[n * sources + source, 0, 2 * slot + 1].astype(jnp.int32)
            base = source * message
            start = base + slot * part
            height = held_ref[n, start:start + rows]
            weight = held_ref[n, start + rows:start + part]
            cell = jnp.where(lane < width, weight, 0.0)
            east = jnp.where(lane < width - 1, weight, 0.0)
            east_step = pltpu.roll(height, BW - 1, 1) - height
            raised = jnp.where(row == rows - 1, 0.0, pltpu.roll(height, rows - 1, 0))
            terms = (cell, cell * height, east, east * east_step, cell * (raised - height))
            for k, term in enumerate(terms):
                total_ref[block, k] += term
            last_ref[n * sources + source, slot] = cell[rows - 8:]
            blocks_ref[(n * sources + source) * CAPACITY + slot] = block

    last = (row == rows - 1) & (lat == lat_count - 1)
    first = (row == 0) & (lat == 0)
    sides = 4.0 - last.astype(F32) - first.astype(F32) + RIDGE
    row8 = row[:8]
    lat_even = lat % 2 == 0

    @pl.loop(0, BLOCKS, unroll=4)
    def _(i):
        cell, height = total_ref[i, 0], total_ref[i, 1]
        east = total_ref[i, 3] / (total_ref[i, 2] + DAMPING)
        north = jnp.where(last, 0.0, total_ref[i, 4] / (cell + DAMPING))
        south = jnp.where(row == 0, 0.0, pltpu.roll(north, 1, 0))
        rhs = MU_DATA * height - (east - pltpu.roll(east, 1, 1)) - (north - south)
        diag = MU_DATA * cell + sides
        rhs_ref[i] = rhs
        diag_ref[i] = diag
        top = pltpu.roll(diag[rows - 8:], 4, 0)
        top = jnp.where(row8 == 0, pltpu.roll(north[rows - 8:], 1, 0), top)
        up = jnp.where(row8 >= 4, rhs[rows - 8:], top)
        down = jnp.where(row8 >= 4, pltpu.roll(diag[:8], 4, 0), rhs[:8])
        one_ref[i] = jnp.where(lat_even, up, down)
        two_ref[i] = jnp.where(lat_even, down, up)
        inverse_ref[i] = 1.0 / (cell[rows - 8:] + DAMPING)


def gather(place, got, rows, chunks=2):
    tiles, message, _, _ = got.shape
    height = tiles * message // chunks
    field = (BLOCKS, rows, BW)
    strip = (BLOCKS, 8, BW)
    vmem = pl.BlockSpec(memory_space=pltpu.VMEM)
    shapes = (field, field, strip, strip, (tiles, CAPACITY, 8, BW), strip)
    return pl.pallas_call(
        gather_kernel,
        out_shape=[jax.ShapeDtypeStruct(s, F32) for s in shapes]
        + [jax.ShapeDtypeStruct((tiles * CAPACITY,), jnp.int32)],
        in_specs=[pl.BlockSpec(memory_space=pltpu.SMEM)] + [pl.BlockSpec(memory_space=pl.ANY)] * 2,
        out_specs=[vmem] * len(shapes) + [pl.BlockSpec(memory_space=pltpu.SMEM)],
        scratch_shapes=[
            pltpu.VMEM((BLOCKS + 1, 5, rows, BW), F32),
            pltpu.VMEM((chunks, height, BW), F32),
            pltpu.SMEM((tiles, 1, BW), F32),
            pltpu.SemaphoreType.DMA,
            pltpu.SemaphoreType.DMA((chunks,)),
        ],
        compiler_params=pltpu.CompilerParams(vmem_limit_bytes=VMEM_BYTES),
        name="gather",
    )(place, got, got.reshape(chunks * height, BW))


def finish_kernel(place_ref, blocks_ref, rhs_ref, diag_ref, part_one_ref, part_two_ref, last_ref,
                  inverse_ref, above_ref, gain_ref, one_ref, two_ref, edge_ref, *fix_refs):
    rows = rhs_ref.shape[1]
    tiles = last_ref.shape[0]
    lat, lon = place_ref[0], place_ref[2]
    lat_even = lat % 2 == 0
    row8 = lax.broadcasted_iota(jnp.int32, (8, BW), 0)
    for ref in fix_refs:
        ref[...] = jnp.zeros_like(ref)

    @pl.loop(0, tiles // 2, unroll=8)
    def _(n):
        for k, ref in enumerate(fix_refs):
            source, slot = 2 * n + k // CAPACITY, k % CAPACITY
            block = blocks_ref[source * CAPACITY + slot]
            ref[block] += last_ref[source, slot] * above_ref[source, slot]

    @pl.loop(0, BLOCKS, unroll=8)
    def _(i):
        gain = sum(ref[i] for ref in fix_refs) * inverse_ref[i]
        gain = jnp.where(row8 == 7, gain, 0.0)
        gain_ref[i] = gain
        up = pltpu.roll(gain, 1, 0) - gain
        one_ref[i] = part_one_ref[i] + jnp.where(lat_even, up, 0.0)
        two_ref[i] = part_two_ref[i] + jnp.where(lat_even, 0.0, up)

    first_edge = (BLOCKS - 1) * (1 - lon % 2)
    for side, block in ((0, first_edge), (1, BLOCKS - 1 - first_edge)):
        edge_ref[side, 0:rows - 8] = rhs_ref[block, 0:rows - 8]
        edge_ref[side, rows - 8:rows] = rhs_ref[block, rows - 8:rows] - gain_ref[block]
        edge_ref[side, rows:2 * rows] = diag_ref[block]
        edge_ref[side, 2 * rows:2 * rows + 8] = jnp.where(lat_even, one_ref[block], two_ref[block])


def finish(place, blocks, rhs, diag, *strips):
    rows = rhs.shape[1]
    strip = (BLOCKS, 8, BW)
    edge = (2, 2 * rows + 8, BW)
    vmem = pl.BlockSpec(memory_space=pltpu.VMEM)
    return pl.pallas_call(
        finish_kernel,
        out_shape=[jax.ShapeDtypeStruct(s, F32) for s in (strip, strip, strip, edge)],
        in_specs=[
            pl.BlockSpec(memory_space=pltpu.SMEM),
            pl.BlockSpec(memory_space=pltpu.SMEM),
        ] + [vmem] * 7,
        out_specs=[vmem] * 4,
        scratch_shapes=[pltpu.VMEM((BLOCKS + 1, 8, BW), F32)] * 4,
        compiler_params=pltpu.CompilerParams(vmem_limit_bytes=VMEM_BYTES),
        name="finish",
    )(place, blocks, rhs, diag, *strips)


def two_sum(a, b):
    total = a + b
    part = total - a
    return total, (a - (total - part)) + (b - part)


def pair_sum(high, low, other_high, other_low):
    total, error = two_sum(high, other_high)
    return total, low + other_low + error


def two_product(a, b):
    def split(x):
        big = 4097.0 * x
        top = big - (big - x)
        return top, x - top

    product = a * b
    (a_top, a_end), (b_top, b_end) = split(a), split(b)
    return product, ((a_top * b_top - product) + a_top * b_end + a_end * b_top) + a_end * b_end


def all_rows(high, low):
    for shift in (4, 2, 1):
        high, low = pair_sum(high, low, pltpu.roll(high, shift, 0), pltpu.roll(low, shift, 0))
    return high, low


PAIRS = [(i, j) for j in range(5) for i in range(min(j, 3) + 1)]
LOW = 16


def basis_kernel(place_ref, rhs_ref, diag_ref, gain_ref, own_one_ref, own_two_ref, one_ref, two_ref,
                 lon_one_ref, lon_two_ref, q_ref, gram_ref, scale_ref, *v_refs):
    rows = rhs_ref.shape[1]
    tall = rows + 16
    lat, lat_count, lon = place_ref[0], place_ref[1], place_ref[2]
    lat_even = lat % 2 == 0
    row = lax.broadcasted_iota(jnp.int32, (rows, BW), 0)
    row8 = row[:8]
    lane = lax.broadcasted_iota(jnp.int32, (tall, BW), 1)

    def assemble(i, rhs, diag, up, one, two):
        south = jnp.where(lat_even, two, one)
        north = jnp.where(lat_even, one, two)
        first = jnp.where(row == 0, south[0:1], 0.0) + rhs
        below = jnp.where(row8 >= 4, south, 0.0)
        above = jnp.where(row8 == 0, north + up, jnp.where(row8 < 4, north, 0.0))
        v_refs[0][i, 8:8 + tall] = jnp.concatenate([below, first, above], axis=0)
        diag = jnp.concatenate([pltpu.roll(south, 4, 0), diag, pltpu.roll(north, 4, 0)], axis=0)
        scale_ref[i] = (diag - MID) * 0.125

    side = (BLOCKS + 1) * (1 - lon % 2)
    for i, ref in ((side, lon_one_ref), (BLOCKS + 1 - side, lon_two_ref)):
        two = 2 * rows
        assemble(i, ref[0:rows], ref[rows:two], ref[two:two + 8], ref[two + 8:two + 16],
                 ref[two + 16:two + 24])

    @pl.loop(0, BLOCKS, unroll=4)
    def _(i):
        up = jnp.where(lat_even, own_one_ref[i], own_two_ref[i])
        tail = rhs_ref[i, rows - 8:rows] - gain_ref[i]
        rhs = jnp.concatenate([rhs_ref[i, 0:rows - 8], tail], axis=0)
        assemble(i + 1, rhs, diag_ref[i], up, one_ref[i], two_ref[i])

    def applied(k, i):
        body = slice(8, 8 + tall)
        v = v_refs[k][i, body]
        left = v_refs[k][jnp.maximum(i - 1, 0), body]
        right = v_refs[k][jnp.minimum(i + 1, BLOCKS + 1), body]
        west = pltpu.roll(jnp.where(lane == BW - 1, left, v), 1, 1)
        east = pltpu.roll(jnp.where(lane == 0, right, v), BW - 1, 1)
        south = v_refs[k][i, 7:7 + tall]
        north = v_refs[k][i, 9:9 + tall]
        image = scale_ref[i] * v - 0.125 * ((west + east) + (south + north))
        if k == 0:
            image = 0.5 * image
        else:
            image = image - 0.0625 * v_refs[k - 1][i, body]
        ends = (jnp.where(lat > 0, image[:8], 0.0), image[8:rows + 8],
                jnp.where(lat < lat_count - 1, image[rows + 8:], 0.0))
        return jnp.concatenate(ends, axis=0)

    for k in range(3):
        @pl.loop(0, BLOCKS + 2, unroll=34)
        def _(i, k=k):
            v_refs[k + 1][i, 8:8 + tall] = applied(k, i)

    def products(i, carry):
        last = applied(3, i + 1)[8:8 + rows]
        q = [v_refs[k][i + 1, 16:16 + rows] for k in range(4)] + [last]
        for k in range(5):
            q_ref[k, i] = q[k]
        out = []
        for total, (a, b) in zip(carry, PAIRS):
            term = q[a] * q[b]
            out.append(total + sum(term[8 * n:8 * n + 8] for n in range(rows // 8)))
        return tuple(out)

    zero = tuple(jnp.zeros((8, BW), F32) for _ in PAIRS)
    totals = lax.fori_loop(0, BLOCKS, products, zero, unroll=8)
    row_of = lax.broadcasted_iota(jnp.int32, (8, BW), 0)
    lane_of = lax.broadcasted_iota(jnp.int32, (8, BW), 1)
    gram = jnp.zeros((8, BW), F32)
    for start in range(0, len(PAIRS), 8):
        high = jnp.zeros((8, BW), F32)
        low = jnp.zeros((8, BW), F32)
        for n, total in enumerate(totals[start:start + 8]):
            pair = all_rows(total, jnp.zeros_like(total))
            high = jnp.where(row_of == n, pair[0], high)
            low = jnp.where(row_of == n, pair[1], low)
        shift = BW // 2
        while shift:
            high, low = pair_sum(high, low, pltpu.roll(high, shift, 1), pltpu.roll(low, shift, 1))
            shift //= 2
        gram = jnp.where(lane_of == row_of + start, high, gram)
        gram = jnp.where(lane_of == row_of + start + LOW, low, gram)
    gram_ref[...] = jnp.sum(gram, axis=0, keepdims=True)


def basis(place, rhs, diag, *strips):
    rows = rhs.shape[1]
    vmem = pl.BlockSpec(memory_space=pltpu.VMEM)
    return pl.pallas_call(
        basis_kernel,
        out_shape=[
            jax.ShapeDtypeStruct((5, BLOCKS, rows, BW), F32),
            jax.ShapeDtypeStruct((1, BW), F32),
        ],
        in_specs=[pl.BlockSpec(memory_space=pltpu.SMEM)] + [vmem] * 9,
        out_specs=[vmem, vmem],
        scratch_shapes=[
            pltpu.VMEM((BLOCKS + 2, rows + 16, BW), F32),
        ] + [pltpu.VMEM((BLOCKS + 2, rows + 32, BW), F32)] * 4,
        compiler_params=pltpu.CompilerParams(vmem_limit_bytes=VMEM_BYTES),
        name="basis",
    )(place, rhs, diag, *strips)


def solved(high, low):
    g = {}
    for n, (a, b) in enumerate(PAIRS):
        g[a, b] = g[b, a] = (high[n], low[n])

    def times(factor, pair):
        return factor * pair[0], factor * pair[1]

    m = [[None] * 4 for _ in range(4)]
    for j in range(4):
        for i in range(j + 1):
            value = pair_sum(*times(MID, g[i, j]), *times(8.0 if j else 16.0, g[i, j + 1]))
            if j:
                value = pair_sum(*value, *times(0.5, g[i, j - 1]))
            m[i][j] = m[j][i] = two_sum(*value)

    work = [[m[i][j][0] for j in range(4)] for i in range(4)]
    inverse = []
    factor = [[None] * 4 for _ in range(4)]
    for k in range(4):
        pivot = work[k][k]
        inverse.append(jnp.where(pivot > 0.0, 1.0 / jnp.where(pivot > 0.0, pivot, 1.0), 0.0))
        for i in range(k + 1, 4):
            factor[i][k] = work[k][i] * inverse[k]
        for i in range(k + 1, 4):
            for j in range(i, 4):
                work[i][j] = work[i][j] - factor[i][k] * work[k][j]

    def solve(y):
        y = list(y)
        for k in range(4):
            for i in range(k + 1, 4):
                y[i] = y[i] - factor[i][k] * y[k]
        y = [y[k] * inverse[k] for k in range(4)]
        for k in range(3, -1, -1):
            for i in range(k):
                y[i] = y[i] - factor[k][i] * y[k]
        return y

    rest = [g[0, i] for i in range(4)]
    c = solve([pair[0] for pair in rest])
    found = [c]
    for _ in range(2):
        for i in range(4):
            for j in range(4):
                product, error = two_product(m[i][j][0], c[j])
                total, lost = two_sum(rest[i][0], -product)
                rest[i] = total, rest[i][1] + (lost - error - m[i][j][1] * c[j])
        rest = [two_sum(*pair) for pair in rest]
        c = solve([pair[0] for pair in rest])
        found.append(c)
    c = [found[0][k] + (found[1][k] + found[2][k]) for k in range(4)]
    r = [
        1.0 - (MID * c[0] + 0.5 * c[1]),
        -(16.0 * c[0] + MID * c[1] + 0.5 * c[2]),
        -(8.0 * c[1] + MID * c[2] + 0.5 * c[3]),
        -(8.0 * c[2] + MID * c[3]),
        -(8.0 * c[3]),
    ]
    return c, r


def combine_kernel(gram_ref, q_ref, x_ref, r_ref):
    rows = q_ref.shape[2]
    terms = [(gram_ref[n:n + 8], jnp.zeros((8, BW), F32)) for n in range(0, gram_ref.shape[0], 8)]
    while len(terms) > 1:
        terms = [pair_sum(*terms[n], *terms[n + 1]) for n in range(0, len(terms), 2)]
    high, low = all_rows(*terms[0])
    high, low = two_sum(high, low + pltpu.roll(high, BW - LOW, 1))
    first = high[0:1, 0:1]
    scale = jnp.where(first > 1e25, 2.0 ** -60, jnp.where(first < 1e-15, 2.0 ** 60, 1.0))
    lane = lax.broadcasted_iota(jnp.int32, (1, BW), 1)

    def pick(values, n):
        row = jnp.where(lane == n, values[0:1], 0.0)
        return scale * jnp.sum(row, axis=1, keepdims=True)

    count = range(len(PAIRS))
    c, r = solved([pick(high, n) for n in count], [pick(low, n) for n in count])
    c = [jnp.broadcast_to(value, (rows, BW)) for value in c]
    r = [jnp.broadcast_to(value, (rows, BW)) for value in r]
    for i in range(q_ref.shape[1]):
        q = [q_ref[k, i] for k in range(5)]
        columns = slice(i * BW, (i + 1) * BW)
        x_ref[:, columns] = sum(c[k] * q[k] for k in range(4))
        r_ref[:, columns] = sum(r[k] * q[k] for k in range(5))


def combine(gram, q):
    _, blocks, rows, _ = q.shape
    out = jax.ShapeDtypeStruct((rows, blocks * BW), F32)
    vmem = pl.BlockSpec(memory_space=pltpu.VMEM)
    return pl.pallas_call(
        combine_kernel,
        out_shape=[out, out],
        in_specs=[vmem, vmem],
        out_specs=[vmem, vmem],
        compiler_params=pltpu.CompilerParams(vmem_limit_bytes=VMEM_BYTES),
        name="combine",
    )(gram, q)


def body(piece_height, piece_weight, piece_column, piece_width):
    lon_count, lat_count = lax.axis_size("lon"), lax.axis_size("lat")
    rows = piece_height.shape[1]
    lon, lat = lax.axis_index("lon"), lax.axis_index("lat")
    place = jnp.stack([lat, jnp.int32(lat_count), lon]).astype(jnp.int32)

    packed = pack(piece_column, piece_width, piece_height, piece_weight, lon_count)
    got = lax.all_to_all(packed, "lon", split_axis=0, concat_axis=0, tiled=True)
    part = 2 * rows
    above = passed_along(got[:, :CAPACITY * part:part], "lat", -1)
    rhs, diag, *strips, blocks = gather(place, got, rows)
    gain, own_one, own_two, edge = finish(place, blocks, rhs, diag, *strips, above)

    one = swapped(own_one, "lat", 0, False)
    two = swapped(own_two, "lat", 1, False)
    first_edge = (BLOCKS - 1) * (1 - lon % 2)
    strips = []
    for start, block in ((0, first_edge), (1, BLOCKS - 1 - first_edge)):
        pick = lambda strip: lax.dynamic_index_in_dim(strip, block, 0, keepdims=False)
        message = jnp.concatenate([edge[start], pick(one), pick(two)], axis=0)
        strips.append(swapped(message, "lon", start, True))
    q, gram = basis(place, rhs, diag, gain, own_one, own_two, one, two, *strips)
    spread = jnp.broadcast_to(gram[None], (lon_count * lat_count, 1, BW))
    grams = lax.all_to_all(spread, ("lon", "lat"), split_axis=0, concat_axis=0, tiled=True)
    return tuple(combine(grams.reshape(lon_count * lat_count, BW), q))


def solution(mesh):
    return jax.shard_map(
        body,
        mesh=mesh,
        in_specs=(P("lon", "lat", None), P("lon", "lat", None), P("lon"), P("lon")),
        out_specs=(P("lat", "lon"), P("lat", "lon")),
        check_vma=False,
    )
```

```python
import jax
import jax.numpy as jnp
from jax import lax
from jax.experimental import pallas as pl
from jax.experimental.pallas import tpu as pltpu
from jax.sharding import PartitionSpec as P

ROWS = 128
COLS_DEV = 4096
BW = 128
BLOCKS = COLS_DEV // BW
CAPACITY = 2

MU_DATA = 0.5
DAMPING = 0.5
RIDGE = 0.05

MID = 4.0
VMEM_BYTES = 40 * 1024 * 1024
PACK_VMEM_BYTES = 60 * 1024 * 1024
F32 = jnp.float32


def passed_along(block, axis, distance):
    devices = range(lax.axis_size(axis))
    route = [(i, i + distance) for i in devices if i + distance in devices]
    return lax.ppermute(block, axis, route)


def swapped(block, axis, start, around):
    count = lax.axis_size(axis)
    lows = range(start, count if around else count - 1, 2)
    pairs = [(low, (low + 1) % count) for low in lows]
    return lax.ppermute(block, axis, pairs + [(b, a) for a, b in pairs])


def pack_kernel(column_ref, width_ref, height_ref, weight_ref, out_ref, held_ref, facts_ref,
                count_ref, in_sem, out_sem, facts_sem):
    tiles, pieces = out_ref.shape[0], height_ref.shape[0]
    rows = height_ref.shape[1]
    part = 2 * rows
    batch = pieces // in_sem.shape[0]
    lane = lax.broadcasted_iota(jnp.int32, (1, BW), 1)

    def loads(g):
        part = pl.ds(g * batch, batch)
        sources = (height_ref, weight_ref)
        return [pltpu.make_async_copy(source.at[part], held_ref.at[part, pl.ds(n * rows, rows)],
                                      in_sem.at[g, n]) for n, source in enumerate(sources)]

    for g in range(in_sem.shape[0]):
        for load in loads(g):
            load.start()

    facts_ref[...] = jnp.zeros_like(facts_ref)

    @pl.loop(0, tiles, unroll=8)
    def _(t):
        count_ref[t] = 0

    for g in range(in_sem.shape[0]):
        for load in loads(g):
            load.wait()

        @pl.loop(g * batch, (g + 1) * batch, unroll=4)
        def _(p):
            tile = column_ref[p] // COLS_DEV
            block = column_ref[p] % COLS_DEV // BW
            slot = count_ref[tile]
            count_ref[tile] = slot + 1
            at = 2 * slot
            facts = jnp.where(lane == at, block + 1, jnp.where(lane == at + 1, width_ref[p], 0))
            facts_ref[tile] += facts.astype(F32)
            pltpu.make_async_copy(held_ref.at[p], out_ref.at[tile, pl.ds(slot * part, part)],
                                  out_sem).start()

    facts = pltpu.make_async_copy(facts_ref, out_ref.at[:, CAPACITY * part], facts_sem)
    facts.start()
    pltpu.make_async_copy(held_ref, out_ref.at[pl.ds(0, pieces), pl.ds(0, part)], out_sem).wait()
    facts.wait()


def pack(piece_column, piece_width, piece_height, piece_weight, tiles, batches=8):
    pieces, rows, _ = piece_height.shape
    tall = lambda array: array.reshape(pieces, rows, 1, BW)
    return pl.pallas_call(
        pack_kernel,
        out_shape=jax.ShapeDtypeStruct((tiles, CAPACITY * 2 * rows + 1, 1, BW), F32),
        in_specs=[
            pl.BlockSpec(memory_space=pltpu.SMEM),
            pl.BlockSpec(memory_space=pltpu.SMEM),
            pl.BlockSpec(memory_space=pl.ANY),
            pl.BlockSpec(memory_space=pl.ANY),
        ],
        out_specs=pl.BlockSpec(memory_space=pl.ANY),
        scratch_shapes=[
            pltpu.VMEM((pieces, 2 * rows, 1, BW), F32),
            pltpu.VMEM((tiles, 1, BW), F32),
            pltpu.SMEM((tiles,), jnp.int32),
            pltpu.SemaphoreType.DMA((batches, 2)),
            pltpu.SemaphoreType.DMA,
            pltpu.SemaphoreType.DMA,
        ],
        compiler_params=pltpu.CompilerParams(vmem_limit_bytes=PACK_VMEM_BYTES),
        name="pack",
    )(piece_column, piece_width, tall(piece_height), tall(piece_weight))


def gather_kernel(place_ref, got_ref, rows_ref, rhs_ref, diag_ref, one_ref, two_ref, last_ref,
                  inverse_ref, blocks_ref, total_ref, held_ref, facts_ref, facts_sem, sem):
    rows = rhs_ref.shape[1]
    lat, lat_count = place_ref[0], place_ref[1]
    part = 2 * rows
    message = CAPACITY * part + 1
    chunks, height, _ = held_ref.shape
    sources = height // message
    lane = lax.broadcasted_iota(jnp.int32, (rows, BW), 1)
    row = lax.broadcasted_iota(jnp.int32, (rows, BW), 0)

    def load(n):
        rows_of = rows_ref.at[pl.ds(n * height, height)]
        return pltpu.make_async_copy(rows_of, held_ref.at[n], sem.at[n])

    facts = pltpu.make_async_copy(got_ref.at[:, message - 1], facts_ref, facts_sem)
    facts.start()
    for n in range(chunks):
        load(n).start()
    total_ref[...] = jnp.zeros_like(total_ref)
    facts.wait()

    @pl.loop(0, chunks)
    def _(n):
        load(n).wait()
        for s in range(sources * CAPACITY):
            source, slot = s // CAPACITY, s % CAPACITY
            block = facts_ref[n * sources + source, 0, 2 * slot].astype(jnp.int32) - 1
            block = jnp.where(block < 0, BLOCKS, block)
            width = facts_ref[n * sources + source, 0, 2 * slot + 1].astype(jnp.int32)
            base = source * message
            start = base + slot * part
            height = held_ref[n, start:start + rows]
            weight = held_ref[n, start + rows:start + part]
            cell = jnp.where(lane < width, weight, 0.0)
            east = jnp.where(lane < width - 1, weight, 0.0)
            east_step = pltpu.roll(height, BW - 1, 1) - height
            raised = jnp.where(row == rows - 1, 0.0, pltpu.roll(height, rows - 1, 0))
            terms = (cell, cell * height, east, east * east_step, cell * (raised - height))
            for k, term in enumerate(terms):
                total_ref[block, k] += term
            last_ref[n * sources + source, slot] = cell[rows - 8:]
            blocks_ref[(n * sources + source) * CAPACITY + slot] = block

    last = (row == rows - 1) & (lat == lat_count - 1)
    first = (row == 0) & (lat == 0)
    sides = 4.0 - last.astype(F32) - first.astype(F32) + RIDGE
    row8 = row[:8]
    lat_even = lat % 2 == 0

    @pl.loop(0, BLOCKS, unroll=4)
    def _(i):
        cell, height = total_ref[i, 0], total_ref[i, 1]
        east = total_ref[i, 3] / (total_ref[i, 2] + DAMPING)
        north = jnp.where(last, 0.0, total_ref[i, 4] / (cell + DAMPING))
        south = jnp.where(row == 0, 0.0, pltpu.roll(north, 1, 0))
        rhs = MU_DATA * height - (east - pltpu.roll(east, 1, 1)) - (north - south)
        diag = MU_DATA * cell + sides
        rhs_ref[i] = rhs
        diag_ref[i] = diag
        top = pltpu.roll(diag[rows - 8:], 4, 0)
        top = jnp.where(row8 == 0, pltpu.roll(north[rows - 8:], 1, 0), top)
        up = jnp.where(row8 >= 4, rhs[rows - 8:], top)
        down = jnp.where(row8 >= 4, pltpu.roll(diag[:8], 4, 0), rhs[:8])
        one_ref[i] = jnp.where(lat_even, up, down)
        two_ref[i] = jnp.where(lat_even, down, up)
        inverse_ref[i] = 1.0 / (cell[rows - 8:] + DAMPING)


def gather(place, got, rows, chunks=2):
    tiles, message, _, _ = got.shape
    height = tiles * message // chunks
    field = (BLOCKS, rows, BW)
    strip = (BLOCKS, 8, BW)
    vmem = pl.BlockSpec(memory_space=pltpu.VMEM)
    shapes = (field, field, strip, strip, (tiles, CAPACITY, 8, BW), strip)
    return pl.pallas_call(
        gather_kernel,
        out_shape=[jax.ShapeDtypeStruct(s, F32) for s in shapes]
        + [jax.ShapeDtypeStruct((tiles * CAPACITY,), jnp.int32)],
        in_specs=[pl.BlockSpec(memory_space=pltpu.SMEM)] + [pl.BlockSpec(memory_space=pl.ANY)] * 2,
        out_specs=[vmem] * len(shapes) + [pl.BlockSpec(memory_space=pltpu.SMEM)],
        scratch_shapes=[
            pltpu.VMEM((BLOCKS + 1, 5, rows, BW), F32),
            pltpu.VMEM((chunks, height, BW), F32),
            pltpu.SMEM((tiles, 1, BW), F32),
            pltpu.SemaphoreType.DMA,
            pltpu.SemaphoreType.DMA((chunks,)),
        ],
        compiler_params=pltpu.CompilerParams(vmem_limit_bytes=VMEM_BYTES),
        name="gather",
    )(place, got, got.reshape(chunks * height, BW))


def finish_kernel(place_ref, blocks_ref, rhs_ref, diag_ref, part_one_ref, part_two_ref, last_ref,
                  inverse_ref, above_ref, gain_ref, one_ref, two_ref, edge_ref, *fix_refs):
    rows = rhs_ref.shape[1]
    tiles = last_ref.shape[0]
    lat, lon = place_ref[0], place_ref[2]
    lat_even = lat % 2 == 0
    row8 = lax.broadcasted_iota(jnp.int32, (8, BW), 0)
    for ref in fix_refs:
        ref[...] = jnp.zeros_like(ref)

    @pl.loop(0, tiles // 2, unroll=8)
    def _(n):
        for k, ref in enumerate(fix_refs):
            source, slot = 2 * n + k // CAPACITY, k % CAPACITY
            block = blocks_ref[source * CAPACITY + slot]
            ref[block] += last_ref[source, slot] * above_ref[source, slot]

    @pl.loop(0, BLOCKS, unroll=8)
    def _(i):
        gain = sum(ref[i] for ref in fix_refs) * inverse_ref[i]
        gain = jnp.where(row8 == 7, gain, 0.0)
        gain_ref[i] = gain
        up = pltpu.roll(gain, 1, 0) - gain
        one_ref[i] = part_one_ref[i] + jnp.where(lat_even, up, 0.0)
        two_ref[i] = part_two_ref[i] + jnp.where(lat_even, 0.0, up)

    first_edge = (BLOCKS - 1) * (1 - lon % 2)
    for side, block in ((0, first_edge), (1, BLOCKS - 1 - first_edge)):
        edge_ref[side, 0:rows - 8] = rhs_ref[block, 0:rows - 8]
        edge_ref[side, rows - 8:rows] = rhs_ref[block, rows - 8:rows] - gain_ref[block]
        edge_ref[side, rows:2 * rows] = diag_ref[block]
        edge_ref[side, 2 * rows:2 * rows + 8] = jnp.where(lat_even, one_ref[block], two_ref[block])


def finish(place, blocks, rhs, diag, *strips):
    rows = rhs.shape[1]
    strip = (BLOCKS, 8, BW)
    edge = (2, 2 * rows + 8, BW)
    vmem = pl.BlockSpec(memory_space=pltpu.VMEM)
    return pl.pallas_call(
        finish_kernel,
        out_shape=[jax.ShapeDtypeStruct(s, F32) for s in (strip, strip, strip, edge)],
        in_specs=[
            pl.BlockSpec(memory_space=pltpu.SMEM),
            pl.BlockSpec(memory_space=pltpu.SMEM),
        ] + [vmem] * 7,
        out_specs=[vmem] * 4,
        scratch_shapes=[pltpu.VMEM((BLOCKS + 1, 8, BW), F32)] * 4,
        compiler_params=pltpu.CompilerParams(vmem_limit_bytes=VMEM_BYTES),
        name="finish",
    )(place, blocks, rhs, diag, *strips)


def two_sum(a, b):
    total = a + b
    part = total - a
    return total, (a - (total - part)) + (b - part)


def pair_sum(high, low, other_high, other_low):
    total, error = two_sum(high, other_high)
    return total, low + other_low + error


def two_product(a, b):
    def split(x):
        big = 4097.0 * x
        top = big - (big - x)
        return top, x - top

    product = a * b
    (a_top, a_end), (b_top, b_end) = split(a), split(b)
    return product, ((a_top * b_top - product) + a_top * b_end + a_end * b_top) + a_end * b_end


def all_rows(high, low):
    for shift in (4, 2, 1):
        high, low = pair_sum(high, low, pltpu.roll(high, shift, 0), pltpu.roll(low, shift, 0))
    return high, low


PAIRS = [(i, j) for j in range(5) for i in range(min(j, 3) + 1)]
LOW = 16


class Field:
    def __init__(self, place_ref, rows, scale_ref, v_refs):
        self.rows, self.tall = rows, rows + 16
        self.scale_ref, self.v_refs = scale_ref, v_refs
        lat, lat_count = place_ref[0], place_ref[1]
        self.lat_even = lat % 2 == 0
        self.has_south, self.has_north = lat > 0, lat < lat_count - 1
        self.row = lax.broadcasted_iota(jnp.int32, (rows, BW), 0)
        self.lane = lax.broadcasted_iota(jnp.int32, (self.tall, BW), 1)

    def assemble(self, i, rhs, diag, up, one, two):
        row8 = self.row[:8]
        south = jnp.where(self.lat_even, two, one)
        north = jnp.where(self.lat_even, one, two)
        first = jnp.where(self.row == 0, south[0:1], 0.0) + rhs
        below = jnp.where(row8 >= 4, south, 0.0)
        above = jnp.where(row8 == 0, north + up, jnp.where(row8 < 4, north, 0.0))
        self.v_refs[0][i, 8:8 + self.tall] = jnp.concatenate([below, first, above], axis=0)
        diag = jnp.concatenate([pltpu.roll(south, 4, 0), diag, pltpu.roll(north, 4, 0)], axis=0)
        self.scale_ref[i] = (diag - MID) * 0.125

    def applied(self, k, i, left, right):
        ref, rows, tall = self.v_refs[k], self.rows, self.tall
        body = slice(8, 8 + tall)
        v = ref[i, body]
        west = pltpu.roll(jnp.where(self.lane == BW - 1, ref[left, body], v), 1, 1)
        east = pltpu.roll(jnp.where(self.lane == 0, ref[right, body], v), BW - 1, 1)
        south = ref[i, 7:7 + tall]
        north = ref[i, 9:9 + tall]
        image = self.scale_ref[i] * v - 0.125 * ((west + east) + (south + north))
        if k == 0:
            image = 0.5 * image
        else:
            image = image - 0.0625 * self.v_refs[k - 1][i, body]
        ends = (jnp.where(self.has_south, image[:8], 0.0), image[8:rows + 8],
                jnp.where(self.has_north, image[rows + 8:], 0.0))
        return jnp.concatenate(ends, axis=0)

    def step(self, k, i, left, right):
        self.v_refs[k + 1][i, 8:8 + self.tall] = self.applied(k, i, left, right)

    def products(self, i, left, right, q_ref, at, totals):
        rows = self.rows
        last = self.applied(3, i, left, right)[8:8 + rows]
        q = [self.v_refs[k][i, 16:16 + rows] for k in range(4)] + [last]
        for k in range(5):
            q_ref[k, at] = q[k]
        out = []
        for total, (a, b) in zip(totals, PAIRS):
            term = q[a] * q[b]
            out.append(total + sum(term[8 * n:8 * n + 8] for n in range(rows // 8)))
        return tuple(out)


NEAR = 6


def inner_kernel(place_ref, rhs_ref, diag_ref, gain_ref, own_one_ref, own_two_ref, one_ref,
                 two_ref, q_ref, totals_ref, sides_ref, scale_ref, *v_refs):
    rows = rhs_ref.shape[1]
    field = Field(place_ref, rows, scale_ref, v_refs)

    @pl.loop(0, BLOCKS, unroll=4)
    def _(i):
        up = jnp.where(field.lat_even, own_one_ref[i], own_two_ref[i])
        tail = rhs_ref[i, rows - 8:rows] - gain_ref[i]
        rhs = jnp.concatenate([rhs_ref[i, 0:rows - 8], tail], axis=0)
        field.assemble(i + 1, rhs, diag_ref[i], up, one_ref[i], two_ref[i])

    for k in range(3):
        @pl.loop(k + 2, BLOCKS - k, unroll=BLOCKS - 2 * k - 2)
        def _(i, k=k):
            field.step(k, i, i - 1, i + 1)

    def products(i, totals):
        return field.products(i, i - 1, i + 1, q_ref, i - 1, totals)

    zero = tuple(jnp.zeros((8, BW), F32) for _ in PAIRS)
    totals = lax.fori_loop(5, BLOCKS - 3, products, zero, unroll=8)
    for n, total in enumerate(totals):
        totals_ref[n] = total
    for k, ref in enumerate((scale_ref,) + v_refs):
        body = slice(8, 24 + rows) if k else slice(0, 16 + rows)
        for n in range(NEAR):
            sides_ref[0, k, n] = ref[n + 1, body]
            sides_ref[1, k, n] = ref[BLOCKS - n, body]


def inner(place, rhs, diag, *strips):
    rows = rhs.shape[1]
    vmem = pl.BlockSpec(memory_space=pltpu.VMEM)
    shapes = ((5, BLOCKS, rows, BW), (len(PAIRS), 8, BW), (2, 5, NEAR, rows + 16, BW))
    return pl.pallas_call(
        inner_kernel,
        out_shape=[jax.ShapeDtypeStruct(s, F32) for s in shapes],
        in_specs=[pl.BlockSpec(memory_space=pltpu.SMEM)] + [vmem] * 7,
        out_specs=[vmem] * 3,
        scratch_shapes=[pltpu.VMEM((BLOCKS + 2, rows + 16, BW), F32)]
        + [pltpu.VMEM((BLOCKS + 2, rows + 32, BW), F32)] * 4,
        compiler_params=pltpu.CompilerParams(vmem_limit_bytes=VMEM_BYTES),
        name="inner",
    )(place, rhs, diag, *strips)


def outer_kernel(place_ref, totals_ref, sides_ref, lon_one_ref, lon_two_ref, q_ref, gram_ref,
                 scale_ref, *v_refs):
    tall = sides_ref.shape[3]
    rows = tall - 16
    field = Field(place_ref, rows, scale_ref, v_refs)
    size = NEAR + 1
    for side in range(2):
        for n in range(NEAR):
            scale_ref[side * size + n + 1] = sides_ref[side, 0, n]
            for k in range(4):
                if n >= k:
                    v_refs[k][side * size + n + 1, 8:8 + tall] = sides_ref[side, k + 1, n]
    one_east = place_ref[2] % 2 == 0
    two = 2 * rows
    for side in range(2):
        first = lon_two_ref[...] if side == 0 else lon_one_ref[...]
        other = lon_one_ref[...] if side == 0 else lon_two_ref[...]
        strip = jnp.where(one_east, first, other)
        field.assemble(side * size, strip[0:rows], strip[rows:two], strip[two:two + 8],
                       strip[two + 8:two + 16], strip[two + 16:two + 24])

    def beside(side, n):
        inward, outward = side * size + n + 1, side * size + max(n - 1, 0)
        return (side * size + n,) + ((outward, inward) if side == 0 else (inward, outward))

    for k in range(3):
        for n in range(k + 2):
            for side in range(2):
                field.step(k, *beside(side, n))
    totals = tuple(totals_ref[n] for n in range(len(PAIRS)))
    for n in range(1, 5):
        for side in range(2):
            totals = field.products(*beside(side, n), q_ref, side * 4 + n - 1, totals)

    row_of = lax.broadcasted_iota(jnp.int32, (8, BW), 0)
    lane_of = lax.broadcasted_iota(jnp.int32, (8, BW), 1)
    gram = jnp.zeros((8, BW), F32)
    for start in range(0, len(PAIRS), 8):
        high = jnp.zeros((8, BW), F32)
        low = jnp.zeros((8, BW), F32)
        for n, total in enumerate(totals[start:start + 8]):
            pair = all_rows(total, jnp.zeros_like(total))
            high = jnp.where(row_of == n, pair[0], high)
            low = jnp.where(row_of == n, pair[1], low)
        shift = BW // 2
        while shift:
            high, low = pair_sum(high, low, pltpu.roll(high, shift, 1), pltpu.roll(low, shift, 1))
            shift //= 2
        gram = jnp.where(lane_of == row_of + start, high, gram)
        gram = jnp.where(lane_of == row_of + start + LOW, low, gram)
    gram_ref[...] = jnp.sum(gram, axis=0, keepdims=True)


def outer(place, totals, sides, one, two):
    tall = sides.shape[3]
    rows = tall - 16
    vmem = pl.BlockSpec(memory_space=pltpu.VMEM)
    return pl.pallas_call(
        outer_kernel,
        out_shape=[
            jax.ShapeDtypeStruct((5, 8, rows, BW), F32),
            jax.ShapeDtypeStruct((1, BW), F32),
        ],
        in_specs=[pl.BlockSpec(memory_space=pltpu.SMEM)] + [vmem] * 4,
        out_specs=[vmem, vmem],
        scratch_shapes=[pltpu.VMEM((2 * (NEAR + 1), tall, BW), F32)]
        + [pltpu.VMEM((2 * (NEAR + 1), tall + 16, BW), F32)] * 4,
        compiler_params=pltpu.CompilerParams(vmem_limit_bytes=VMEM_BYTES),
        name="outer",
    )(place, totals, sides, one, two)


def solved(high, low):
    g = {}
    for n, (a, b) in enumerate(PAIRS):
        g[a, b] = g[b, a] = (high[n], low[n])

    def times(factor, pair):
        return factor * pair[0], factor * pair[1]

    m = [[None] * 4 for _ in range(4)]
    for j in range(4):
        for i in range(j + 1):
            value = pair_sum(*times(MID, g[i, j]), *times(8.0 if j else 16.0, g[i, j + 1]))
            if j:
                value = pair_sum(*value, *times(0.5, g[i, j - 1]))
            m[i][j] = m[j][i] = two_sum(*value)

    work = [[m[i][j][0] for j in range(4)] for i in range(4)]
    inverse = []
    factor = [[None] * 4 for _ in range(4)]
    for k in range(4):
        pivot = work[k][k]
        inverse.append(jnp.where(pivot > 0.0, 1.0 / jnp.where(pivot > 0.0, pivot, 1.0), 0.0))
        for i in range(k + 1, 4):
            factor[i][k] = work[k][i] * inverse[k]
        for i in range(k + 1, 4):
            for j in range(i, 4):
                work[i][j] = work[i][j] - factor[i][k] * work[k][j]

    def solve(y):
        y = list(y)
        for k in range(4):
            for i in range(k + 1, 4):
                y[i] = y[i] - factor[i][k] * y[k]
        y = [y[k] * inverse[k] for k in range(4)]
        for k in range(3, -1, -1):
            for i in range(k):
                y[i] = y[i] - factor[k][i] * y[k]
        return y

    rest = [g[0, i] for i in range(4)]
    c = solve([pair[0] for pair in rest])
    found = [c]
    for _ in range(2):
        for i in range(4):
            for j in range(4):
                product, error = two_product(m[i][j][0], c[j])
                total, lost = two_sum(rest[i][0], -product)
                rest[i] = total, rest[i][1] + (lost - error - m[i][j][1] * c[j])
        rest = [two_sum(*pair) for pair in rest]
        c = solve([pair[0] for pair in rest])
        found.append(c)
    c = [found[0][k] + (found[1][k] + found[2][k]) for k in range(4)]
    r = [
        1.0 - (MID * c[0] + 0.5 * c[1]),
        -(16.0 * c[0] + MID * c[1] + 0.5 * c[2]),
        -(8.0 * c[1] + MID * c[2] + 0.5 * c[3]),
        -(8.0 * c[2] + MID * c[3]),
        -(8.0 * c[3]),
    ]
    return c, r


def combine_kernel(gram_ref, q_ref, sides_ref, x_ref, r_ref):
    rows = q_ref.shape[2]
    terms = [(gram_ref[n:n + 8], jnp.zeros((8, BW), F32)) for n in range(0, gram_ref.shape[0], 8)]
    while len(terms) > 1:
        terms = [pair_sum(*terms[n], *terms[n + 1]) for n in range(0, len(terms), 2)]
    high, low = all_rows(*terms[0])
    high, low = two_sum(high, low + pltpu.roll(high, BW - LOW, 1))
    first = high[0:1, 0:1]
    scale = jnp.where(first > 1e25, 2.0 ** -60, jnp.where(first < 1e-15, 2.0 ** 60, 1.0))
    lane = lax.broadcasted_iota(jnp.int32, (1, BW), 1)

    def pick(values, n):
        row = jnp.where(lane == n, values[0:1], 0.0)
        return scale * jnp.sum(row, axis=1, keepdims=True)

    count = range(len(PAIRS))
    c, r = solved([pick(high, n) for n in count], [pick(low, n) for n in count])
    c = [jnp.broadcast_to(value, (rows, BW)) for value in c]
    r = [jnp.broadcast_to(value, (rows, BW)) for value in r]
    for i in range(q_ref.shape[1]):
        if i < 4:
            q = [sides_ref[k, i] for k in range(5)]
        elif i >= BLOCKS - 4:
            q = [sides_ref[k, 4 + BLOCKS - 1 - i] for k in range(5)]
        else:
            q = [q_ref[k, i] for k in range(5)]
        columns = slice(i * BW, (i + 1) * BW)
        x_ref[:, columns] = sum(c[k] * q[k] for k in range(4))
        r_ref[:, columns] = sum(r[k] * q[k] for k in range(5))


def combine(gram, q, sides):
    _, blocks, rows, _ = q.shape
    out = jax.ShapeDtypeStruct((rows, blocks * BW), F32)
    vmem = pl.BlockSpec(memory_space=pltpu.VMEM)
    return pl.pallas_call(
        combine_kernel,
        out_shape=[out, out],
        in_specs=[vmem] * 3,
        out_specs=[vmem, vmem],
        compiler_params=pltpu.CompilerParams(vmem_limit_bytes=VMEM_BYTES),
        name="combine",
    )(gram, q, sides)


def body(piece_height, piece_weight, piece_column, piece_width):
    lon_count, lat_count = lax.axis_size("lon"), lax.axis_size("lat")
    rows = piece_height.shape[1]
    lon, lat = lax.axis_index("lon"), lax.axis_index("lat")
    place = jnp.stack([lat, jnp.int32(lat_count), lon]).astype(jnp.int32)

    packed = pack(piece_column, piece_width, piece_height, piece_weight, lon_count)
    got = lax.all_to_all(packed, "lon", split_axis=0, concat_axis=0, tiled=True)
    part = 2 * rows
    above = passed_along(got[:, :CAPACITY * part:part], "lat", -1)
    rhs, diag, *strips, blocks = gather(place, got, rows)
    gain, own_one, own_two, edge = finish(place, blocks, rhs, diag, *strips, above)

    one = swapped(own_one, "lat", 0, False)
    two = swapped(own_two, "lat", 1, False)
    first_edge = (BLOCKS - 1) * (1 - lon % 2)
    strips = []
    for start, block in ((0, first_edge), (1, BLOCKS - 1 - first_edge)):
        pick = lambda strip: lax.dynamic_index_in_dim(strip, block, 0, keepdims=False)
        message = jnp.concatenate([edge[start], pick(one), pick(two)], axis=0)
        strips.append(swapped(message, "lon", start, True))
    q, totals, near = inner(place, rhs, diag, gain, own_one, own_two, one, two)
    sides, gram = outer(place, totals, near, *strips)
    spread = jnp.broadcast_to(gram[None], (lon_count * lat_count, 1, BW))
    grams = lax.all_to_all(spread, ("lon", "lat"), split_axis=0, concat_axis=0, tiled=True)
    return tuple(combine(grams.reshape(lon_count * lat_count, BW), q, sides))


def solution(mesh):
    return jax.shard_map(
        body,
        mesh=mesh,
        in_specs=(P("lon", "lat", None), P("lon", "lat", None), P("lon"), P("lon")),
        out_specs=(P("lat", "lon"), P("lat", "lon")),
        check_vma=False,
    )
```

```python
import jax
import jax.numpy as jnp
from jax import lax
from jax.experimental import pallas as pl
from jax.experimental.pallas import tpu as pltpu
from jax.sharding import PartitionSpec as P

ROWS = 128
COLS_DEV = 4096
BW = 128
BLOCKS = COLS_DEV // BW
CAPACITY = 2

MU_DATA = 0.5
DAMPING = 0.5
RIDGE = 0.05

MID = 4.0
VMEM_BYTES = 40 * 1024 * 1024
PACK_VMEM_BYTES = 60 * 1024 * 1024
F32 = jnp.float32


def passed_along(block, axis, distance):
    devices = range(lax.axis_size(axis))
    route = [(i, i + distance) for i in devices if i + distance in devices]
    return lax.ppermute(block, axis, route)


def swapped(block, axis, start, around):
    count = lax.axis_size(axis)
    lows = range(start, count if around else count - 1, 2)
    pairs = [(low, (low + 1) % count) for low in lows]
    return lax.ppermute(block, axis, pairs + [(b, a) for a, b in pairs])


def pack_kernel(column_ref, width_ref, height_ref, weight_ref, out_ref, held_ref, facts_ref,
                count_ref, slot_ref, in_sem, out_sem, facts_sem):
    tiles, pieces = out_ref.shape[0], height_ref.shape[0]
    rows = height_ref.shape[1]
    part = 2 * rows
    batch = pieces // in_sem.shape[0]
    lane = lax.broadcasted_iota(jnp.int32, (1, BW), 1)

    def loads(g):
        part = pl.ds(g * batch, batch)
        sources = (height_ref, weight_ref)
        return [pltpu.make_async_copy(source.at[part], held_ref.at[part, pl.ds(n * rows, rows)],
                                      in_sem.at[g, n]) for n, source in enumerate(sources)]

    for g in range(in_sem.shape[0]):
        for load in loads(g):
            load.start()

    facts_ref[...] = jnp.zeros_like(facts_ref)

    @pl.loop(0, tiles, unroll=8)
    def _(t):
        count_ref[t] = 0

    @pl.loop(0, pieces, unroll=8)
    def _(p):
        tile = column_ref[p] // COLS_DEV
        block = column_ref[p] % COLS_DEV // BW
        slot = count_ref[tile]
        count_ref[tile] = slot + 1
        slot_ref[p] = slot
        at = 2 * slot
        facts = jnp.where(lane == at, block + 1, jnp.where(lane == at + 1, width_ref[p], 0))
        facts_ref[tile] += facts.astype(F32)

    facts = pltpu.make_async_copy(facts_ref, out_ref.at[:, CAPACITY * part], facts_sem)
    facts.start()
    for g in range(in_sem.shape[0]):
        for load in loads(g):
            load.wait()

        @pl.loop(g * batch, (g + 1) * batch, unroll=8)
        def _(p):
            target = out_ref.at[column_ref[p] // COLS_DEV, pl.ds(slot_ref[p] * part, part)]
            pltpu.make_async_copy(held_ref.at[p], target, out_sem).start()

    pltpu.make_async_copy(held_ref, out_ref.at[pl.ds(0, pieces), pl.ds(0, part)], out_sem).wait()
    facts.wait()


def pack(piece_column, piece_width, piece_height, piece_weight, tiles, batches=4):
    pieces, rows, _ = piece_height.shape
    tall = lambda array: array.reshape(pieces, rows, 1, BW)
    return pl.pallas_call(
        pack_kernel,
        out_shape=jax.ShapeDtypeStruct((tiles, CAPACITY * 2 * rows + 1, 1, BW), F32),
        in_specs=[
            pl.BlockSpec(memory_space=pltpu.SMEM),
            pl.BlockSpec(memory_space=pltpu.SMEM),
            pl.BlockSpec(memory_space=pl.ANY),
            pl.BlockSpec(memory_space=pl.ANY),
        ],
        out_specs=pl.BlockSpec(memory_space=pl.ANY),
        scratch_shapes=[
            pltpu.VMEM((pieces, 2 * rows, 1, BW), F32),
            pltpu.VMEM((tiles, 1, BW), F32),
            pltpu.SMEM((tiles,), jnp.int32),
            pltpu.SMEM((pieces,), jnp.int32),
            pltpu.SemaphoreType.DMA((batches, 2)),
            pltpu.SemaphoreType.DMA,
            pltpu.SemaphoreType.DMA,
        ],
        compiler_params=pltpu.CompilerParams(vmem_limit_bytes=PACK_VMEM_BYTES),
        name="pack",
    )(piece_column, piece_width, tall(piece_height), tall(piece_weight))


def gather_kernel(place_ref, got_ref, rows_ref, rhs_ref, diag_ref, one_ref, two_ref, last_ref,
                  inverse_ref, blocks_ref, total_ref, held_ref, facts_ref, facts_sem, sem):
    rows = rhs_ref.shape[1]
    lat, lat_count = place_ref[0], place_ref[1]
    part = 2 * rows
    message = CAPACITY * part + 1
    chunks, height, _ = held_ref.shape
    sources = height // message
    lane = lax.broadcasted_iota(jnp.int32, (rows, BW), 1)
    row = lax.broadcasted_iota(jnp.int32, (rows, BW), 0)

    def load(n):
        rows_of = rows_ref.at[pl.ds(n * height, height)]
        return pltpu.make_async_copy(rows_of, held_ref.at[n], sem.at[n])

    facts = pltpu.make_async_copy(got_ref.at[:, message - 1], facts_ref, facts_sem)
    facts.start()
    for n in range(chunks):
        load(n).start()
    total_ref[...] = jnp.zeros_like(total_ref)
    facts.wait()

    @pl.loop(0, chunks)
    def _(n):
        load(n).wait()
        for s in range(sources * CAPACITY):
            source, slot = s // CAPACITY, s % CAPACITY
            block = facts_ref[n * sources + source, 0, 2 * slot].astype(jnp.int32) - 1
            block = jnp.where(block < 0, BLOCKS, block)
            width = facts_ref[n * sources + source, 0, 2 * slot + 1].astype(jnp.int32)
            base = source * message
            start = base + slot * part
            height = held_ref[n, start:start + rows]
            weight = held_ref[n, start + rows:start + part]
            cell = jnp.where(lane < width, weight, 0.0)
            east = jnp.where(lane < width - 1, weight, 0.0)
            east_step = pltpu.roll(height, BW - 1, 1) - height
            raised = jnp.where(row == rows - 1, 0.0, pltpu.roll(height, rows - 1, 0))
            terms = (cell, cell * height, east, east * east_step, cell * (raised - height))
            for k, term in enumerate(terms):
                total_ref[block, k] += term
            last_ref[n * sources + source, slot] = cell[rows - 8:]
            blocks_ref[(n * sources + source) * CAPACITY + slot] = block

    last = (row == rows - 1) & (lat == lat_count - 1)
    first = (row == 0) & (lat == 0)
    sides = 4.0 - last.astype(F32) - first.astype(F32) + RIDGE
    row8 = row[:8]
    lat_even = lat % 2 == 0

    @pl.loop(0, BLOCKS, unroll=32)
    def _(i):
        cell, height = total_ref[i, 0], total_ref[i, 1]
        east = total_ref[i, 3] / (total_ref[i, 2] + DAMPING)
        north = jnp.where(last, 0.0, total_ref[i, 4] / (cell + DAMPING))
        south = jnp.where(row == 0, 0.0, pltpu.roll(north, 1, 0))
        rhs = MU_DATA * height - (east - pltpu.roll(east, 1, 1)) - (north - south)
        diag = MU_DATA * cell + sides
        rhs_ref[i] = rhs
        diag_ref[i] = diag
        top = pltpu.roll(diag[rows - 8:], 4, 0)
        top = jnp.where(row8 == 0, pltpu.roll(north[rows - 8:], 1, 0), top)
        up = jnp.where(row8 >= 4, rhs[rows - 8:], top)
        down = jnp.where(row8 >= 4, pltpu.roll(diag[:8], 4, 0), rhs[:8])
        one_ref[i] = jnp.where(lat_even, up, down)
        two_ref[i] = jnp.where(lat_even, down, up)
        inverse_ref[i] = 1.0 / (cell[rows - 8:] + DAMPING)


def gather(place, got, rows, chunks=2):
    tiles, message, _, _ = got.shape
    height = tiles * message // chunks
    field = (BLOCKS, rows, BW)
    strip = (BLOCKS, 8, BW)
    vmem = pl.BlockSpec(memory_space=pltpu.VMEM)
    shapes = (field, field, strip, strip, (tiles, CAPACITY, 8, BW), strip)
    return pl.pallas_call(
        gather_kernel,
        out_shape=[jax.ShapeDtypeStruct(s, F32) for s in shapes]
        + [jax.ShapeDtypeStruct((tiles * CAPACITY,), jnp.int32)],
        in_specs=[pl.BlockSpec(memory_space=pltpu.SMEM)] + [pl.BlockSpec(memory_space=pl.ANY)] * 2,
        out_specs=[vmem] * len(shapes) + [pl.BlockSpec(memory_space=pltpu.SMEM)],
        scratch_shapes=[
            pltpu.VMEM((BLOCKS + 1, 5, rows, BW), F32),
            pltpu.VMEM((chunks, height, BW), F32),
            pltpu.SMEM((tiles, 1, BW), F32),
            pltpu.SemaphoreType.DMA,
            pltpu.SemaphoreType.DMA((chunks,)),
        ],
        compiler_params=pltpu.CompilerParams(vmem_limit_bytes=VMEM_BYTES),
        name="gather",
    )(place, got, got.reshape(chunks * height, BW))


def finish_kernel(place_ref, blocks_ref, rhs_ref, diag_ref, part_one_ref, part_two_ref, last_ref,
                  inverse_ref, above_ref, gain_ref, one_ref, two_ref, edge_ref, *fix_refs):
    rows = rhs_ref.shape[1]
    tiles = last_ref.shape[0]
    lat, lon = place_ref[0], place_ref[2]
    lat_even = lat % 2 == 0
    row8 = lax.broadcasted_iota(jnp.int32, (8, BW), 0)
    for ref in fix_refs:
        ref[...] = jnp.zeros_like(ref)

    @pl.loop(0, tiles // 2, unroll=8)
    def _(n):
        for k, ref in enumerate(fix_refs):
            source, slot = 2 * n + k // CAPACITY, k % CAPACITY
            block = blocks_ref[source * CAPACITY + slot]
            ref[block] += last_ref[source, slot] * above_ref[source, slot]

    @pl.loop(0, BLOCKS, unroll=8)
    def _(i):
        gain = sum(ref[i] for ref in fix_refs) * inverse_ref[i]
        gain = jnp.where(row8 == 7, gain, 0.0)
        gain_ref[i] = gain
        up = pltpu.roll(gain, 1, 0) - gain
        one_ref[i] = part_one_ref[i] + jnp.where(lat_even, up, 0.0)
        two_ref[i] = part_two_ref[i] + jnp.where(lat_even, 0.0, up)

    first_edge = (BLOCKS - 1) * (1 - lon % 2)
    for side, block in ((0, first_edge), (1, BLOCKS - 1 - first_edge)):
        edge_ref[side, 0:rows - 8] = rhs_ref[block, 0:rows - 8]
        edge_ref[side, rows - 8:rows] = rhs_ref[block, rows - 8:rows] - gain_ref[block]
        edge_ref[side, rows:2 * rows] = diag_ref[block]
        edge_ref[side, 2 * rows:2 * rows + 8] = jnp.where(lat_even, one_ref[block], two_ref[block])


def finish(place, blocks, rhs, diag, *strips):
    rows = rhs.shape[1]
    strip = (BLOCKS, 8, BW)
    edge = (2, 2 * rows + 8, BW)
    vmem = pl.BlockSpec(memory_space=pltpu.VMEM)
    return pl.pallas_call(
        finish_kernel,
        out_shape=[jax.ShapeDtypeStruct(s, F32) for s in (strip, strip, strip, edge)],
        in_specs=[
            pl.BlockSpec(memory_space=pltpu.SMEM),
            pl.BlockSpec(memory_space=pltpu.SMEM),
        ] + [vmem] * 7,
        out_specs=[vmem] * 4,
        scratch_shapes=[pltpu.VMEM((BLOCKS + 1, 8, BW), F32)] * 4,
        compiler_params=pltpu.CompilerParams(vmem_limit_bytes=VMEM_BYTES),
        name="finish",
    )(place, blocks, rhs, diag, *strips)


def two_sum(a, b):
    total = a + b
    part = total - a
    return total, (a - (total - part)) + (b - part)


def pair_sum(high, low, other_high, other_low):
    total, error = two_sum(high, other_high)
    return total, low + other_low + error


def two_product(a, b):
    def split(x):
        big = 4097.0 * x
        top = big - (big - x)
        return top, x - top

    product = a * b
    (a_top, a_end), (b_top, b_end) = split(a), split(b)
    return product, ((a_top * b_top - product) + a_top * b_end + a_end * b_top) + a_end * b_end


def all_rows(high, low):
    for shift in (4, 2, 1):
        high, low = pair_sum(high, low, pltpu.roll(high, shift, 0), pltpu.roll(low, shift, 0))
    return high, low


PAIRS = [(i, j) for j in range(5) for i in range(min(j, 3) + 1)]
LOW = 16


class Field:
    def __init__(self, place_ref, rows, scale_ref, v_refs):
        self.rows, self.tall = rows, rows + 16
        self.scale_ref, self.v_refs = scale_ref, v_refs
        lat, lat_count = place_ref[0], place_ref[1]
        self.lat_even = lat % 2 == 0
        self.has_south, self.has_north = lat > 0, lat < lat_count - 1
        self.row = lax.broadcasted_iota(jnp.int32, (rows, BW), 0)
        self.lane = lax.broadcasted_iota(jnp.int32, (self.tall, BW), 1)

    def assemble(self, i, rhs, diag, up, one, two):
        row8 = self.row[:8]
        south = jnp.where(self.lat_even, two, one)
        north = jnp.where(self.lat_even, one, two)
        first = jnp.where(self.row == 0, south[0:1], 0.0) + rhs
        below = jnp.where(row8 >= 4, south, 0.0)
        above = jnp.where(row8 == 0, north + up, jnp.where(row8 < 4, north, 0.0))
        self.v_refs[0][i, 8:8 + self.tall] = jnp.concatenate([below, first, above], axis=0)
        diag = jnp.concatenate([pltpu.roll(south, 4, 0), diag, pltpu.roll(north, 4, 0)], axis=0)
        self.scale_ref[i] = (diag - MID) * 0.125

    def applied(self, k, i, left, right):
        ref, rows, tall = self.v_refs[k], self.rows, self.tall
        body = slice(8, 8 + tall)
        v = ref[i, body]
        west = pltpu.roll(jnp.where(self.lane == BW - 1, ref[left, body], v), 1, 1)
        east = pltpu.roll(jnp.where(self.lane == 0, ref[right, body], v), BW - 1, 1)
        south = ref[i, 7:7 + tall]
        north = ref[i, 9:9 + tall]
        image = self.scale_ref[i] * v - 0.125 * ((west + east) + (south + north))
        if k == 0:
            image = 0.5 * image
        else:
            image = image - 0.0625 * self.v_refs[k - 1][i, body]
        ends = (jnp.where(self.has_south, image[:8], 0.0), image[8:rows + 8],
                jnp.where(self.has_north, image[rows + 8:], 0.0))
        return jnp.concatenate(ends, axis=0)

    def step(self, k, i, left, right):
        self.v_refs[k + 1][i, 8:8 + self.tall] = self.applied(k, i, left, right)

    def products(self, i, left, right, q_ref, at, totals):
        rows = self.rows
        last = self.applied(3, i, left, right)[8:8 + rows]
        q = [self.v_refs[k][i, 16:16 + rows] for k in range(4)] + [last]
        for k in range(5):
            q_ref[k, at] = q[k]
        out = []
        for total, (a, b) in zip(totals, PAIRS):
            term = q[a] * q[b]
            out.append(total + sum(term[8 * n:8 * n + 8] for n in range(rows // 8)))
        return tuple(out)


NEAR = 6


def inner_kernel(place_ref, rhs_ref, diag_ref, gain_ref, own_one_ref, own_two_ref, one_ref,
                 two_ref, q_ref, totals_ref, sides_ref, scale_ref, *v_refs):
    rows = rhs_ref.shape[1]
    field = Field(place_ref, rows, scale_ref, v_refs)

    @pl.loop(0, BLOCKS, unroll=4)
    def _(i):
        up = jnp.where(field.lat_even, own_one_ref[i], own_two_ref[i])
        tail = rhs_ref[i, rows - 8:rows] - gain_ref[i]
        rhs = jnp.concatenate([rhs_ref[i, 0:rows - 8], tail], axis=0)
        field.assemble(i + 1, rhs, diag_ref[i], up, one_ref[i], two_ref[i])

    for k in range(3):
        @pl.loop(k + 2, BLOCKS - k, unroll=BLOCKS - 2 * k - 2)
        def _(i, k=k):
            field.step(k, i, i - 1, i + 1)

    def products(i, totals):
        return field.products(i, i - 1, i + 1, q_ref, i - 1, totals)

    zero = tuple(jnp.zeros((8, BW), F32) for _ in PAIRS)
    totals = lax.fori_loop(5, BLOCKS - 3, products, zero, unroll=8)
    for n, total in enumerate(totals):
        totals_ref[n] = total
    for k, ref in enumerate((scale_ref,) + v_refs):
        body = slice(8, 24 + rows) if k else slice(0, 16 + rows)
        for n in range(NEAR):
            sides_ref[0, k, n] = ref[n + 1, body]
            sides_ref[1, k, n] = ref[BLOCKS - n, body]


def inner(place, rhs, diag, *strips):
    rows = rhs.shape[1]
    vmem = pl.BlockSpec(memory_space=pltpu.VMEM)
    shapes = ((5, BLOCKS, rows, BW), (len(PAIRS), 8, BW), (2, 5, NEAR, rows + 16, BW))
    return pl.pallas_call(
        inner_kernel,
        out_shape=[jax.ShapeDtypeStruct(s, F32) for s in shapes],
        in_specs=[pl.BlockSpec(memory_space=pltpu.SMEM)] + [vmem] * 7,
        out_specs=[vmem] * 3,
        scratch_shapes=[pltpu.VMEM((BLOCKS + 2, rows + 16, BW), F32)]
        + [pltpu.VMEM((BLOCKS + 2, rows + 32, BW), F32)] * 4,
        compiler_params=pltpu.CompilerParams(vmem_limit_bytes=VMEM_BYTES),
        name="inner",
    )(place, rhs, diag, *strips)


def outer_kernel(place_ref, totals_ref, sides_ref, lon_one_ref, lon_two_ref, q_ref, gram_ref,
                 scale_ref, *v_refs):
    tall = sides_ref.shape[3]
    rows = tall - 16
    field = Field(place_ref, rows, scale_ref, v_refs)
    size = NEAR + 1
    for side in range(2):
        for n in range(NEAR):
            scale_ref[side * size + n + 1] = sides_ref[side, 0, n]
            for k in range(4):
                if n >= k:
                    v_refs[k][side * size + n + 1, 8:8 + tall] = sides_ref[side, k + 1, n]
    one_east = place_ref[2] % 2 == 0
    two = 2 * rows
    for side in range(2):
        first = lon_two_ref[...] if side == 0 else lon_one_ref[...]
        other = lon_one_ref[...] if side == 0 else lon_two_ref[...]
        strip = jnp.where(one_east, first, other)
        field.assemble(side * size, strip[0:rows], strip[rows:two], strip[two:two + 8],
                       strip[two + 8:two + 16], strip[two + 16:two + 24])

    def beside(side, n):
        inward, outward = side * size + n + 1, side * size + max(n - 1, 0)
        return (side * size + n,) + ((outward, inward) if side == 0 else (inward, outward))

    for k in range(3):
        for n in range(k + 2):
            for side in range(2):
                field.step(k, *beside(side, n))
    totals = tuple(totals_ref[n] for n in range(len(PAIRS)))
    for n in range(1, 5):
        for side in range(2):
            totals = field.products(*beside(side, n), q_ref, side * 4 + n - 1, totals)

    row_of = lax.broadcasted_iota(jnp.int32, (8, BW), 0)
    lane_of = lax.broadcasted_iota(jnp.int32, (8, BW), 1)
    gram = jnp.zeros((8, BW), F32)
    for start in range(0, len(PAIRS), 8):
        high = jnp.zeros((8, BW), F32)
        low = jnp.zeros((8, BW), F32)
        for n, total in enumerate(totals[start:start + 8]):
            pair = all_rows(total, jnp.zeros_like(total))
            high = jnp.where(row_of == n, pair[0], high)
            low = jnp.where(row_of == n, pair[1], low)
        shift = BW // 2
        while shift:
            high, low = pair_sum(high, low, pltpu.roll(high, shift, 1), pltpu.roll(low, shift, 1))
            shift //= 2
        gram = jnp.where(lane_of == row_of + start, high, gram)
        gram = jnp.where(lane_of == row_of + start + LOW, low, gram)
    gram_ref[...] = jnp.sum(gram, axis=0, keepdims=True)


def outer(place, totals, sides, one, two):
    tall = sides.shape[3]
    rows = tall - 16
    vmem = pl.BlockSpec(memory_space=pltpu.VMEM)
    return pl.pallas_call(
        outer_kernel,
        out_shape=[
            jax.ShapeDtypeStruct((5, 8, rows, BW), F32),
            jax.ShapeDtypeStruct((1, BW), F32),
        ],
        in_specs=[pl.BlockSpec(memory_space=pltpu.SMEM)] + [vmem] * 4,
        out_specs=[vmem, vmem],
        scratch_shapes=[pltpu.VMEM((2 * (NEAR + 1), tall, BW), F32)]
        + [pltpu.VMEM((2 * (NEAR + 1), tall + 16, BW), F32)] * 4,
        compiler_params=pltpu.CompilerParams(vmem_limit_bytes=VMEM_BYTES),
        name="outer",
    )(place, totals, sides, one, two)


def solved(high, low):
    g = {}
    for n, (a, b) in enumerate(PAIRS):
        g[a, b] = g[b, a] = (high[n], low[n])

    def times(factor, pair):
        return factor * pair[0], factor * pair[1]

    m = [[None] * 4 for _ in range(4)]
    for j in range(4):
        for i in range(j + 1):
            value = pair_sum(*times(MID, g[i, j]), *times(8.0 if j else 16.0, g[i, j + 1]))
            if j:
                value = pair_sum(*value, *times(0.5, g[i, j - 1]))
            m[i][j] = m[j][i] = two_sum(*value)

    work = [[m[i][j][0] for j in range(4)] for i in range(4)]
    inverse = []
    factor = [[None] * 4 for _ in range(4)]
    for k in range(4):
        pivot = work[k][k]
        inverse.append(jnp.where(pivot > 0.0, 1.0 / jnp.where(pivot > 0.0, pivot, 1.0), 0.0))
        for i in range(k + 1, 4):
            factor[i][k] = work[k][i] * inverse[k]
        for i in range(k + 1, 4):
            for j in range(i, 4):
                work[i][j] = work[i][j] - factor[i][k] * work[k][j]

    def solve(y):
        y = list(y)
        for k in range(4):
            for i in range(k + 1, 4):
                y[i] = y[i] - factor[i][k] * y[k]
        y = [y[k] * inverse[k] for k in range(4)]
        for k in range(3, -1, -1):
            for i in range(k):
                y[i] = y[i] - factor[k][i] * y[k]
        return y

    rest = [g[0, i] for i in range(4)]
    c = solve([pair[0] for pair in rest])
    found = [c]
    for _ in range(2):
        for i in range(4):
            for j in range(4):
                product, error = two_product(m[i][j][0], c[j])
                total, lost = two_sum(rest[i][0], -product)
                rest[i] = total, rest[i][1] + (lost - error - m[i][j][1] * c[j])
        rest = [two_sum(*pair) for pair in rest]
        c = solve([pair[0] for pair in rest])
        found.append(c)
    c = [found[0][k] + (found[1][k] + found[2][k]) for k in range(4)]
    r = [
        1.0 - (MID * c[0] + 0.5 * c[1]),
        -(16.0 * c[0] + MID * c[1] + 0.5 * c[2]),
        -(8.0 * c[1] + MID * c[2] + 0.5 * c[3]),
        -(8.0 * c[2] + MID * c[3]),
        -(8.0 * c[3]),
    ]
    return c, r


def combine_kernel(gram_ref, q_ref, sides_ref, x_out_ref, r_out_ref, x_ref, r_ref, sem):
    rows = q_ref.shape[2]
    terms = [(gram_ref[n:n + 8], jnp.zeros((8, BW), F32)) for n in range(0, gram_ref.shape[0], 8)]
    while len(terms) > 1:
        terms = [pair_sum(*terms[n], *terms[n + 1]) for n in range(0, len(terms), 2)]
    high, low = all_rows(*terms[0])
    high, low = two_sum(high, low + pltpu.roll(high, BW - LOW, 1))
    first = high[0:1, 0:1]
    scale = jnp.where(first > 1e25, 2.0 ** -60, jnp.where(first < 1e-15, 2.0 ** 60, 1.0))
    lane = lax.broadcasted_iota(jnp.int32, (1, BW), 1)

    def pick(values, n):
        row = jnp.where(lane == n, values[0:1], 0.0)
        return scale * jnp.sum(row, axis=1, keepdims=True)

    count = range(len(PAIRS))
    c, r = solved([pick(high, n) for n in count], [pick(low, n) for n in count])
    c = [jnp.broadcast_to(value, (rows, BW)) for value in c]
    r = [jnp.broadcast_to(value, (rows, BW)) for value in r]
    copies = []
    batch = BLOCKS // sem.shape[0]
    for i in range(BLOCKS):
        if i < 4:
            q = [sides_ref[k, i] for k in range(5)]
        elif i >= BLOCKS - 4:
            q = [sides_ref[k, 4 + BLOCKS - 1 - i] for k in range(5)]
        else:
            q = [q_ref[k, i] for k in range(5)]
        columns = slice(i * BW, (i + 1) * BW)
        x_ref[:, columns] = sum(c[k] * q[k] for k in range(4))
        r_ref[:, columns] = sum(r[k] * q[k] for k in range(5))
        if i % batch == batch - 1:
            done = pl.ds((i + 1 - batch) * BW, batch * BW)
            for n, (held, out) in enumerate(((x_ref, x_out_ref), (r_ref, r_out_ref))):
                copies.append(pltpu.make_async_copy(held.at[:, done], out.at[:, done],
                                                    sem.at[i // batch, n]))
                copies[-1].start()
    for copy in copies:
        copy.wait()


def combine(gram, q, sides):
    _, blocks, rows, _ = q.shape
    out = jax.ShapeDtypeStruct((rows, blocks * BW), F32)
    vmem = pl.BlockSpec(memory_space=pltpu.VMEM)
    return pl.pallas_call(
        combine_kernel,
        out_shape=[out, out],
        in_specs=[vmem] * 3,
        out_specs=[pl.BlockSpec(memory_space=pl.ANY)] * 2,
        scratch_shapes=[pltpu.VMEM(out.shape, F32)] * 2 + [pltpu.SemaphoreType.DMA((4, 2))],
        compiler_params=pltpu.CompilerParams(vmem_limit_bytes=VMEM_BYTES),
        name="combine",
    )(gram, q, sides)


def body(piece_height, piece_weight, piece_column, piece_width):
    lon_count, lat_count = lax.axis_size("lon"), lax.axis_size("lat")
    rows = piece_height.shape[1]
    lon, lat = lax.axis_index("lon"), lax.axis_index("lat")
    place = jnp.stack([lat, jnp.int32(lat_count), lon]).astype(jnp.int32)

    packed = pack(piece_column, piece_width, piece_height, piece_weight, lon_count)
    got = lax.all_to_all(packed, "lon", split_axis=0, concat_axis=0, tiled=True)
    part = 2 * rows
    above = passed_along(got[:, :CAPACITY * part:part], "lat", -1)
    rhs, diag, *strips, blocks = gather(place, got, rows)
    gain, own_one, own_two, edge = finish(place, blocks, rhs, diag, *strips, above)

    one = swapped(own_one, "lat", 0, False)
    two = swapped(own_two, "lat", 1, False)
    first_edge = (BLOCKS - 1) * (1 - lon % 2)
    strips = []
    for start, block in ((0, first_edge), (1, BLOCKS - 1 - first_edge)):
        pick = lambda strip: lax.dynamic_index_in_dim(strip, block, 0, keepdims=False)
        message = jnp.concatenate([edge[start], pick(one), pick(two)], axis=0)
        strips.append(swapped(message, "lon", start, True))
    q, totals, near = inner(place, rhs, diag, gain, own_one, own_two, one, two)
    sides, gram = outer(place, totals, near, *strips)
    spread = jnp.broadcast_to(gram[None], (lon_count * lat_count, 1, BW))
    grams = lax.all_to_all(spread, ("lon", "lat"), split_axis=0, concat_axis=0, tiled=True)
    return tuple(combine(grams.reshape(lon_count * lat_count, BW), q, sides))


def solution(mesh):
    return jax.shard_map(
        body,
        mesh=mesh,
        in_specs=(P("lon", "lat", None), P("lon", "lat", None), P("lon"), P("lon")),
        out_specs=(P("lat", "lon"), P("lat", "lon")),
        check_vma=False,
    )
```

```python
import jax
import jax.numpy as jnp
from jax import lax
from jax.experimental import pallas as pl
from jax.experimental.pallas import tpu as pltpu
from jax.sharding import PartitionSpec as P

ROWS = 128
COLS_DEV = 4096
BW = 128
BLOCKS = COLS_DEV // BW
CAPACITY = 2

MU_DATA = 0.5
DAMPING = 0.5
RIDGE = 0.05

MID = 4.0
VMEM_BYTES = 40 * 1024 * 1024
PACK_VMEM_BYTES = 60 * 1024 * 1024
F32 = jnp.float32


def passed_along(block, axis, distance):
    devices = range(lax.axis_size(axis))
    route = [(i, i + distance) for i in devices if i + distance in devices]
    return lax.ppermute(block, axis, route)


def swapped(block, axis, start, around):
    count = lax.axis_size(axis)
    lows = range(start, count if around else count - 1, 2)
    pairs = [(low, (low + 1) % count) for low in lows]
    return lax.ppermute(block, axis, pairs + [(b, a) for a, b in pairs])


def pack_kernel(column_ref, width_ref, height_ref, weight_ref, out_ref, held_ref, facts_ref,
                count_ref, slot_ref, in_sem, out_sem, facts_sem):
    tiles, pieces = out_ref.shape[0], height_ref.shape[0]
    rows = height_ref.shape[1]
    part = 2 * rows
    batch = pieces // in_sem.shape[0]
    lane = lax.broadcasted_iota(jnp.int32, (1, BW), 1)

    def loads(g):
        part = pl.ds(g * batch, batch)
        sources = (height_ref, weight_ref)
        return [pltpu.make_async_copy(source.at[part], held_ref.at[part, pl.ds(n * rows, rows)],
                                      in_sem.at[g, n]) for n, source in enumerate(sources)]

    for g in range(in_sem.shape[0]):
        for load in loads(g):
            load.start()

    facts_ref[...] = jnp.zeros_like(facts_ref)

    @pl.loop(0, tiles, unroll=8)
    def _(t):
        count_ref[t] = 0

    @pl.loop(0, pieces, unroll=8)
    def _(p):
        tile = column_ref[p] // COLS_DEV
        block = column_ref[p] % COLS_DEV // BW
        slot = count_ref[tile]
        count_ref[tile] = slot + 1
        slot_ref[p] = slot
        at = 2 * slot
        facts = jnp.where(lane == at, block + 1, jnp.where(lane == at + 1, width_ref[p], 0))
        facts_ref[tile] += facts.astype(F32)

    facts = pltpu.make_async_copy(facts_ref, out_ref.at[:, CAPACITY * part], facts_sem)
    facts.start()
    for g in range(in_sem.shape[0]):
        for load in loads(g):
            load.wait()

        @pl.loop(g * batch, (g + 1) * batch, unroll=8)
        def _(p):
            target = out_ref.at[column_ref[p] // COLS_DEV, pl.ds(slot_ref[p] * part, part)]
            pltpu.make_async_copy(held_ref.at[p], target, out_sem).start()

    pltpu.make_async_copy(held_ref, out_ref.at[pl.ds(0, pieces), pl.ds(0, part)], out_sem).wait()
    facts.wait()


def pack(piece_column, piece_width, piece_height, piece_weight, tiles, batches=4):
    pieces, rows, _ = piece_height.shape
    tall = lambda array: array.reshape(pieces, rows, 1, BW)
    return pl.pallas_call(
        pack_kernel,
        out_shape=jax.ShapeDtypeStruct((tiles, CAPACITY * 2 * rows + 1, 1, BW), F32),
        in_specs=[
            pl.BlockSpec(memory_space=pltpu.SMEM),
            pl.BlockSpec(memory_space=pltpu.SMEM),
            pl.BlockSpec(memory_space=pl.ANY),
            pl.BlockSpec(memory_space=pl.ANY),
        ],
        out_specs=pl.BlockSpec(memory_space=pl.ANY),
        scratch_shapes=[
            pltpu.VMEM((pieces, 2 * rows, 1, BW), F32),
            pltpu.VMEM((tiles, 1, BW), F32),
            pltpu.SMEM((tiles,), jnp.int32),
            pltpu.SMEM((pieces,), jnp.int32),
            pltpu.SemaphoreType.DMA((batches, 2)),
            pltpu.SemaphoreType.DMA,
            pltpu.SemaphoreType.DMA,
        ],
        compiler_params=pltpu.CompilerParams(vmem_limit_bytes=PACK_VMEM_BYTES),
        name="pack",
    )(piece_column, piece_width, tall(piece_height), tall(piece_weight))


def gather_kernel(place_ref, got_ref, rows_ref, rhs_ref, diag_ref, one_ref, two_ref, last_ref,
                  inverse_ref, blocks_ref, total_ref, held_ref, facts_ref, facts_sem, sem):
    rows = rhs_ref.shape[1]
    lat, lat_count = place_ref[0], place_ref[1]
    part = 2 * rows
    message = CAPACITY * part + 1
    chunks, height, _ = held_ref.shape
    sources = height // message
    lane = lax.broadcasted_iota(jnp.int32, (rows, BW), 1)
    row = lax.broadcasted_iota(jnp.int32, (rows, BW), 0)

    def load(n):
        rows_of = rows_ref.at[pl.ds(n * height, height)]
        return pltpu.make_async_copy(rows_of, held_ref.at[n], sem.at[n])

    facts = pltpu.make_async_copy(got_ref.at[:, message - 1], facts_ref, facts_sem)
    facts.start()
    for n in range(chunks):
        load(n).start()
    total_ref[...] = jnp.zeros_like(total_ref)
    facts.wait()

    @pl.loop(0, chunks)
    def _(n):
        load(n).wait()
        for s in range(sources * CAPACITY):
            source, slot = s // CAPACITY, s % CAPACITY
            block = facts_ref[n * sources + source, 0, 2 * slot].astype(jnp.int32) - 1
            block = jnp.where(block < 0, BLOCKS, block)
            width = facts_ref[n * sources + source, 0, 2 * slot + 1].astype(jnp.int32)
            base = source * message
            start = base + slot * part
            height = held_ref[n, start:start + rows]
            weight = held_ref[n, start + rows:start + part]
            cell = jnp.where(lane < width, weight, 0.0)
            east = jnp.where(lane < width - 1, weight, 0.0)
            east_step = pltpu.roll(height, BW - 1, 1) - height
            raised = jnp.where(row == rows - 1, 0.0, pltpu.roll(height, rows - 1, 0))
            terms = (cell, cell * height, east, east * east_step, cell * (raised - height))
            for k, term in enumerate(terms):
                total_ref[block, k] += term
            last_ref[n * sources + source, slot] = cell[rows - 8:]
            blocks_ref[(n * sources + source) * CAPACITY + slot] = block

    last = (row == rows - 1) & (lat == lat_count - 1)
    first = (row == 0) & (lat == 0)
    sides = 4.0 - last.astype(F32) - first.astype(F32) + RIDGE
    row8 = row[:8]
    lat_even = lat % 2 == 0

    @pl.loop(0, BLOCKS, unroll=32)
    def _(i):
        cell, height = total_ref[i, 0], total_ref[i, 1]
        east = total_ref[i, 3] / (total_ref[i, 2] + DAMPING)
        north = jnp.where(last, 0.0, total_ref[i, 4] / (cell + DAMPING))
        south = jnp.where(row == 0, 0.0, pltpu.roll(north, 1, 0))
        rhs = MU_DATA * height - (east - pltpu.roll(east, 1, 1)) - (north - south)
        diag = MU_DATA * cell + sides
        rhs_ref[i] = rhs
        diag_ref[i] = diag
        top = pltpu.roll(diag[rows - 8:], 4, 0)
        top = jnp.where(row8 == 0, pltpu.roll(north[rows - 8:], 1, 0), top)
        up = jnp.where(row8 >= 4, rhs[rows - 8:], top)
        down = jnp.where(row8 >= 4, pltpu.roll(diag[:8], 4, 0), rhs[:8])
        one_ref[i] = jnp.where(lat_even, up, down)
        two_ref[i] = jnp.where(lat_even, down, up)
        inverse_ref[i] = 1.0 / (cell[rows - 8:] + DAMPING)


def gather(place, got, rows, chunks=4):
    tiles, message, _, _ = got.shape
    height = tiles * message // chunks
    field = (BLOCKS, rows, BW)
    strip = (BLOCKS, 8, BW)
    vmem = pl.BlockSpec(memory_space=pltpu.VMEM)
    shapes = (field, field, strip, strip, (tiles, CAPACITY, 8, BW), strip)
    return pl.pallas_call(
        gather_kernel,
        out_shape=[jax.ShapeDtypeStruct(s, F32) for s in shapes]
        + [jax.ShapeDtypeStruct((tiles * CAPACITY,), jnp.int32)],
        in_specs=[pl.BlockSpec(memory_space=pltpu.SMEM)] + [pl.BlockSpec(memory_space=pl.ANY)] * 2,
        out_specs=[vmem] * len(shapes) + [pl.BlockSpec(memory_space=pltpu.SMEM)],
        scratch_shapes=[
            pltpu.VMEM((BLOCKS + 1, 5, rows, BW), F32),
            pltpu.VMEM((chunks, height, BW), F32),
            pltpu.SMEM((tiles, 1, BW), F32),
            pltpu.SemaphoreType.DMA,
            pltpu.SemaphoreType.DMA((chunks,)),
        ],
        compiler_params=pltpu.CompilerParams(vmem_limit_bytes=VMEM_BYTES),
        name="gather",
    )(place, got, got.reshape(chunks * height, BW))


def finish_kernel(place_ref, blocks_ref, rhs_ref, diag_ref, part_one_ref, part_two_ref, last_ref,
                  inverse_ref, above_ref, gain_ref, one_ref, two_ref, edge_ref, *fix_refs):
    rows = rhs_ref.shape[1]
    tiles = last_ref.shape[0]
    lat, lon = place_ref[0], place_ref[2]
    lat_even = lat % 2 == 0
    row8 = lax.broadcasted_iota(jnp.int32, (8, BW), 0)
    for ref in fix_refs:
        ref[...] = jnp.zeros_like(ref)

    @pl.loop(0, tiles // 2, unroll=8)
    def _(n):
        for k, ref in enumerate(fix_refs):
            source, slot = 2 * n + k // CAPACITY, k % CAPACITY
            block = blocks_ref[source * CAPACITY + slot]
            ref[block] += last_ref[source, slot] * above_ref[source, slot]

    @pl.loop(0, BLOCKS, unroll=8)
    def _(i):
        gain = sum(ref[i] for ref in fix_refs) * inverse_ref[i]
        gain = jnp.where(row8 == 7, gain, 0.0)
        gain_ref[i] = gain
        up = pltpu.roll(gain, 1, 0) - gain
        one_ref[i] = part_one_ref[i] + jnp.where(lat_even, up, 0.0)
        two_ref[i] = part_two_ref[i] + jnp.where(lat_even, 0.0, up)

    first_edge = (BLOCKS - 1) * (1 - lon % 2)
    for side, block in ((0, first_edge), (1, BLOCKS - 1 - first_edge)):
        edge_ref[side, 0:rows - 8] = rhs_ref[block, 0:rows - 8]
        edge_ref[side, rows - 8:rows] = rhs_ref[block, rows - 8:rows] - gain_ref[block]
        edge_ref[side, rows:2 * rows] = diag_ref[block]
        edge_ref[side, 2 * rows:2 * rows + 8] = jnp.where(lat_even, one_ref[block], two_ref[block])


def finish(place, blocks, rhs, diag, *strips):
    rows = rhs.shape[1]
    strip = (BLOCKS, 8, BW)
    edge = (2, 2 * rows + 8, BW)
    vmem = pl.BlockSpec(memory_space=pltpu.VMEM)
    return pl.pallas_call(
        finish_kernel,
        out_shape=[jax.ShapeDtypeStruct(s, F32) for s in (strip, strip, strip, edge)],
        in_specs=[
            pl.BlockSpec(memory_space=pltpu.SMEM),
            pl.BlockSpec(memory_space=pltpu.SMEM),
        ] + [vmem] * 7,
        out_specs=[vmem] * 4,
        scratch_shapes=[pltpu.VMEM((BLOCKS + 1, 8, BW), F32)] * 4,
        compiler_params=pltpu.CompilerParams(vmem_limit_bytes=VMEM_BYTES),
        name="finish",
    )(place, blocks, rhs, diag, *strips)


def two_sum(a, b):
    total = a + b
    part = total - a
    return total, (a - (total - part)) + (b - part)


def pair_sum(high, low, other_high, other_low):
    total, error = two_sum(high, other_high)
    return total, low + other_low + error


def two_product(a, b):
    def split(x):
        big = 4097.0 * x
        top = big - (big - x)
        return top, x - top

    product = a * b
    (a_top, a_end), (b_top, b_end) = split(a), split(b)
    return product, ((a_top * b_top - product) + a_top * b_end + a_end * b_top) + a_end * b_end


def all_rows(high, low):
    for shift in (4, 2, 1):
        high, low = pair_sum(high, low, pltpu.roll(high, shift, 0), pltpu.roll(low, shift, 0))
    return high, low


PAIRS = [(i, j) for j in range(5) for i in range(min(j, 3) + 1)]
LOW = 16


class Field:
    def __init__(self, place_ref, rows, scale_ref, v_refs):
        self.rows, self.tall = rows, rows + 16
        self.scale_ref, self.v_refs = scale_ref, v_refs
        lat, lat_count = place_ref[0], place_ref[1]
        self.lat_even = lat % 2 == 0
        self.has_south, self.has_north = lat > 0, lat < lat_count - 1
        self.row = lax.broadcasted_iota(jnp.int32, (rows, BW), 0)
        self.lane = lax.broadcasted_iota(jnp.int32, (self.tall, BW), 1)

    def assemble(self, i, rhs, diag, up, one, two):
        row8 = self.row[:8]
        south = jnp.where(self.lat_even, two, one)
        north = jnp.where(self.lat_even, one, two)
        first = jnp.where(self.row == 0, south[0:1], 0.0) + rhs
        below = jnp.where(row8 >= 4, south, 0.0)
        above = jnp.where(row8 == 0, north + up, jnp.where(row8 < 4, north, 0.0))
        self.v_refs[0][i, 8:8 + self.tall] = jnp.concatenate([below, first, above], axis=0)
        diag = jnp.concatenate([pltpu.roll(south, 4, 0), diag, pltpu.roll(north, 4, 0)], axis=0)
        self.scale_ref[i] = (diag - MID) * 0.125

    def applied(self, k, i, left, right):
        ref, rows, tall = self.v_refs[k], self.rows, self.tall
        body = slice(8, 8 + tall)
        v = ref[i, body]
        west = pltpu.roll(jnp.where(self.lane == BW - 1, ref[left, body], v), 1, 1)
        east = pltpu.roll(jnp.where(self.lane == 0, ref[right, body], v), BW - 1, 1)
        south = ref[i, 7:7 + tall]
        north = ref[i, 9:9 + tall]
        image = self.scale_ref[i] * v - 0.125 * ((west + east) + (south + north))
        if k == 0:
            image = 0.5 * image
        else:
            image = image - 0.0625 * self.v_refs[k - 1][i, body]
        ends = (jnp.where(self.has_south, image[:8], 0.0), image[8:rows + 8],
                jnp.where(self.has_north, image[rows + 8:], 0.0))
        return jnp.concatenate(ends, axis=0)

    def step(self, k, i, left, right):
        self.v_refs[k + 1][i, 8:8 + self.tall] = self.applied(k, i, left, right)

    def products(self, i, left, right, q_ref, at, totals):
        rows = self.rows
        last = self.applied(3, i, left, right)[8:8 + rows]
        q = [self.v_refs[k][i, 16:16 + rows] for k in range(4)] + [last]
        for k in range(5):
            q_ref[k, at] = q[k]
        out = []
        for total, (a, b) in zip(totals, PAIRS):
            term = q[a] * q[b]
            out.append(total + sum(term[8 * n:8 * n + 8] for n in range(rows // 8)))
        return tuple(out)


NEAR = 6


def inner_kernel(place_ref, rhs_ref, diag_ref, gain_ref, own_one_ref, own_two_ref, one_ref,
                 two_ref, q_ref, totals_ref, sides_ref, scale_ref, *v_refs):
    rows = rhs_ref.shape[1]
    field = Field(place_ref, rows, scale_ref, v_refs)

    @pl.loop(0, BLOCKS, unroll=4)
    def _(i):
        up = jnp.where(field.lat_even, own_one_ref[i], own_two_ref[i])
        tail = rhs_ref[i, rows - 8:rows] - gain_ref[i]
        rhs = jnp.concatenate([rhs_ref[i, 0:rows - 8], tail], axis=0)
        field.assemble(i + 1, rhs, diag_ref[i], up, one_ref[i], two_ref[i])

    for k in range(3):
        @pl.loop(k + 2, BLOCKS - k, unroll=BLOCKS - 2 * k - 2)
        def _(i, k=k):
            field.step(k, i, i - 1, i + 1)

    def products(i, totals):
        return field.products(i, i - 1, i + 1, q_ref, i - 1, totals)

    zero = tuple(jnp.zeros((8, BW), F32) for _ in PAIRS)
    totals = lax.fori_loop(5, BLOCKS - 3, products, zero, unroll=8)
    for n, total in enumerate(totals):
        totals_ref[n] = total
    for k, ref in enumerate((scale_ref,) + v_refs):
        body = slice(8, 24 + rows) if k else slice(0, 16 + rows)
        for n in range(NEAR):
            sides_ref[0, k, n] = ref[n + 1, body]
            sides_ref[1, k, n] = ref[BLOCKS - n, body]


def inner(place, rhs, diag, *strips):
    rows = rhs.shape[1]
    vmem = pl.BlockSpec(memory_space=pltpu.VMEM)
    shapes = ((5, BLOCKS, rows, BW), (len(PAIRS), 8, BW), (2, 5, NEAR, rows + 16, BW))
    return pl.pallas_call(
        inner_kernel,
        out_shape=[jax.ShapeDtypeStruct(s, F32) for s in shapes],
        in_specs=[pl.BlockSpec(memory_space=pltpu.SMEM)] + [vmem] * 7,
        out_specs=[vmem] * 3,
        scratch_shapes=[pltpu.VMEM((BLOCKS + 2, rows + 16, BW), F32)]
        + [pltpu.VMEM((BLOCKS + 2, rows + 32, BW), F32)] * 4,
        compiler_params=pltpu.CompilerParams(vmem_limit_bytes=VMEM_BYTES),
        name="inner",
    )(place, rhs, diag, *strips)


def outer_kernel(place_ref, totals_ref, sides_ref, lon_one_ref, lon_two_ref, q_ref, gram_ref,
                 scale_ref, *v_refs):
    tall = sides_ref.shape[3]
    rows = tall - 16
    field = Field(place_ref, rows, scale_ref, v_refs)
    size = NEAR + 1
    for side in range(2):
        for n in range(NEAR):
            scale_ref[side * size + n + 1] = sides_ref[side, 0, n]
            for k in range(4):
                if n >= k:
                    v_refs[k][side * size + n + 1, 8:8 + tall] = sides_ref[side, k + 1, n]
    one_east = place_ref[2] % 2 == 0
    two = 2 * rows
    for side in range(2):
        first = lon_two_ref[...] if side == 0 else lon_one_ref[...]
        other = lon_one_ref[...] if side == 0 else lon_two_ref[...]
        strip = jnp.where(one_east, first, other)
        field.assemble(side * size, strip[0:rows], strip[rows:two], strip[two:two + 8],
                       strip[two + 8:two + 16], strip[two + 16:two + 24])

    def beside(side, n):
        inward, outward = side * size + n + 1, side * size + max(n - 1, 0)
        return (side * size + n,) + ((outward, inward) if side == 0 else (inward, outward))

    for k in range(3):
        for n in range(k + 2):
            for side in range(2):
                field.step(k, *beside(side, n))
    totals = tuple(totals_ref[n] for n in range(len(PAIRS)))
    for n in range(1, 5):
        for side in range(2):
            totals = field.products(*beside(side, n), q_ref, side * 4 + n - 1, totals)

    row_of = lax.broadcasted_iota(jnp.int32, (8, BW), 0)
    lane_of = lax.broadcasted_iota(jnp.int32, (8, BW), 1)
    gram = jnp.zeros((8, BW), F32)
    for start in range(0, len(PAIRS), 8):
        high = jnp.zeros((8, BW), F32)
        low = jnp.zeros((8, BW), F32)
        for n, total in enumerate(totals[start:start + 8]):
            pair = all_rows(total, jnp.zeros_like(total))
            high = jnp.where(row_of == n, pair[0], high)
            low = jnp.where(row_of == n, pair[1], low)
        shift = BW // 2
        while shift:
            high, low = pair_sum(high, low, pltpu.roll(high, shift, 1), pltpu.roll(low, shift, 1))
            shift //= 2
        gram = jnp.where(lane_of == row_of + start, high, gram)
        gram = jnp.where(lane_of == row_of + start + LOW, low, gram)
    gram_ref[...] = jnp.sum(gram, axis=0, keepdims=True)


def outer(place, totals, sides, one, two):
    tall = sides.shape[3]
    rows = tall - 16
    vmem = pl.BlockSpec(memory_space=pltpu.VMEM)
    return pl.pallas_call(
        outer_kernel,
        out_shape=[
            jax.ShapeDtypeStruct((5, 8, rows, BW), F32),
            jax.ShapeDtypeStruct((1, BW), F32),
        ],
        in_specs=[pl.BlockSpec(memory_space=pltpu.SMEM)] + [vmem] * 4,
        out_specs=[vmem, vmem],
        scratch_shapes=[pltpu.VMEM((2 * (NEAR + 1), tall, BW), F32)]
        + [pltpu.VMEM((2 * (NEAR + 1), tall + 16, BW), F32)] * 4,
        compiler_params=pltpu.CompilerParams(vmem_limit_bytes=VMEM_BYTES),
        name="outer",
    )(place, totals, sides, one, two)


def solved(high, low):
    g = {}
    for n, (a, b) in enumerate(PAIRS):
        g[a, b] = g[b, a] = (high[n], low[n])

    def times(factor, pair):
        return factor * pair[0], factor * pair[1]

    m = [[None] * 4 for _ in range(4)]
    for j in range(4):
        for i in range(j + 1):
            value = pair_sum(*times(MID, g[i, j]), *times(8.0 if j else 16.0, g[i, j + 1]))
            if j:
                value = pair_sum(*value, *times(0.5, g[i, j - 1]))
            m[i][j] = m[j][i] = two_sum(*value)

    work = [[m[i][j][0] for j in range(4)] for i in range(4)]
    inverse = []
    factor = [[None] * 4 for _ in range(4)]
    for k in range(4):
        pivot = work[k][k]
        inverse.append(jnp.where(pivot > 0.0, 1.0 / jnp.where(pivot > 0.0, pivot, 1.0), 0.0))
        for i in range(k + 1, 4):
            factor[i][k] = work[k][i] * inverse[k]
        for i in range(k + 1, 4):
            for j in range(i, 4):
                work[i][j] = work[i][j] - factor[i][k] * work[k][j]

    def solve(y):
        y = list(y)
        for k in range(4):
            for i in range(k + 1, 4):
                y[i] = y[i] - factor[i][k] * y[k]
        y = [y[k] * inverse[k] for k in range(4)]
        for k in range(3, -1, -1):
            for i in range(k):
                y[i] = y[i] - factor[k][i] * y[k]
        return y

    rest = [g[0, i] for i in range(4)]
    c = solve([pair[0] for pair in rest])
    found = [c]
    for _ in range(2):
        for i in range(4):
            for j in range(4):
                product, error = two_product(m[i][j][0], c[j])
                total, lost = two_sum(rest[i][0], -product)
                rest[i] = total, rest[i][1] + (lost - error - m[i][j][1] * c[j])
        rest = [two_sum(*pair) for pair in rest]
        c = solve([pair[0] for pair in rest])
        found.append(c)
    c = [found[0][k] + (found[1][k] + found[2][k]) for k in range(4)]
    r = [
        1.0 - (MID * c[0] + 0.5 * c[1]),
        -(16.0 * c[0] + MID * c[1] + 0.5 * c[2]),
        -(8.0 * c[1] + MID * c[2] + 0.5 * c[3]),
        -(8.0 * c[2] + MID * c[3]),
        -(8.0 * c[3]),
    ]
    return c, r


def combine_kernel(gram_ref, q_ref, sides_ref, x_out_ref, r_out_ref, x_ref, r_ref, sem):
    rows = q_ref.shape[2]
    terms = [(gram_ref[n:n + 8], jnp.zeros((8, BW), F32)) for n in range(0, gram_ref.shape[0], 8)]
    while len(terms) > 1:
        terms = [pair_sum(*terms[n], *terms[n + 1]) for n in range(0, len(terms), 2)]
    high, low = all_rows(*terms[0])
    high, low = two_sum(high, low + pltpu.roll(high, BW - LOW, 1))
    first = high[0:1, 0:1]
    scale = jnp.where(first > 1e25, 2.0 ** -60, jnp.where(first < 1e-15, 2.0 ** 60, 1.0))
    lane = lax.broadcasted_iota(jnp.int32, (1, BW), 1)

    def pick(values, n):
        row = jnp.where(lane == n, values[0:1], 0.0)
        return scale * jnp.sum(row, axis=1, keepdims=True)

    count = range(len(PAIRS))
    c, r = solved([pick(high, n) for n in count], [pick(low, n) for n in count])
    c = [jnp.broadcast_to(value, (rows, BW)) for value in c]
    r = [jnp.broadcast_to(value, (rows, BW)) for value in r]
    copies = []
    batch = BLOCKS // sem.shape[0]
    for i in range(BLOCKS):
        if i < 4:
            q = [sides_ref[k, i] for k in range(5)]
        elif i >= BLOCKS - 4:
            q = [sides_ref[k, 4 + BLOCKS - 1 - i] for k in range(5)]
        else:
            q = [q_ref[k, i] for k in range(5)]
        columns = slice(i * BW, (i + 1) * BW)
        x_ref[:, columns] = sum(c[k] * q[k] for k in range(4))
        r_ref[:, columns] = sum(r[k] * q[k] for k in range(5))
        if i % batch == batch - 1:
            done = pl.ds((i + 1 - batch) * BW, batch * BW)
            for n, (held, out) in enumerate(((x_ref, x_out_ref), (r_ref, r_out_ref))):
                copies.append(pltpu.make_async_copy(held.at[:, done], out.at[:, done],
                                                    sem.at[i // batch, n]))
                copies[-1].start()
    for copy in copies:
        copy.wait()


def combine(gram, q, sides):
    _, blocks, rows, _ = q.shape
    out = jax.ShapeDtypeStruct((rows, blocks * BW), F32)
    vmem = pl.BlockSpec(memory_space=pltpu.VMEM)
    return pl.pallas_call(
        combine_kernel,
        out_shape=[out, out],
        in_specs=[vmem] * 3,
        out_specs=[pl.BlockSpec(memory_space=pl.ANY)] * 2,
        scratch_shapes=[pltpu.VMEM(out.shape, F32)] * 2 + [pltpu.SemaphoreType.DMA((4, 2))],
        compiler_params=pltpu.CompilerParams(vmem_limit_bytes=VMEM_BYTES),
        name="combine",
    )(gram, q, sides)


def body(piece_height, piece_weight, piece_column, piece_width):
    lon_count, lat_count = lax.axis_size("lon"), lax.axis_size("lat")
    rows = piece_height.shape[1]
    lon, lat = lax.axis_index("lon"), lax.axis_index("lat")
    place = jnp.stack([lat, jnp.int32(lat_count), lon]).astype(jnp.int32)

    packed = pack(piece_column, piece_width, piece_height, piece_weight, lon_count)
    got = lax.all_to_all(packed, "lon", split_axis=0, concat_axis=0, tiled=True)
    part = 2 * rows
    above = passed_along(got[:, :CAPACITY * part:part], "lat", -1)
    rhs, diag, *strips, blocks = gather(place, got, rows)
    gain, own_one, own_two, edge = finish(place, blocks, rhs, diag, *strips, above)

    one = swapped(own_one, "lat", 0, False)
    two = swapped(own_two, "lat", 1, False)
    first_edge = (BLOCKS - 1) * (1 - lon % 2)
    strips = []
    for start, block in ((0, first_edge), (1, BLOCKS - 1 - first_edge)):
        pick = lambda strip: lax.dynamic_index_in_dim(strip, block, 0, keepdims=False)
        message = jnp.concatenate([edge[start], pick(one), pick(two)], axis=0)
        strips.append(swapped(message, "lon", start, True))
    q, totals, near = inner(place, rhs, diag, gain, own_one, own_two, one, two)
    sides, gram = outer(place, totals, near, *strips)
    spread = jnp.broadcast_to(gram[None], (lon_count * lat_count, 1, BW))
    grams = lax.all_to_all(spread, ("lat", "lon"), split_axis=0, concat_axis=0, tiled=True)
    return tuple(combine(grams.reshape(lon_count * lat_count, BW), q, sides))


def solution(mesh):
    return jax.shard_map(
        body,
        mesh=mesh,
        in_specs=(P("lon", "lat", None), P("lon", "lat", None), P("lon"), P("lon")),
        out_specs=(P("lat", "lon"), P("lat", "lon")),
        check_vma=False,
    )
```

```python
import jax
import jax.numpy as jnp
from jax import lax
from jax.experimental import pallas as pl
from jax.experimental.pallas import tpu as pltpu
from jax.sharding import PartitionSpec as P

ROWS = 128
COLS_DEV = 4096
BW = 128
BLOCKS = COLS_DEV // BW
CAPACITY = 2

MU_DATA = 0.5
DAMPING = 0.5
RIDGE = 0.05

MID = 4.0
VMEM_BYTES = 40 * 1024 * 1024
PACK_VMEM_BYTES = 60 * 1024 * 1024
F32 = jnp.float32


def passed_along(block, axis, distance):
    devices = range(lax.axis_size(axis))
    route = [(i, i + distance) for i in devices if i + distance in devices]
    return lax.ppermute(block, axis, route)


def swapped(block, axis, start, around):
    count = lax.axis_size(axis)
    lows = range(start, count if around else count - 1, 2)
    pairs = [(low, (low + 1) % count) for low in lows]
    return lax.ppermute(block, axis, pairs + [(b, a) for a, b in pairs])


def pack_kernel(column_ref, width_ref, height_ref, weight_ref, out_ref, held_ref, facts_ref,
                count_ref, slot_ref, in_sem, out_sem, facts_sem):
    tiles, pieces = out_ref.shape[0], height_ref.shape[0]
    rows = height_ref.shape[1]
    part = 2 * rows
    batch = pieces // in_sem.shape[0]
    lane = lax.broadcasted_iota(jnp.int32, (1, BW), 1)

    def loads(g):
        part = pl.ds(g * batch, batch)
        sources = (height_ref, weight_ref)
        return [pltpu.make_async_copy(source.at[part], held_ref.at[part, pl.ds(n * rows, rows)],
                                      in_sem.at[g, n]) for n, source in enumerate(sources)]

    for g in range(in_sem.shape[0]):
        for load in loads(g):
            load.start()

    facts_ref[...] = jnp.zeros_like(facts_ref)

    @pl.loop(0, tiles, unroll=8)
    def _(t):
        count_ref[t] = 0

    @pl.loop(0, pieces, unroll=8)
    def _(p):
        tile = column_ref[p] // COLS_DEV
        block = column_ref[p] % COLS_DEV // BW
        slot = count_ref[tile]
        count_ref[tile] = slot + 1
        slot_ref[p] = slot
        at = 2 * slot
        facts = jnp.where(lane == at, block + 1, jnp.where(lane == at + 1, width_ref[p], 0))
        facts_ref[tile] += facts.astype(F32)

    facts = pltpu.make_async_copy(facts_ref, out_ref.at[:, CAPACITY * part], facts_sem)
    facts.start()
    for g in range(in_sem.shape[0]):
        for load in loads(g):
            load.wait()

        @pl.loop(g * batch, (g + 1) * batch, unroll=8)
        def _(p):
            target = out_ref.at[column_ref[p] // COLS_DEV, pl.ds(slot_ref[p] * part, part)]
            pltpu.make_async_copy(held_ref.at[p], target, out_sem).start()

    pltpu.make_async_copy(held_ref, out_ref.at[pl.ds(0, pieces), pl.ds(0, part)], out_sem).wait()
    facts.wait()


def pack(piece_column, piece_width, piece_height, piece_weight, tiles, batches=4):
    pieces, rows, _ = piece_height.shape
    tall = lambda array: array.reshape(pieces, rows, 1, BW)
    return pl.pallas_call(
        pack_kernel,
        out_shape=jax.ShapeDtypeStruct((tiles, CAPACITY * 2 * rows + 1, 1, BW), F32),
        in_specs=[
            pl.BlockSpec(memory_space=pltpu.SMEM),
            pl.BlockSpec(memory_space=pltpu.SMEM),
            pl.BlockSpec(memory_space=pl.ANY),
            pl.BlockSpec(memory_space=pl.ANY),
        ],
        out_specs=pl.BlockSpec(memory_space=pl.ANY),
        scratch_shapes=[
            pltpu.VMEM((pieces, 2 * rows, 1, BW), F32),
            pltpu.VMEM((tiles, 1, BW), F32),
            pltpu.SMEM((tiles,), jnp.int32),
            pltpu.SMEM((pieces,), jnp.int32),
            pltpu.SemaphoreType.DMA((batches, 2)),
            pltpu.SemaphoreType.DMA,
            pltpu.SemaphoreType.DMA,
        ],
        compiler_params=pltpu.CompilerParams(vmem_limit_bytes=PACK_VMEM_BYTES),
        name="pack",
    )(piece_column, piece_width, tall(piece_height), tall(piece_weight))


def gather_kernel(place_ref, got_ref, rows_ref, rhs_ref, diag_ref, one_ref, two_ref, last_ref,
                  inverse_ref, blocks_ref, total_ref, held_ref, facts_ref, facts_sem, sem):
    rows = rhs_ref.shape[1]
    lat, lat_count = place_ref[0], place_ref[1]
    part = 2 * rows
    message = CAPACITY * part + 1
    chunks, height, _ = held_ref.shape
    sources = height // message
    lane = lax.broadcasted_iota(jnp.int32, (rows, BW), 1)
    row = lax.broadcasted_iota(jnp.int32, (rows, BW), 0)

    def load(n):
        rows_of = rows_ref.at[pl.ds(n * height, height)]
        return pltpu.make_async_copy(rows_of, held_ref.at[n], sem.at[n])

    facts = pltpu.make_async_copy(got_ref.at[:, message - 1], facts_ref, facts_sem)
    facts.start()
    for n in range(chunks):
        load(n).start()
    total_ref[...] = jnp.zeros_like(total_ref)
    facts.wait()

    @pl.loop(0, chunks)
    def _(n):
        load(n).wait()
        for s in range(sources * CAPACITY):
            source, slot = s // CAPACITY, s % CAPACITY
            block = facts_ref[n * sources + source, 0, 2 * slot].astype(jnp.int32) - 1
            block = jnp.where(block < 0, BLOCKS, block)
            width = facts_ref[n * sources + source, 0, 2 * slot + 1].astype(jnp.int32)
            base = source * message
            start = base + slot * part
            height = held_ref[n, start:start + rows]
            weight = held_ref[n, start + rows:start + part]
            cell = jnp.where(lane < width, weight, 0.0)
            east = jnp.where(lane < width - 1, weight, 0.0)
            east_step = pltpu.roll(height, BW - 1, 1) - height
            raised = jnp.where(row == rows - 1, 0.0, pltpu.roll(height, rows - 1, 0))
            terms = (cell, cell * height, east, east * east_step, cell * (raised - height))
            for k, term in enumerate(terms):
                total_ref[block, k] += term
            last_ref[n * sources + source, slot] = cell[rows - 8:]
            blocks_ref[(n * sources + source) * CAPACITY + slot] = block

    last = (row == rows - 1) & (lat == lat_count - 1)
    first = (row == 0) & (lat == 0)
    sides = 4.0 - last.astype(F32) - first.astype(F32) + RIDGE
    row8 = row[:8]
    lat_even = lat % 2 == 0

    @pl.loop(0, BLOCKS, unroll=32)
    def _(i):
        cell, height = total_ref[i, 0], total_ref[i, 1]
        east = total_ref[i, 3] / (total_ref[i, 2] + DAMPING)
        north = jnp.where(last, 0.0, total_ref[i, 4] / (cell + DAMPING))
        south = jnp.where(row == 0, 0.0, pltpu.roll(north, 1, 0))
        rhs = MU_DATA * height - (east - pltpu.roll(east, 1, 1)) - (north - south)
        diag = MU_DATA * cell + sides
        rhs_ref[i] = rhs
        diag_ref[i] = diag
        top = pltpu.roll(diag[rows - 8:], 4, 0)
        top = jnp.where(row8 == 0, pltpu.roll(north[rows - 8:], 1, 0), top)
        up = jnp.where(row8 >= 4, rhs[rows - 8:], top)
        down = jnp.where(row8 >= 4, pltpu.roll(diag[:8], 4, 0), rhs[:8])
        one_ref[i] = jnp.where(lat_even, up, down)
        two_ref[i] = jnp.where(lat_even, down, up)
        inverse_ref[i] = 1.0 / (cell[rows - 8:] + DAMPING)


def gather(place, got, rows, chunks=2):
    tiles, message, _, _ = got.shape
    height = tiles * message // chunks
    field = (BLOCKS, rows, BW)
    strip = (BLOCKS, 8, BW)
    vmem = pl.BlockSpec(memory_space=pltpu.VMEM)
    shapes = (field, field, strip, strip, (tiles, CAPACITY, 8, BW), strip)
    return pl.pallas_call(
        gather_kernel,
        out_shape=[jax.ShapeDtypeStruct(s, F32) for s in shapes]
        + [jax.ShapeDtypeStruct((tiles * CAPACITY,), jnp.int32)],
        in_specs=[pl.BlockSpec(memory_space=pltpu.SMEM)] + [pl.BlockSpec(memory_space=pl.ANY)] * 2,
        out_specs=[vmem] * len(shapes) + [pl.BlockSpec(memory_space=pltpu.SMEM)],
        scratch_shapes=[
            pltpu.VMEM((BLOCKS + 1, 5, rows, BW), F32),
            pltpu.VMEM((chunks, height, BW), F32),
            pltpu.SMEM((tiles, 1, BW), F32),
            pltpu.SemaphoreType.DMA,
            pltpu.SemaphoreType.DMA((chunks,)),
        ],
        compiler_params=pltpu.CompilerParams(vmem_limit_bytes=VMEM_BYTES),
        name="gather",
    )(place, got, got.reshape(chunks * height, BW))


def finish_kernel(place_ref, blocks_ref, rhs_ref, diag_ref, part_one_ref, part_two_ref, last_ref,
                  inverse_ref, above_ref, gain_ref, one_ref, two_ref, edge_ref, *fix_refs):
    rows = rhs_ref.shape[1]
    tiles = last_ref.shape[0]
    lat, lon = place_ref[0], place_ref[2]
    lat_even = lat % 2 == 0
    row8 = lax.broadcasted_iota(jnp.int32, (8, BW), 0)
    for ref in fix_refs:
        ref[...] = jnp.zeros_like(ref)

    @pl.loop(0, tiles // 2, unroll=8)
    def _(n):
        for k, ref in enumerate(fix_refs):
            source, slot = 2 * n + k // CAPACITY, k % CAPACITY
            block = blocks_ref[source * CAPACITY + slot]
            ref[block] += last_ref[source, slot] * above_ref[source, slot]

    @pl.loop(0, BLOCKS, unroll=8)
    def _(i):
        gain = sum(ref[i] for ref in fix_refs) * inverse_ref[i]
        gain = jnp.where(row8 == 7, gain, 0.0)
        gain_ref[i] = gain
        up = pltpu.roll(gain, 1, 0) - gain
        one_ref[i] = part_one_ref[i] + jnp.where(lat_even, up, 0.0)
        two_ref[i] = part_two_ref[i] + jnp.where(lat_even, 0.0, up)

    first_edge = (BLOCKS - 1) * (1 - lon % 2)
    for side, block in ((0, first_edge), (1, BLOCKS - 1 - first_edge)):
        edge_ref[side, 0:rows - 8] = rhs_ref[block, 0:rows - 8]
        edge_ref[side, rows - 8:rows] = rhs_ref[block, rows - 8:rows] - gain_ref[block]
        edge_ref[side, rows:2 * rows] = diag_ref[block]
        edge_ref[side, 2 * rows:2 * rows + 8] = jnp.where(lat_even, one_ref[block], two_ref[block])


def finish(place, blocks, rhs, diag, *strips):
    rows = rhs.shape[1]
    strip = (BLOCKS, 8, BW)
    edge = (2, 2 * rows + 8, BW)
    vmem = pl.BlockSpec(memory_space=pltpu.VMEM)
    return pl.pallas_call(
        finish_kernel,
        out_shape=[jax.ShapeDtypeStruct(s, F32) for s in (strip, strip, strip, edge)],
        in_specs=[
            pl.BlockSpec(memory_space=pltpu.SMEM),
            pl.BlockSpec(memory_space=pltpu.SMEM),
        ] + [vmem] * 7,
        out_specs=[vmem] * 4,
        scratch_shapes=[pltpu.VMEM((BLOCKS + 1, 8, BW), F32)] * 4,
        compiler_params=pltpu.CompilerParams(vmem_limit_bytes=VMEM_BYTES),
        name="finish",
    )(place, blocks, rhs, diag, *strips)


def two_sum(a, b):
    total = a + b
    part = total - a
    return total, (a - (total - part)) + (b - part)


def pair_sum(high, low, other_high, other_low):
    total, error = two_sum(high, other_high)
    return total, low + other_low + error


def two_product(a, b):
    def split(x):
        big = 4097.0 * x
        top = big - (big - x)
        return top, x - top

    product = a * b
    (a_top, a_end), (b_top, b_end) = split(a), split(b)
    return product, ((a_top * b_top - product) + a_top * b_end + a_end * b_top) + a_end * b_end


def all_rows(high, low):
    for shift in (4, 2, 1):
        high, low = pair_sum(high, low, pltpu.roll(high, shift, 0), pltpu.roll(low, shift, 0))
    return high, low


PAIRS = [(i, j) for j in range(5) for i in range(min(j, 3) + 1)]
LOW = 16


class Field:
    def __init__(self, place_ref, rows, scale_ref, v_refs):
        self.rows, self.tall = rows, rows + 16
        self.scale_ref, self.v_refs = scale_ref, v_refs
        lat, lat_count = place_ref[0], place_ref[1]
        self.lat_even = lat % 2 == 0
        self.has_south, self.has_north = lat > 0, lat < lat_count - 1
        self.row = lax.broadcasted_iota(jnp.int32, (rows, BW), 0)
        self.lane = lax.broadcasted_iota(jnp.int32, (self.tall, BW), 1)

    def assemble(self, i, rhs, diag, up, one, two):
        row8 = self.row[:8]
        south = jnp.where(self.lat_even, two, one)
        north = jnp.where(self.lat_even, one, two)
        first = jnp.where(self.row == 0, south[0:1], 0.0) + rhs
        below = jnp.where(row8 >= 4, south, 0.0)
        above = jnp.where(row8 == 0, north + up, jnp.where(row8 < 4, north, 0.0))
        self.v_refs[0][i, 8:8 + self.tall] = jnp.concatenate([below, first, above], axis=0)
        diag = jnp.concatenate([pltpu.roll(south, 4, 0), diag, pltpu.roll(north, 4, 0)], axis=0)
        self.scale_ref[i] = (diag - MID) * 0.125

    def applied(self, k, i, left, right):
        ref, rows, tall = self.v_refs[k], self.rows, self.tall
        body = slice(8, 8 + tall)
        v = ref[i, body]
        west = pltpu.roll(jnp.where(self.lane == BW - 1, ref[left, body], v), 1, 1)
        east = pltpu.roll(jnp.where(self.lane == 0, ref[right, body], v), BW - 1, 1)
        south = ref[i, 7:7 + tall]
        north = ref[i, 9:9 + tall]
        image = self.scale_ref[i] * v - 0.125 * ((west + east) + (south + north))
        if k == 0:
            image = 0.5 * image
        else:
            image = image - 0.0625 * self.v_refs[k - 1][i, body]
        ends = (jnp.where(self.has_south, image[:8], 0.0), image[8:rows + 8],
                jnp.where(self.has_north, image[rows + 8:], 0.0))
        return jnp.concatenate(ends, axis=0)

    def step(self, k, i, left, right):
        self.v_refs[k + 1][i, 8:8 + self.tall] = self.applied(k, i, left, right)

    def products(self, i, left, right, q_ref, at, totals):
        rows = self.rows
        last = self.applied(3, i, left, right)[8:8 + rows]
        q = [self.v_refs[k][i, 16:16 + rows] for k in range(4)] + [last]
        for k in range(5):
            q_ref[k, at] = q[k]
        out = []
        for total, (a, b) in zip(totals, PAIRS):
            term = q[a] * q[b]
            out.append(total + sum(term[8 * n:8 * n + 8] for n in range(rows // 8)))
        return tuple(out)


NEAR = 6


def inner_kernel(place_ref, rhs_ref, diag_ref, gain_ref, own_one_ref, own_two_ref, one_ref,
                 two_ref, q_ref, totals_ref, sides_ref, scale_ref, *v_refs):
    rows = rhs_ref.shape[1]
    field = Field(place_ref, rows, scale_ref, v_refs)

    @pl.loop(0, BLOCKS, unroll=4)
    def _(i):
        up = jnp.where(field.lat_even, own_one_ref[i], own_two_ref[i])
        tail = rhs_ref[i, rows - 8:rows] - gain_ref[i]
        rhs = jnp.concatenate([rhs_ref[i, 0:rows - 8], tail], axis=0)
        field.assemble(i + 1, rhs, diag_ref[i], up, one_ref[i], two_ref[i])

    for k in range(3):
        @pl.loop(k + 2, BLOCKS - k, unroll=BLOCKS - 2 * k - 2)
        def _(i, k=k):
            field.step(k, i, i - 1, i + 1)

    def products(i, totals):
        return field.products(i, i - 1, i + 1, q_ref, i - 1, totals)

    zero = tuple(jnp.zeros((8, BW), F32) for _ in PAIRS)
    totals = lax.fori_loop(5, BLOCKS - 3, products, zero, unroll=8)
    for n, total in enumerate(totals):
        totals_ref[n] = total
    for k, ref in enumerate((scale_ref,) + v_refs):
        body = slice(8, 24 + rows) if k else slice(0, 16 + rows)
        for n in range(NEAR):
            sides_ref[0, k, n] = ref[n + 1, body]
            sides_ref[1, k, n] = ref[BLOCKS - n, body]


def inner(place, rhs, diag, *strips):
    rows = rhs.shape[1]
    vmem = pl.BlockSpec(memory_space=pltpu.VMEM)
    shapes = ((5, BLOCKS, rows, BW), (len(PAIRS), 8, BW), (2, 5, NEAR, rows + 16, BW))
    return pl.pallas_call(
        inner_kernel,
        out_shape=[jax.ShapeDtypeStruct(s, F32) for s in shapes],
        in_specs=[pl.BlockSpec(memory_space=pltpu.SMEM)] + [vmem] * 7,
        out_specs=[vmem] * 3,
        scratch_shapes=[pltpu.VMEM((BLOCKS + 2, rows + 16, BW), F32)]
        + [pltpu.VMEM((BLOCKS + 2, rows + 32, BW), F32)] * 4,
        compiler_params=pltpu.CompilerParams(vmem_limit_bytes=VMEM_BYTES),
        name="inner",
    )(place, rhs, diag, *strips)


def outer_kernel(place_ref, totals_ref, sides_ref, lon_one_ref, lon_two_ref, q_ref, gram_ref,
                 scale_ref, *v_refs):
    tall = sides_ref.shape[3]
    rows = tall - 16
    field = Field(place_ref, rows, scale_ref, v_refs)
    size = NEAR + 1
    for side in range(2):
        for n in range(NEAR):
            scale_ref[side * size + n + 1] = sides_ref[side, 0, n]
            for k in range(4):
                if n >= k:
                    v_refs[k][side * size + n + 1, 8:8 + tall] = sides_ref[side, k + 1, n]
    one_east = place_ref[2] % 2 == 0
    two = 2 * rows
    for side in range(2):
        first = lon_two_ref[...] if side == 0 else lon_one_ref[...]
        other = lon_one_ref[...] if side == 0 else lon_two_ref[...]
        strip = jnp.where(one_east, first, other)
        field.assemble(side * size, strip[0:rows], strip[rows:two], strip[two:two + 8],
                       strip[two + 8:two + 16], strip[two + 16:two + 24])

    def beside(side, n):
        inward, outward = side * size + n + 1, side * size + max(n - 1, 0)
        return (side * size + n,) + ((outward, inward) if side == 0 else (inward, outward))

    for k in range(3):
        for n in range(k + 2):
            for side in range(2):
                field.step(k, *beside(side, n))
    totals = tuple(totals_ref[n] for n in range(len(PAIRS)))
    for n in range(1, 5):
        for side in range(2):
            totals = field.products(*beside(side, n), q_ref, side * 4 + n - 1, totals)

    row_of = lax.broadcasted_iota(jnp.int32, (8, BW), 0)
    lane_of = lax.broadcasted_iota(jnp.int32, (8, BW), 1)
    gram = jnp.zeros((8, BW), F32)
    for start in range(0, len(PAIRS), 8):
        high = jnp.zeros((8, BW), F32)
        low = jnp.zeros((8, BW), F32)
        for n, total in enumerate(totals[start:start + 8]):
            pair = all_rows(total, jnp.zeros_like(total))
            high = jnp.where(row_of == n, pair[0], high)
            low = jnp.where(row_of == n, pair[1], low)
        shift = BW // 2
        while shift:
            high, low = pair_sum(high, low, pltpu.roll(high, shift, 1), pltpu.roll(low, shift, 1))
            shift //= 2
        gram = jnp.where(lane_of == row_of + start, high, gram)
        gram = jnp.where(lane_of == row_of + start + LOW, low, gram)
    row = jnp.sum(gram, axis=0, keepdims=True)
    gram_ref[...] = jnp.broadcast_to(row[None], gram_ref.shape)


def outer(place, totals, sides, one, two, devices):
    tall = sides.shape[3]
    rows = tall - 16
    vmem = pl.BlockSpec(memory_space=pltpu.VMEM)
    return pl.pallas_call(
        outer_kernel,
        out_shape=[
            jax.ShapeDtypeStruct((5, 8, rows, BW), F32),
            jax.ShapeDtypeStruct((devices, 1, BW), F32),
        ],
        in_specs=[pl.BlockSpec(memory_space=pltpu.SMEM)] + [vmem] * 4,
        out_specs=[vmem, vmem],
        scratch_shapes=[pltpu.VMEM((2 * (NEAR + 1), tall, BW), F32)]
        + [pltpu.VMEM((2 * (NEAR + 1), tall + 16, BW), F32)] * 4,
        compiler_params=pltpu.CompilerParams(vmem_limit_bytes=VMEM_BYTES),
        name="outer",
    )(place, totals, sides, one, two)


def solved(high, low):
    g = {}
    for n, (a, b) in enumerate(PAIRS):
        g[a, b] = g[b, a] = (high[n], low[n])

    def times(factor, pair):
        return factor * pair[0], factor * pair[1]

    m = [[None] * 4 for _ in range(4)]
    for j in range(4):
        for i in range(j + 1):
            value = pair_sum(*times(MID, g[i, j]), *times(8.0 if j else 16.0, g[i, j + 1]))
            if j:
                value = pair_sum(*value, *times(0.5, g[i, j - 1]))
            m[i][j] = m[j][i] = two_sum(*value)

    work = [[m[i][j][0] for j in range(4)] for i in range(4)]
    inverse = []
    factor = [[None] * 4 for _ in range(4)]
    for k in range(4):
        pivot = work[k][k]
        inverse.append(jnp.where(pivot > 0.0, 1.0 / jnp.where(pivot > 0.0, pivot, 1.0), 0.0))
        for i in range(k + 1, 4):
            factor[i][k] = work[k][i] * inverse[k]
        for i in range(k + 1, 4):
            for j in range(i, 4):
                work[i][j] = work[i][j] - factor[i][k] * work[k][j]

    def solve(y):
        y = list(y)
        for k in range(4):
            for i in range(k + 1, 4):
                y[i] = y[i] - factor[i][k] * y[k]
        y = [y[k] * inverse[k] for k in range(4)]
        for k in range(3, -1, -1):
            for i in range(k):
                y[i] = y[i] - factor[k][i] * y[k]
        return y

    rest = [g[0, i] for i in range(4)]
    c = solve([pair[0] for pair in rest])
    found = [c]
    for _ in range(2):
        for i in range(4):
            for j in range(4):
                product, error = two_product(m[i][j][0], c[j])
                total, lost = two_sum(rest[i][0], -product)
                rest[i] = total, rest[i][1] + (lost - error - m[i][j][1] * c[j])
        rest = [two_sum(*pair) for pair in rest]
        c = solve([pair[0] for pair in rest])
        found.append(c)
    c = [found[0][k] + (found[1][k] + found[2][k]) for k in range(4)]
    r = [
        1.0 - (MID * c[0] + 0.5 * c[1]),
        -(16.0 * c[0] + MID * c[1] + 0.5 * c[2]),
        -(8.0 * c[1] + MID * c[2] + 0.5 * c[3]),
        -(8.0 * c[2] + MID * c[3]),
        -(8.0 * c[3]),
    ]
    return c, r


def combine_kernel(gram_ref, q_ref, sides_ref, x_out_ref, r_out_ref, x_ref, r_ref, sem):
    rows = q_ref.shape[2]
    terms = [(gram_ref[n:n + 8], jnp.zeros((8, BW), F32)) for n in range(0, gram_ref.shape[0], 8)]
    while len(terms) > 1:
        terms = [pair_sum(*terms[n], *terms[n + 1]) for n in range(0, len(terms), 2)]
    high, low = all_rows(*terms[0])
    high, low = two_sum(high, low + pltpu.roll(high, BW - LOW, 1))
    first = high[0:1, 0:1]
    scale = jnp.where(first > 1e25, 2.0 ** -60, jnp.where(first < 1e-15, 2.0 ** 60, 1.0))
    lane = lax.broadcasted_iota(jnp.int32, (1, BW), 1)

    def pick(values, n):
        row = jnp.where(lane == n, values[0:1], 0.0)
        return scale * jnp.sum(row, axis=1, keepdims=True)

    count = range(len(PAIRS))
    c, r = solved([pick(high, n) for n in count], [pick(low, n) for n in count])
    c = [jnp.broadcast_to(value, (rows, BW)) for value in c]
    r = [jnp.broadcast_to(value, (rows, BW)) for value in r]
    copies = []
    batch = BLOCKS // sem.shape[0]
    for i in range(BLOCKS):
        if i < 4:
            q = [sides_ref[k, i] for k in range(5)]
        elif i >= BLOCKS - 4:
            q = [sides_ref[k, 4 + BLOCKS - 1 - i] for k in range(5)]
        else:
            q = [q_ref[k, i] for k in range(5)]
        columns = slice(i * BW, (i + 1) * BW)
        x_ref[:, columns] = sum(c[k] * q[k] for k in range(4))
        r_ref[:, columns] = sum(r[k] * q[k] for k in range(5))
        if i % batch == batch - 1:
            done = pl.ds((i + 1 - batch) * BW, batch * BW)
            for n, (held, out) in enumerate(((x_ref, x_out_ref), (r_ref, r_out_ref))):
                copies.append(pltpu.make_async_copy(held.at[:, done], out.at[:, done],
                                                    sem.at[i // batch, n]))
                copies[-1].start()
    for copy in copies:
        copy.wait()


def combine(gram, q, sides):
    _, blocks, rows, _ = q.shape
    out = jax.ShapeDtypeStruct((rows, blocks * BW), F32)
    vmem = pl.BlockSpec(memory_space=pltpu.VMEM)
    return pl.pallas_call(
        combine_kernel,
        out_shape=[out, out],
        in_specs=[vmem] * 3,
        out_specs=[pl.BlockSpec(memory_space=pl.ANY)] * 2,
        scratch_shapes=[pltpu.VMEM(out.shape, F32)] * 2 + [pltpu.SemaphoreType.DMA((4, 2))],
        compiler_params=pltpu.CompilerParams(vmem_limit_bytes=VMEM_BYTES),
        name="combine",
    )(gram, q, sides)


def body(piece_height, piece_weight, piece_column, piece_width):
    lon_count, lat_count = lax.axis_size("lon"), lax.axis_size("lat")
    rows = piece_height.shape[1]
    lon, lat = lax.axis_index("lon"), lax.axis_index("lat")
    place = jnp.stack([lat, jnp.int32(lat_count), lon]).astype(jnp.int32)

    packed = pack(piece_column, piece_width, piece_height, piece_weight, lon_count)
    got = lax.all_to_all(packed, "lon", split_axis=0, concat_axis=0, tiled=True)
    part = 2 * rows
    above = passed_along(got[:, :CAPACITY * part:part], "lat", -1)
    rhs, diag, *strips, blocks = gather(place, got, rows)
    gain, own_one, own_two, edge = finish(place, blocks, rhs, diag, *strips, above)

    one = swapped(own_one, "lat", 0, False)
    two = swapped(own_two, "lat", 1, False)
    first_edge = (BLOCKS - 1) * (1 - lon % 2)
    strips = []
    for start, block in ((0, first_edge), (1, BLOCKS - 1 - first_edge)):
        pick = lambda strip: lax.dynamic_index_in_dim(strip, block, 0, keepdims=False)
        message = jnp.concatenate([edge[start], pick(one), pick(two)], axis=0)
        strips.append(swapped(message, "lon", start, True))
    q, totals, near = inner(place, rhs, diag, gain, own_one, own_two, one, two)
    sides, spread = outer(place, totals, near, *strips, lon_count * lat_count)
    grams = lax.all_to_all(spread, ("lon", "lat"), split_axis=0, concat_axis=0, tiled=True)
    return tuple(combine(grams.reshape(lon_count * lat_count, BW), q, sides))


def solution(mesh):
    return jax.shard_map(
        body,
        mesh=mesh,
        in_specs=(P("lon", "lat", None), P("lon", "lat", None), P("lon"), P("lon")),
        out_specs=(P("lat", "lon"), P("lat", "lon")),
        check_vma=False,
    )
```

```python
import jax
import jax.numpy as jnp
from jax import lax
from jax.experimental import pallas as pl
from jax.experimental.pallas import tpu as pltpu
from jax.sharding import PartitionSpec as P

ROWS = 128
COLS_DEV = 4096
BW = 128
BLOCKS = COLS_DEV // BW
CAPACITY = 2

MU_DATA = 0.5
DAMPING = 0.5
RIDGE = 0.05

MID = 4.0
VMEM_BYTES = 40 * 1024 * 1024
PACK_VMEM_BYTES = 60 * 1024 * 1024
F32 = jnp.float32


def passed_along(block, axis, distance):
    devices = range(lax.axis_size(axis))
    route = [(i, i + distance) for i in devices if i + distance in devices]
    return lax.ppermute(block, axis, route)


def swapped(block, axis, start, around):
    count = lax.axis_size(axis)
    lows = range(start, count if around else count - 1, 2)
    pairs = [(low, (low + 1) % count) for low in lows]
    return lax.ppermute(block, axis, pairs + [(b, a) for a, b in pairs])


def pack_kernel(column_ref, width_ref, height_ref, weight_ref, out_ref, held_ref, facts_ref,
                count_ref, slot_ref, in_sem, out_sem, facts_sem):
    tiles, pieces = out_ref.shape[0], height_ref.shape[0]
    rows = height_ref.shape[1]
    part = 2 * rows
    batch = pieces // in_sem.shape[0]
    lane = lax.broadcasted_iota(jnp.int32, (1, BW), 1)

    def loads(g):
        part = pl.ds(g * batch, batch)
        sources = (height_ref, weight_ref)
        return [pltpu.make_async_copy(source.at[part], held_ref.at[part, pl.ds(n * rows, rows)],
                                      in_sem.at[g, n]) for n, source in enumerate(sources)]

    for g in range(in_sem.shape[0]):
        for load in loads(g):
            load.start()

    facts_ref[...] = jnp.zeros_like(facts_ref)

    @pl.loop(0, tiles, unroll=8)
    def _(t):
        count_ref[t] = 0

    @pl.loop(0, pieces, unroll=32)
    def _(p):
        tile = column_ref[p] // COLS_DEV
        block = column_ref[p] % COLS_DEV // BW
        slot = count_ref[tile]
        count_ref[tile] = slot + 1
        slot_ref[p] = slot
        at = 2 * slot
        facts = jnp.where(lane == at, block + 1, jnp.where(lane == at + 1, width_ref[p], 0))
        facts_ref[tile] += facts.astype(F32)

    facts = pltpu.make_async_copy(facts_ref, out_ref.at[:, CAPACITY * part], facts_sem)
    facts.start()
    for g in range(in_sem.shape[0]):
        for load in loads(g):
            load.wait()

        @pl.loop(g * batch, (g + 1) * batch, unroll=8)
        def _(p):
            target = out_ref.at[column_ref[p] // COLS_DEV, pl.ds(slot_ref[p] * part, part)]
            pltpu.make_async_copy(held_ref.at[p], target, out_sem).start()

    pltpu.make_async_copy(held_ref, out_ref.at[pl.ds(0, pieces), pl.ds(0, part)], out_sem).wait()
    facts.wait()


def pack(piece_column, piece_width, piece_height, piece_weight, tiles, batches=4):
    pieces, rows, _ = piece_height.shape
    tall = lambda array: array.reshape(pieces, rows, 1, BW)
    return pl.pallas_call(
        pack_kernel,
        out_shape=jax.ShapeDtypeStruct((tiles, CAPACITY * 2 * rows + 1, 1, BW), F32),
        in_specs=[
            pl.BlockSpec(memory_space=pltpu.SMEM),
            pl.BlockSpec(memory_space=pltpu.SMEM),
            pl.BlockSpec(memory_space=pl.ANY),
            pl.BlockSpec(memory_space=pl.ANY),
        ],
        out_specs=pl.BlockSpec(memory_space=pl.ANY),
        scratch_shapes=[
            pltpu.VMEM((pieces, 2 * rows, 1, BW), F32),
            pltpu.VMEM((tiles, 1, BW), F32),
            pltpu.SMEM((tiles,), jnp.int32),
            pltpu.SMEM((pieces,), jnp.int32),
            pltpu.SemaphoreType.DMA((batches, 2)),
            pltpu.SemaphoreType.DMA,
            pltpu.SemaphoreType.DMA,
        ],
        compiler_params=pltpu.CompilerParams(vmem_limit_bytes=PACK_VMEM_BYTES),
        name="pack",
    )(piece_column, piece_width, tall(piece_height), tall(piece_weight))


def gather_kernel(place_ref, got_ref, rows_ref, rhs_ref, diag_ref, one_ref, two_ref, last_ref,
                  inverse_ref, blocks_ref, total_ref, held_ref, facts_ref, facts_sem, sem):
    rows = rhs_ref.shape[1]
    lat, lat_count = place_ref[0], place_ref[1]
    part = 2 * rows
    message = CAPACITY * part + 1
    chunks, height, _ = held_ref.shape
    sources = height // message
    lane = lax.broadcasted_iota(jnp.int32, (rows, BW), 1)
    row = lax.broadcasted_iota(jnp.int32, (rows, BW), 0)

    def load(n):
        rows_of = rows_ref.at[pl.ds(n * height, height)]
        return pltpu.make_async_copy(rows_of, held_ref.at[n], sem.at[n])

    facts = pltpu.make_async_copy(got_ref.at[:, message - 1], facts_ref, facts_sem)
    facts.start()
    for n in range(chunks):
        load(n).start()
    total_ref[...] = jnp.zeros_like(total_ref)
    facts.wait()

    @pl.loop(0, chunks)
    def _(n):
        load(n).wait()
        for s in range(sources * CAPACITY):
            source, slot = s // CAPACITY, s % CAPACITY
            block = facts_ref[n * sources + source, 0, 2 * slot].astype(jnp.int32) - 1
            block = jnp.where(block < 0, BLOCKS, block)
            width = facts_ref[n * sources + source, 0, 2 * slot + 1].astype(jnp.int32)
            base = source * message
            start = base + slot * part
            height = held_ref[n, start:start + rows]
            weight = held_ref[n, start + rows:start + part]
            cell = jnp.where(lane < width, weight, 0.0)
            east = jnp.where(lane < width - 1, weight, 0.0)
            east_step = pltpu.roll(height, BW - 1, 1) - height
            raised = jnp.where(row == rows - 1, 0.0, pltpu.roll(height, rows - 1, 0))
            terms = (cell, cell * height, east, east * east_step, cell * (raised - height))
            for k, term in enumerate(terms):
                total_ref[block, k] += term
            last_ref[n * sources + source, slot] = cell[rows - 8:]
            blocks_ref[(n * sources + source) * CAPACITY + slot] = block

    last = (row == rows - 1) & (lat == lat_count - 1)
    first = (row == 0) & (lat == 0)
    sides = 4.0 - last.astype(F32) - first.astype(F32) + RIDGE
    row8 = row[:8]
    lat_even = lat % 2 == 0

    @pl.loop(0, BLOCKS, unroll=32)
    def _(i):
        cell, height = total_ref[i, 0], total_ref[i, 1]
        east = total_ref[i, 3] / (total_ref[i, 2] + DAMPING)
        north = jnp.where(last, 0.0, total_ref[i, 4] / (cell + DAMPING))
        south = jnp.where(row == 0, 0.0, pltpu.roll(north, 1, 0))
        rhs = MU_DATA * height - (east - pltpu.roll(east, 1, 1)) - (north - south)
        diag = MU_DATA * cell + sides
        rhs_ref[i] = rhs
        diag_ref[i] = diag
        top = pltpu.roll(diag[rows - 8:], 4, 0)
        top = jnp.where(row8 == 0, pltpu.roll(north[rows - 8:], 1, 0), top)
        up = jnp.where(row8 >= 4, rhs[rows - 8:], top)
        down = jnp.where(row8 >= 4, pltpu.roll(diag[:8], 4, 0), rhs[:8])
        one_ref[i] = jnp.where(lat_even, up, down)
        two_ref[i] = jnp.where(lat_even, down, up)
        inverse_ref[i] = 1.0 / (cell[rows - 8:] + DAMPING)


def gather(place, got, rows, chunks=2):
    tiles, message, _, _ = got.shape
    height = tiles * message // chunks
    field = (BLOCKS, rows, BW)
    strip = (BLOCKS, 8, BW)
    vmem = pl.BlockSpec(memory_space=pltpu.VMEM)
    shapes = (field, field, strip, strip, (tiles, CAPACITY, 8, BW), strip)
    return pl.pallas_call(
        gather_kernel,
        out_shape=[jax.ShapeDtypeStruct(s, F32) for s in shapes]
        + [jax.ShapeDtypeStruct((tiles * CAPACITY,), jnp.int32)],
        in_specs=[pl.BlockSpec(memory_space=pltpu.SMEM)] + [pl.BlockSpec(memory_space=pl.ANY)] * 2,
        out_specs=[vmem] * len(shapes) + [pl.BlockSpec(memory_space=pltpu.SMEM)],
        scratch_shapes=[
            pltpu.VMEM((BLOCKS + 1, 5, rows, BW), F32),
            pltpu.VMEM((chunks, height, BW), F32),
            pltpu.SMEM((tiles, 1, BW), F32),
            pltpu.SemaphoreType.DMA,
            pltpu.SemaphoreType.DMA((chunks,)),
        ],
        compiler_params=pltpu.CompilerParams(vmem_limit_bytes=VMEM_BYTES),
        name="gather",
    )(place, got, got.reshape(chunks * height, BW))


def finish_kernel(place_ref, blocks_ref, rhs_ref, diag_ref, part_one_ref, part_two_ref, last_ref,
                  inverse_ref, above_ref, gain_ref, one_ref, two_ref, edge_ref, *fix_refs):
    rows = rhs_ref.shape[1]
    tiles = last_ref.shape[0]
    lat, lon = place_ref[0], place_ref[2]
    lat_even = lat % 2 == 0
    row8 = lax.broadcasted_iota(jnp.int32, (8, BW), 0)
    for ref in fix_refs:
        ref[...] = jnp.zeros_like(ref)

    @pl.loop(0, tiles // 2, unroll=8)
    def _(n):
        for k, ref in enumerate(fix_refs):
            source, slot = 2 * n + k // CAPACITY, k % CAPACITY
            block = blocks_ref[source * CAPACITY + slot]
            ref[block] += last_ref[source, slot] * above_ref[source, slot]

    @pl.loop(0, BLOCKS, unroll=8)
    def _(i):
        gain = sum(ref[i] for ref in fix_refs) * inverse_ref[i]
        gain = jnp.where(row8 == 7, gain, 0.0)
        gain_ref[i] = gain
        up = pltpu.roll(gain, 1, 0) - gain
        one_ref[i] = part_one_ref[i] + jnp.where(lat_even, up, 0.0)
        two_ref[i] = part_two_ref[i] + jnp.where(lat_even, 0.0, up)

    first_edge = (BLOCKS - 1) * (1 - lon % 2)
    for side, block in ((0, first_edge), (1, BLOCKS - 1 - first_edge)):
        edge_ref[side, 0:rows - 8] = rhs_ref[block, 0:rows - 8]
        edge_ref[side, rows - 8:rows] = rhs_ref[block, rows - 8:rows] - gain_ref[block]
        edge_ref[side, rows:2 * rows] = diag_ref[block]
        edge_ref[side, 2 * rows:2 * rows + 8] = jnp.where(lat_even, one_ref[block], two_ref[block])


def finish(place, blocks, rhs, diag, *strips):
    rows = rhs.shape[1]
    strip = (BLOCKS, 8, BW)
    edge = (2, 2 * rows + 8, BW)
    vmem = pl.BlockSpec(memory_space=pltpu.VMEM)
    return pl.pallas_call(
        finish_kernel,
        out_shape=[jax.ShapeDtypeStruct(s, F32) for s in (strip, strip, strip, edge)],
        in_specs=[
            pl.BlockSpec(memory_space=pltpu.SMEM),
            pl.BlockSpec(memory_space=pltpu.SMEM),
        ] + [vmem] * 7,
        out_specs=[vmem] * 4,
        scratch_shapes=[pltpu.VMEM((BLOCKS + 1, 8, BW), F32)] * 4,
        compiler_params=pltpu.CompilerParams(vmem_limit_bytes=VMEM_BYTES),
        name="finish",
    )(place, blocks, rhs, diag, *strips)


def two_sum(a, b):
    total = a + b
    part = total - a
    return total, (a - (total - part)) + (b - part)


def pair_sum(high, low, other_high, other_low):
    total, error = two_sum(high, other_high)
    return total, low + other_low + error


def two_product(a, b):
    def split(x):
        big = 4097.0 * x
        top = big - (big - x)
        return top, x - top

    product = a * b
    (a_top, a_end), (b_top, b_end) = split(a), split(b)
    return product, ((a_top * b_top - product) + a_top * b_end + a_end * b_top) + a_end * b_end


def all_rows(high, low):
    for shift in (4, 2, 1):
        high, low = pair_sum(high, low, pltpu.roll(high, shift, 0), pltpu.roll(low, shift, 0))
    return high, low


PAIRS = [(i, j) for j in range(5) for i in range(min(j, 3) + 1)]
LOW = 16


class Field:
    def __init__(self, place_ref, rows, scale_ref, v_refs):
        self.rows, self.tall = rows, rows + 16
        self.scale_ref, self.v_refs = scale_ref, v_refs
        lat, lat_count = place_ref[0], place_ref[1]
        self.lat_even = lat % 2 == 0
        self.has_south, self.has_north = lat > 0, lat < lat_count - 1
        self.row = lax.broadcasted_iota(jnp.int32, (rows, BW), 0)
        self.lane = lax.broadcasted_iota(jnp.int32, (self.tall, BW), 1)

    def assemble(self, i, rhs, diag, up, one, two):
        row8 = self.row[:8]
        south = jnp.where(self.lat_even, two, one)
        north = jnp.where(self.lat_even, one, two)
        first = jnp.where(self.row == 0, south[0:1], 0.0) + rhs
        below = jnp.where(row8 >= 4, south, 0.0)
        above = jnp.where(row8 == 0, north + up, jnp.where(row8 < 4, north, 0.0))
        self.v_refs[0][i, 8:8 + self.tall] = jnp.concatenate([below, first, above], axis=0)
        diag = jnp.concatenate([pltpu.roll(south, 4, 0), diag, pltpu.roll(north, 4, 0)], axis=0)
        self.scale_ref[i] = (diag - MID) * 0.125

    def applied(self, k, i, left, right):
        ref, rows, tall = self.v_refs[k], self.rows, self.tall
        body = slice(8, 8 + tall)
        v = ref[i, body]
        west = pltpu.roll(jnp.where(self.lane == BW - 1, ref[left, body], v), 1, 1)
        east = pltpu.roll(jnp.where(self.lane == 0, ref[right, body], v), BW - 1, 1)
        south = ref[i, 7:7 + tall]
        north = ref[i, 9:9 + tall]
        image = self.scale_ref[i] * v - 0.125 * ((west + east) + (south + north))
        if k == 0:
            image = 0.5 * image
        else:
            image = image - 0.0625 * self.v_refs[k - 1][i, body]
        ends = (jnp.where(self.has_south, image[:8], 0.0), image[8:rows + 8],
                jnp.where(self.has_north, image[rows + 8:], 0.0))
        return jnp.concatenate(ends, axis=0)

    def step(self, k, i, left, right):
        self.v_refs[k + 1][i, 8:8 + self.tall] = self.applied(k, i, left, right)

    def products(self, i, left, right, q_ref, at, totals):
        rows = self.rows
        last = self.applied(3, i, left, right)[8:8 + rows]
        q = [self.v_refs[k][i, 16:16 + rows] for k in range(4)] + [last]
        for k in range(5):
            q_ref[k, at] = q[k]
        out = []
        for total, (a, b) in zip(totals, PAIRS):
            term = q[a] * q[b]
            out.append(total + sum(term[8 * n:8 * n + 8] for n in range(rows // 8)))
        return tuple(out)


NEAR = 6


def inner_kernel(place_ref, rhs_ref, diag_ref, gain_ref, own_one_ref, own_two_ref, one_ref,
                 two_ref, q_ref, totals_ref, sides_ref, scale_ref, *v_refs):
    rows = rhs_ref.shape[1]
    field = Field(place_ref, rows, scale_ref, v_refs)

    @pl.loop(0, BLOCKS, unroll=4)
    def _(i):
        up = jnp.where(field.lat_even, own_one_ref[i], own_two_ref[i])
        tail = rhs_ref[i, rows - 8:rows] - gain_ref[i]
        rhs = jnp.concatenate([rhs_ref[i, 0:rows - 8], tail], axis=0)
        field.assemble(i + 1, rhs, diag_ref[i], up, one_ref[i], two_ref[i])

    for k in range(3):
        @pl.loop(k + 2, BLOCKS - k, unroll=BLOCKS - 2 * k - 2)
        def _(i, k=k):
            field.step(k, i, i - 1, i + 1)

    def products(i, totals):
        return field.products(i, i - 1, i + 1, q_ref, i - 1, totals)

    zero = tuple(jnp.zeros((8, BW), F32) for _ in PAIRS)
    totals = lax.fori_loop(5, BLOCKS - 3, products, zero, unroll=8)
    for n, total in enumerate(totals):
        totals_ref[n] = total
    for k, ref in enumerate((scale_ref,) + v_refs):
        body = slice(8, 24 + rows) if k else slice(0, 16 + rows)
        for n in range(NEAR):
            sides_ref[0, k, n] = ref[n + 1, body]
            sides_ref[1, k, n] = ref[BLOCKS - n, body]


def inner(place, rhs, diag, *strips):
    rows = rhs.shape[1]
    vmem = pl.BlockSpec(memory_space=pltpu.VMEM)
    shapes = ((5, BLOCKS, rows, BW), (len(PAIRS), 8, BW), (2, 5, NEAR, rows + 16, BW))
    return pl.pallas_call(
        inner_kernel,
        out_shape=[jax.ShapeDtypeStruct(s, F32) for s in shapes],
        in_specs=[pl.BlockSpec(memory_space=pltpu.SMEM)] + [vmem] * 7,
        out_specs=[vmem] * 3,
        scratch_shapes=[pltpu.VMEM((BLOCKS + 2, rows + 16, BW), F32)]
        + [pltpu.VMEM((BLOCKS + 2, rows + 32, BW), F32)] * 4,
        compiler_params=pltpu.CompilerParams(vmem_limit_bytes=VMEM_BYTES),
        name="inner",
    )(place, rhs, diag, *strips)


def outer_kernel(place_ref, totals_ref, sides_ref, lon_one_ref, lon_two_ref, q_ref, gram_ref,
                 scale_ref, *v_refs):
    tall = sides_ref.shape[3]
    rows = tall - 16
    field = Field(place_ref, rows, scale_ref, v_refs)
    size = NEAR + 1
    for side in range(2):
        for n in range(NEAR):
            scale_ref[side * size + n + 1] = sides_ref[side, 0, n]
            for k in range(4):
                if n >= k:
                    v_refs[k][side * size + n + 1, 8:8 + tall] = sides_ref[side, k + 1, n]
    one_east = place_ref[2] % 2 == 0
    two = 2 * rows
    for side in range(2):
        first = lon_two_ref[...] if side == 0 else lon_one_ref[...]
        other = lon_one_ref[...] if side == 0 else lon_two_ref[...]
        strip = jnp.where(one_east, first, other)
        field.assemble(side * size, strip[0:rows], strip[rows:two], strip[two:two + 8],
                       strip[two + 8:two + 16], strip[two + 16:two + 24])

    def beside(side, n):
        inward, outward = side * size + n + 1, side * size + max(n - 1, 0)
        return (side * size + n,) + ((outward, inward) if side == 0 else (inward, outward))

    for k in range(3):
        for n in range(k + 2):
            for side in range(2):
                field.step(k, *beside(side, n))
    totals = tuple(totals_ref[n] for n in range(len(PAIRS)))
    for n in range(1, 5):
        for side in range(2):
            totals = field.products(*beside(side, n), q_ref, side * 4 + n - 1, totals)

    row_of = lax.broadcasted_iota(jnp.int32, (8, BW), 0)
    lane_of = lax.broadcasted_iota(jnp.int32, (8, BW), 1)
    gram = jnp.zeros((8, BW), F32)
    for start in range(0, len(PAIRS), 8):
        high = jnp.zeros((8, BW), F32)
        low = jnp.zeros((8, BW), F32)
        for n, total in enumerate(totals[start:start + 8]):
            pair = all_rows(total, jnp.zeros_like(total))
            high = jnp.where(row_of == n, pair[0], high)
            low = jnp.where(row_of == n, pair[1], low)
        shift = BW // 2
        while shift:
            high, low = pair_sum(high, low, pltpu.roll(high, shift, 1), pltpu.roll(low, shift, 1))
            shift //= 2
        gram = jnp.where(lane_of == row_of + start, high, gram)
        gram = jnp.where(lane_of == row_of + start + LOW, low, gram)
    row = jnp.sum(gram, axis=0, keepdims=True)
    gram_ref[...] = jnp.broadcast_to(row[None], gram_ref.shape)


def outer(place, totals, sides, one, two, devices):
    tall = sides.shape[3]
    rows = tall - 16
    vmem = pl.BlockSpec(memory_space=pltpu.VMEM)
    return pl.pallas_call(
        outer_kernel,
        out_shape=[
            jax.ShapeDtypeStruct((5, 8, rows, BW), F32),
            jax.ShapeDtypeStruct((devices, 1, BW), F32),
        ],
        in_specs=[pl.BlockSpec(memory_space=pltpu.SMEM)] + [vmem] * 4,
        out_specs=[vmem, vmem],
        scratch_shapes=[pltpu.VMEM((2 * (NEAR + 1), tall, BW), F32)]
        + [pltpu.VMEM((2 * (NEAR + 1), tall + 16, BW), F32)] * 4,
        compiler_params=pltpu.CompilerParams(vmem_limit_bytes=VMEM_BYTES),
        name="outer",
    )(place, totals, sides, one, two)


def solved(high, low):
    g = {}
    for n, (a, b) in enumerate(PAIRS):
        g[a, b] = g[b, a] = (high[n], low[n])

    def times(factor, pair):
        return factor * pair[0], factor * pair[1]

    m = [[None] * 4 for _ in range(4)]
    for j in range(4):
        for i in range(j + 1):
            value = pair_sum(*times(MID, g[i, j]), *times(8.0 if j else 16.0, g[i, j + 1]))
            if j:
                value = pair_sum(*value, *times(0.5, g[i, j - 1]))
            m[i][j] = m[j][i] = two_sum(*value)

    work = [[m[i][j][0] for j in range(4)] for i in range(4)]
    inverse = []
    factor = [[None] * 4 for _ in range(4)]
    for k in range(4):
        pivot = work[k][k]
        inverse.append(jnp.where(pivot > 0.0, 1.0 / jnp.where(pivot > 0.0, pivot, 1.0), 0.0))
        for i in range(k + 1, 4):
            factor[i][k] = work[k][i] * inverse[k]
        for i in range(k + 1, 4):
            for j in range(i, 4):
                work[i][j] = work[i][j] - factor[i][k] * work[k][j]

    def solve(y):
        y = list(y)
        for k in range(4):
            for i in range(k + 1, 4):
                y[i] = y[i] - factor[i][k] * y[k]
        y = [y[k] * inverse[k] for k in range(4)]
        for k in range(3, -1, -1):
            for i in range(k):
                y[i] = y[i] - factor[k][i] * y[k]
        return y

    rest = [g[0, i] for i in range(4)]
    c = solve([pair[0] for pair in rest])
    found = [c]
    for _ in range(2):
        for i in range(4):
            for j in range(4):
                product, error = two_product(m[i][j][0], c[j])
                total, lost = two_sum(rest[i][0], -product)
                rest[i] = total, rest[i][1] + (lost - error - m[i][j][1] * c[j])
        rest = [two_sum(*pair) for pair in rest]
        c = solve([pair[0] for pair in rest])
        found.append(c)
    c = [found[0][k] + (found[1][k] + found[2][k]) for k in range(4)]
    r = [
        1.0 - (MID * c[0] + 0.5 * c[1]),
        -(16.0 * c[0] + MID * c[1] + 0.5 * c[2]),
        -(8.0 * c[1] + MID * c[2] + 0.5 * c[3]),
        -(8.0 * c[2] + MID * c[3]),
        -(8.0 * c[3]),
    ]
    return c, r


def combine_kernel(gram_ref, q_ref, sides_ref, x_out_ref, r_out_ref, x_ref, r_ref, sem):
    rows = q_ref.shape[2]
    terms = [(gram_ref[n:n + 8], jnp.zeros((8, BW), F32)) for n in range(0, gram_ref.shape[0], 8)]
    while len(terms) > 1:
        terms = [pair_sum(*terms[n], *terms[n + 1]) for n in range(0, len(terms), 2)]
    high, low = all_rows(*terms[0])
    high, low = two_sum(high, low + pltpu.roll(high, BW - LOW, 1))
    first = high[0:1, 0:1]
    scale = jnp.where(first > 1e25, 2.0 ** -60, jnp.where(first < 1e-15, 2.0 ** 60, 1.0))
    lane = lax.broadcasted_iota(jnp.int32, (1, BW), 1)

    def pick(values, n):
        row = jnp.where(lane == n, values[0:1], 0.0)
        return scale * jnp.sum(row, axis=1, keepdims=True)

    count = range(len(PAIRS))
    c, r = solved([pick(high, n) for n in count], [pick(low, n) for n in count])
    c = [jnp.broadcast_to(value, (rows, BW)) for value in c]
    r = [jnp.broadcast_to(value, (rows, BW)) for value in r]
    copies = []
    batch = BLOCKS // sem.shape[0]
    for i in range(BLOCKS):
        if i < 4:
            q = [sides_ref[k, i] for k in range(5)]
        elif i >= BLOCKS - 4:
            q = [sides_ref[k, 4 + BLOCKS - 1 - i] for k in range(5)]
        else:
            q = [q_ref[k, i] for k in range(5)]
        columns = slice(i * BW, (i + 1) * BW)
        x_ref[:, columns] = sum(c[k] * q[k] for k in range(4))
        r_ref[:, columns] = sum(r[k] * q[k] for k in range(5))
        if i % batch == batch - 1:
            done = pl.ds((i + 1 - batch) * BW, batch * BW)
            for n, (held, out) in enumerate(((x_ref, x_out_ref), (r_ref, r_out_ref))):
                copies.append(pltpu.make_async_copy(held.at[:, done], out.at[:, done],
                                                    sem.at[i // batch, n]))
                copies[-1].start()
    for copy in copies:
        copy.wait()


def combine(gram, q, sides):
    _, blocks, rows, _ = q.shape
    out = jax.ShapeDtypeStruct((rows, blocks * BW), F32)
    vmem = pl.BlockSpec(memory_space=pltpu.VMEM)
    return pl.pallas_call(
        combine_kernel,
        out_shape=[out, out],
        in_specs=[vmem] * 3,
        out_specs=[pl.BlockSpec(memory_space=pl.ANY)] * 2,
        scratch_shapes=[pltpu.VMEM(out.shape, F32)] * 2 + [pltpu.SemaphoreType.DMA((4, 2))],
        compiler_params=pltpu.CompilerParams(vmem_limit_bytes=VMEM_BYTES),
        name="combine",
    )(gram, q, sides)


def body(piece_height, piece_weight, piece_column, piece_width):
    lon_count, lat_count = lax.axis_size("lon"), lax.axis_size("lat")
    rows = piece_height.shape[1]
    lon, lat = lax.axis_index("lon"), lax.axis_index("lat")
    place = jnp.stack([lat, jnp.int32(lat_count), lon]).astype(jnp.int32)

    packed = pack(piece_column, piece_width, piece_height, piece_weight, lon_count)
    got = lax.all_to_all(packed, "lon", split_axis=0, concat_axis=0, tiled=True)
    part = 2 * rows
    above = passed_along(got[:, :CAPACITY * part:part], "lat", -1)
    rhs, diag, *strips, blocks = gather(place, got, rows)
    gain, own_one, own_two, edge = finish(place, blocks, rhs, diag, *strips, above)

    one = swapped(own_one, "lat", 0, False)
    two = swapped(own_two, "lat", 1, False)
    first_edge = (BLOCKS - 1) * (1 - lon % 2)
    strips = []
    for start, block in ((0, first_edge), (1, BLOCKS - 1 - first_edge)):
        pick = lambda strip: lax.dynamic_index_in_dim(strip, block, 0, keepdims=False)
        message = jnp.concatenate([edge[start], pick(one), pick(two)], axis=0)
        strips.append(swapped(message, "lon", start, True))
    q, totals, near = inner(place, rhs, diag, gain, own_one, own_two, one, two)
    sides, spread = outer(place, totals, near, *strips, lon_count * lat_count)
    grams = lax.all_to_all(spread, ("lon", "lat"), split_axis=0, concat_axis=0, tiled=True)
    return tuple(combine(grams.reshape(lon_count * lat_count, BW), q, sides))


def solution(mesh):
    return jax.shard_map(
        body,
        mesh=mesh,
        in_specs=(P("lon", "lat", None), P("lon", "lat", None), P("lon"), P("lon")),
        out_specs=(P("lat", "lon"), P("lat", "lon")),
        check_vma=False,
    )
```
